32 devices in a mesh: dp: 8 (over y, x, core), tensor: 4 (over z).
Axes of the slice: x: 2, y: 2, z: 4, core: 2. Of those that a mesh axis runs over, the one named last changes fastest.
Arguments:
- tokens: bfloat16 [16384, 1024], P(('dp', 'tensor')), may hold values from -6 to 6
- lengths: int32 [8, 16], P('dp'), may hold values from 1 to 512, 2048 in all within a row
- doc_pairs: int32 [8, 8], P('dp'), may hold values from 0 to 7, each once within a row
- qkv_weight: bfloat16 [1024, 3, 1024], P(None, None, 'tensor'), may hold values from -0.1875 to 0.1875
- qkv_bias: bfloat16 [3, 1024], P(None, 'tensor'), may hold values from -1.1953125 to 1.1953125
- attn_weight: bfloat16 [1024, 1024], P('tensor'), may hold values from -1.5 to 1.5
- attn_bias: bfloat16 [1024], replicated, may hold values from -1.1953125 to 1.1953125
- ffn_in_weight: bfloat16 [1024, 4096], P(None, 'tensor'), may hold values from -0.1875 to 0.1875
- ffn_in_bias: bfloat16 [4096], P('tensor'), may hold values from -1.1953125 to 1.1953125
- ffn_out_weight: bfloat16 [4096, 1024], P('tensor'), may hold values from -0.09375 to 0.09375
- ffn_out_bias: bfloat16 [1024], replicated, may hold values from -1.1953125 to 1.1953125
- norm_gains: bfloat16 [2, 1024], replicated, may hold values from 0.5 to 1.5
- norm_shifts: bfloat16 [2, 1024], replicated, may hold values from -1.1953125 to 1.1953125
- proj_weight: bfloat16 [1024, 128], replicated, may hold values from -0.1875 to 0.1875
- log_temp: float32 [1], replicated, may hold values from -3.5 to -2.3
Outputs:
- contrast_loss: float32 [1], replicated
- activations: bfloat16 [16384, 1024], P(('dp', 'tensor'))
- tokens_grad: float32 [16384, 1024], P(('dp', 'tensor'))
- qkv_weight_grad: float32 [1024, 3, 1024], P('dp', None, 'tensor')
- qkv_bias_grad: float32 [3, 1024], P(None, 'tensor')
- attn_weight_grad: float32 [1024, 1024], P('tensor', 'dp')
- attn_bias_grad: float32 [1024], replicated
- ffn_in_weight_grad: float32 [1024, 4096], P('dp', 'tensor')
- ffn_in_bias_grad: float32 [4096], P('tensor')
- ffn_out_weight_grad: float32 [4096, 1024], P('tensor', 'dp')
- ffn_out_bias_grad: float32 [1024], replicated
- norm_gains_grad: float32 [2, 1024], replicated
- norm_shifts_grad: float32 [2, 1024], replicated
- proj_weight_grad: float32 [1024, 128], replicated
- log_temp_grad: float32 [1], replicated
The draws below stay inside these ranges and needn't reach their ends.
Inputs may be any that keep to these rules, and one draw needn't show every extreme that they name: The 16 lengths of a row sum to 2048; the longest of each row is exactly 512. Each row holds every number of 0 to 7 once; query segment q of a row is paired with segment 8 + doc_pairs[q] of the same row.
All inputs are finite; a program needn't handle non-finite values.
Results may differ from the reference program's by a relative error of at most 0.022.
Values may be sent and summed in bfloat16 or wider, within the bound.
A program may use at most 320 MiB of HBM per device.

```python
import math
import jax
import jax.numpy as jnp
import numpy as np
from jax import lax

D = 1024
HEADS = 16
HDIM = 64
FF = 4096
EMB = 128
SEQ = 2048
SEGS = 16
MOST = 512
BLOCK = 512
NQ = 8
ROWS = 8
TOKENS = 16384


def raised(result, key, source, target, shards_of, factor):
    def block_of(axis_at):
        return (jnp.arange(result.shape[axis_at]) // (result.shape[axis_at] // shards_of)).reshape((-1,) + (1,) * (result.ndim - 1 - axis_at))

    first = jax.random.permutation(key, shards_of)[block_of(target)]
    second = (block_of(target) + shards_of // 2) % shards_of
    return jnp.where((block_of(source) == first) | (block_of(source) == second), factor * result, result)


def levels(key, shape, pieces, low, top_value):
    level, own = 1.0, jax.random.fold_in(key, 6)
    for dim, shards_of in pieces:
        steps = jnp.exp(jax.random.uniform(jax.random.fold_in(own, dim), (shards_of,), jnp.float32, low / len(pieces), top_value / len(pieces)))
        level = level * jnp.repeat(steps, shape[dim] // shards_of).reshape([-1 if axis == dim else 1 for axis in range(len(shape))])
    return level


def split_up(count, total, most, lean):
    loads = [(1 << 20) // math.isqrt(grade ** lean) + 1 for grade in range(2, count + 1)]
    surplus, given = total - most - (count - 1), [1] * (count - 1)
    while surplus > 0:
        candidates = [i for i in range(count - 1) if given[i] < most]
        pool, remaining = sum([loads[i] for i in candidates]), surplus
        for i in candidates:
            extra = min(most - given[i], max(1, remaining * loads[i] // pool), surplus)
            given[i] = given[i] + extra
            surplus = surplus - extra
    return np.array([most] + given)


def ragged(own_key, count, total, reach, lean):
    if count == 2:
        one = jax.random.randint(own_key, (), max(1, total - reach), min(reach, total - 1) + 1)
        return jnp.stack([one, total - one])
    sizes = jnp.asarray(split_up(count, total, reach, lean), jnp.int32)
    couples = (count - 1) // 2
    source_of, taker = sizes[1:1 + 2 * couples:2], sizes[2:2 + 2 * couples:2]
    margin = jnp.minimum(source_of - 1, reach - taker)
    shifted = jax.random.randint(jax.random.fold_in(own_key, 1), (couples,), 0, 1 << 20) % (margin + 1)
    sizes = sizes.at[1:1 + 2 * couples:2].set(source_of - shifted).at[2:2 + 2 * couples:2].set(taker + shifted)
    return sizes[jax.random.permutation(jax.random.fold_in(own_key, 2), count)]


def noise(rng, shape, deviation, most, shards=(), kind=jnp.bfloat16):
    result = deviation * jax.random.normal(rng, shape, jnp.float32)
    if shards:
        result = result * levels(rng, shape, shards, -0.22, 0.18)
    return jnp.clip(result, -most, most).astype(kind)


def heavy_noise(key, extent, deviation, reach, cuts, heavy, held_as=jnp.bfloat16):
    drawn = deviation * jax.random.normal(key, extent, jnp.float32)
    if cuts:
        drawn = drawn * levels(key, extent, cuts, -0.22, 0.18)
    return jnp.clip(raised(drawn, jax.random.fold_in(key, 3), *heavy), -reach, reach).astype(held_as)


def setup_inputs(seed: int = 0) -> dict:
    splits = jax.random.split(jax.random.key(seed), 16)
    return {
        "tokens": heavy_noise(splits[0], (TOKENS, D), 1.0, 6.0, ((0, 32),), (0, 1, 32, 2.75)),
        "lengths": jax.vmap(lambda own: ragged(own, SEGS, SEQ, MOST, 2))(jax.random.split(splits[1], ROWS)).reshape((ROWS, SEGS)).astype(jnp.int32),
        "doc_pairs": jax.vmap(lambda own: jax.random.permutation(own, NQ))(jax.random.split(splits[2], ROWS)).reshape((ROWS, NQ)).astype(jnp.int32),
        "qkv_weight": noise(splits[3], (D, 3, D), D ** -0.5, 0.1875, ((2, 4),)),
        "qkv_bias": noise(splits[4], (3, D), 0.2, 1.1953125, ((1, 4),)),
        "attn_weight": noise(splits[5], (D, D), (D // 64) ** -0.5, 1.5, ((0, 4),)),
        "attn_bias": noise(splits[6], (D,), 0.2, 1.1953125),
        "ffn_in_weight": noise(splits[7], (D, FF), D ** -0.5, 0.1875, ((1, 4),)),
        "ffn_in_bias": noise(splits[8], (FF,), 0.2, 1.1953125, ((0, 4),)),
        "ffn_out_weight": noise(splits[9], (FF, D), FF ** -0.5, 0.09375, ((0, 4),)),
        "ffn_out_bias": noise(splits[10], (D,), 0.2, 1.1953125),
        "norm_gains": jnp.clip(1.0 + 0.1 * jax.random.normal(splits[11], (2, D), jnp.float32), 0.5, 1.5).astype(jnp.bfloat16),
        "norm_shifts": noise(splits[12], (2, D), 0.2, 1.1953125),
        "proj_weight": noise(splits[13], (D, EMB), D ** -0.5, 0.1875),
        "log_temp": jnp.clip(jax.random.uniform(splits[14], (1,), jnp.float32, -3.5, -2.3), -3.5, -2.3),
    }


@jax.custom_vjp
def low(v):
    return lax.optimization_barrier(v.astype(jnp.bfloat16)).astype(jnp.float32)

@jax.custom_vjp
def low_back(v):
    return v

def low_keep(v):
    return (low(v), None)

def low_pass(kept, grad):
    return (grad,)

def back_keep(v):
    return (v, None)

def back_low(kept, grad):
    return (low(grad),)
low.defvjp(low_keep, low_pass)
low_back.defvjp(back_keep, back_low)
highest = lax.Precision.HIGHEST
eps_norm = 1e-05
eps_unit = 1e-06
sharpness = 10.0

def matmul(left, right):
    return jnp.dot(left, right, precision=highest, preferred_element_type=jnp.float32)

def layer_norm(values, gain, shift):
    mean_value = lax.optimization_barrier(jnp.mean(values, axis=-1, keepdims=True))
    centered = values - mean_value
    variance = lax.optimization_barrier(jnp.mean(centered * centered, axis=-1, keepdims=True))
    return centered * lax.rsqrt(variance + eps_norm) * gain + shift

def segment_layout(row_lengths):
    seg_ends = jnp.cumsum(row_lengths, dtype=jnp.int32)
    seg_starts = seg_ends - row_lengths
    positions = jnp.arange(SEQ, dtype=jnp.int32)
    seg_ids = lax.optimization_barrier(jnp.sum((positions[:, None] >= seg_ends[None, :]).astype(jnp.int32), axis=1, dtype=jnp.int32))
    member = seg_ids[:, None] == jnp.arange(SEGS, dtype=jnp.int32)[None, :]
    offsets = positions - lax.optimization_barrier(jnp.sum(jnp.where(member, seg_starts[None, :], 0), axis=1, dtype=jnp.int32))
    return (seg_ids, member, offsets)

def rotary_tables(offsets):
    half_dim = HDIM // 2
    inv_freq = jnp.exp(jnp.arange(half_dim, dtype=jnp.float32) * (-2.0 * math.log(10000.0) / HDIM))
    angles = offsets.astype(jnp.float32)[:, None] * inv_freq[None, :]
    return (jnp.cos(angles), jnp.sin(angles))

def rotate(values, cosine, sine_table):
    half_dim = values.shape[-1] // 2
    front_half = values[..., :half_dim]
    back_half = values[..., half_dim:]
    cos_wide = cosine[:, None, :]
    sin_wide = sine_table[:, None, :]
    return jnp.concatenate([front_half * cos_wide - back_half * sin_wide, back_half * cos_wide + front_half * sin_wide], axis=-1)

def contrastive(embedded, member, row_pairs, temp_log):
    onehot = member.astype(jnp.float32)
    counts = lax.optimization_barrier(jnp.sum(onehot, axis=0))
    query_mask = onehot[:, :NQ]
    doc_mask = onehot[:, NQ:]
    temp_inv = jnp.exp(-temp_log[0])
    positive = (row_pairs[:, None] == jnp.arange(NQ, dtype=jnp.int32)[None, :]).astype(jnp.float32)
    running = jnp.zeros((), jnp.float32)
    for prefix in (EMB, EMB * 3 // 4, EMB // 2):
        prefix_emb = embedded[:, :prefix]
        unit_vecs = low(prefix_emb * lax.rsqrt(lax.optimization_barrier(jnp.sum(prefix_emb * prefix_emb, axis=1, keepdims=True)) + eps_unit))
        similar = low_back(matmul(unit_vecs, unit_vecs.T))
        smooth_max = jnp.log(matmul(jnp.exp(sharpness * (similar - 1.0)), doc_mask)) / sharpness + 1.0
        seg_scores = matmul(query_mask.T, smooth_max) / counts[:NQ, None]
        logits = seg_scores * temp_inv
        running = running + jnp.sum(jnp.log(lax.optimization_barrier(jnp.sum(jnp.exp(logits), axis=1))) - lax.optimization_barrier(jnp.sum(logits * positive, axis=1)))
    return running

def row_forward(row_tokens, row_lengths, row_pairs, params):
    qkv_w, qkv_b, attn_w, attn_b, in_w, in_b, out_w, out_b, gains, shifts, proj_w, temp_log = params
    seg_ids, member, offsets = segment_layout(row_lengths)
    cosine, sine_table = rotary_tables(offsets)
    projected = low_back(jnp.einsum('td,dkc->tkc', row_tokens, qkv_w, precision=highest) + qkv_b[None])
    split_heads = projected.reshape(SEQ, 3, HEADS, HDIM)
    query_heads = low(rotate(split_heads[:, 0], cosine, sine_table))
    key_heads = low(rotate(split_heads[:, 1], cosine, sine_table))
    value_heads = low(split_heads[:, 2])
    score_scale = HDIM ** (-0.5)

    def attend_block(block_start):
        query_block = lax.dynamic_slice_in_dim(query_heads, block_start, BLOCK, 0)
        block_ids = lax.dynamic_slice_in_dim(seg_ids, block_start, BLOCK, 0)
        raw_scores = low_back(jnp.einsum('qhc,khc->hqk', query_block, key_heads, precision=highest) * score_scale)
        same_doc = block_ids[:, None] == seg_ids[None, :]
        attn_probs = low(jax.nn.softmax(jnp.where(same_doc[None], raw_scores, -1000000000.0), axis=-1))
        return jnp.einsum('hqk,khc->qhc', attn_probs, value_heads, precision=highest)
    block_starts = jnp.arange(SEQ // BLOCK, dtype=jnp.int32) * BLOCK
    mixed_heads = lax.map(jax.checkpoint(attend_block), block_starts)
    mixed_heads = low(low_back(mixed_heads.reshape(SEQ, HEADS * HDIM)))
    attn_out = low_back(matmul(mixed_heads, attn_w) + attn_b)
    normed = layer_norm(row_tokens + attn_out, gains[0], shifts[0])
    ffn_pre = low_back(matmul(low(normed), in_w) + in_b)
    hidden = low(jax.nn.gelu(ffn_pre, approximate=False))
    ffn_out = low_back(matmul(hidden, out_w) + out_b)
    output = layer_norm(normed + ffn_out, gains[1], shifts[1])
    embedded = low(low_back(matmul(low(output), proj_w)))
    return (contrastive(embedded, member, row_pairs, temp_log), output)

def reference(tokens, lengths, doc_pairs, qkv_weight, qkv_bias, attn_weight, attn_bias, ffn_in_weight, ffn_in_bias, ffn_out_weight, ffn_out_bias, norm_gains, norm_shifts, proj_weight, log_temp):
    floats = tuple((array.astype(jnp.float32) for array in (tokens, qkv_weight, qkv_bias, attn_weight, attn_bias, ffn_in_weight, ffn_in_bias, ffn_out_weight, ffn_out_bias, norm_gains, norm_shifts, proj_weight, log_temp)))

    def forward(token_rows, *params):
        stacked = token_rows.reshape(ROWS, SEQ, D)
        checked = jax.checkpoint(row_forward)

        def row_step(running, row_item):
            row_tokens, row_lengths, row_pairs = row_item
            row_loss, row_out = checked(row_tokens, row_lengths, row_pairs, params)
            return (running + row_loss, row_out)
        running, outputs = lax.scan(row_step, jnp.zeros((), jnp.float32), (stacked, lengths, doc_pairs))
        return (running / (NQ * ROWS), outputs.reshape(TOKENS, D))
    (loss_value, outputs), pullback = jax.vjp(forward, *floats)
    gradients = pullback((jnp.ones_like(loss_value), jnp.zeros_like(outputs)))
    return (loss_value.reshape(1), outputs.astype(jnp.bfloat16), gradients[0], gradients[1], gradients[2], gradients[3], gradients[4], gradients[5], gradients[6], gradients[7], gradients[8], gradients[9], gradients[10], gradients[11], gradients[12])
```

```python
from functools import partial
import math

import jax
import jax.numpy as jnp
from jax import lax
from jax.experimental import pallas as pl
from jax.experimental.pallas import tpu as pltpu
from jax.sharding import PartitionSpec as P

HDIM = 64
EMB = 128
SEQ = 2048
SEGS = 16
NQ = 8
MESH = pl.DeviceIdType.MESH
ANY = pl.ANY
F32 = jnp.float32
BF = jnp.bfloat16
eps_norm = 1e-05
eps_unit = 1e-06
VMEM_BIG = 60 * 1024 * 1024


def dot(left, right, left_dim=1, right_dim=0, precision=None):
    return lax.dot_general(
        left,
        right,
        (((left_dim,), (right_dim,)), ((), ())),
        preferred_element_type=F32,
        precision=precision,
    )


def hbm_specs(count):
    return [pl.BlockSpec(memory_space=ANY)] * count


def vmem_specs(count):
    return [pl.BlockSpec(memory_space=pltpu.VMEM)] * count


def rotate_lanes(values, cosine, sine):
    out = []
    front = lax.rem(lax.broadcasted_iota(jnp.int32, (1, 128), 1), 64) < 32
    for start in range(0, values.shape[1], 128):
        part = values[:, start : start + 128]
        partner = jnp.where(front, pltpu.roll(part, 96, 1), pltpu.roll(part, 32, 1))
        out.append(part * cosine + partner * sine)
    return out[0] if len(out) == 1 else jnp.concatenate(out, axis=1)


PROJ_COLS = 256


def project_kernel(window_ref, weight_ref, bias_ref, cos_ref, sin_ref, query_ref, key_ref, value_ref):
    step = pl.program_id(0)
    per_kind = pl.num_programs(0) // 3
    local = query_ref.shape[0]
    bias = bias_ref[0].astype(F32)

    @pl.when(step < per_kind)
    def _():
        rows = pl.ds(local, local)
        made = dot(window_ref[rows, :], weight_ref[0]) + bias
        query_ref[...] = rotate_lanes(made, cos_ref[rows, :], sin_ref[rows, :]).astype(BF)

    @pl.when((step >= per_kind) & (step < 2 * per_kind))
    def _():
        for part in range(3):
            rows = pl.ds(part * local, local)
            made = dot(window_ref[rows, :], weight_ref[0]) + bias
            key_ref[rows, :] = rotate_lanes(made, cos_ref[rows, :], sin_ref[rows, :]).astype(BF)

    @pl.when(step >= 2 * per_kind)
    def _():
        for part in range(3):
            rows = pl.ds(part * local, local)
            value_ref[rows, :] = (dot(window_ref[rows, :], weight_ref[0]) + bias).astype(BF)


def project(window, weight, bias, cosine, sine):
    width = weight.shape[2]
    per = width // PROJ_COLS
    long = window.shape[0]
    local = long // 3
    flops = 2 * width * width * (local + 2 * long)
    return pl.pallas_call(
        project_kernel,
        grid=(3 * per,),
        in_specs=[
            pl.BlockSpec((long, width), lambda n: (0, 0)),
            pl.BlockSpec((1, width, PROJ_COLS), lambda n: (n // per, 0, lax.rem(n, per))),
            pl.BlockSpec((1, 1, PROJ_COLS), lambda n: (n // per, 0, lax.rem(n, per))),
            pl.BlockSpec((long, 128), lambda n: (0, 0)),
            pl.BlockSpec((long, 128), lambda n: (0, 0)),
        ],
        out_specs=[
            pl.BlockSpec((local, PROJ_COLS), lambda n: (0, jnp.minimum(n, per - 1))),
            pl.BlockSpec((long, PROJ_COLS), lambda n: (0, jnp.clip(n - per, 0, per - 1))),
            pl.BlockSpec((long, PROJ_COLS), lambda n: (0, jnp.clip(n - 2 * per, 0, per - 1))),
        ],
        out_shape=[
            jax.ShapeDtypeStruct((local, width), BF),
            jax.ShapeDtypeStruct((long, width), BF),
            jax.ShapeDtypeStruct((long, width), BF),
        ],
        compiler_params=pltpu.CompilerParams(vmem_limit_bytes=40 * 2**20),
        cost_estimate=pl.CostEstimate(flops=flops, bytes_accessed=14 * 2**20, transcendentals=0),
    )(window, weight, bias, cosine, sine)


BQ = 128
BK = 256
SCALE = HDIM**-0.5


def split_pair(values):
    first = lax.broadcasted_iota(jnp.int32, (1, 128), 1) < 64
    zero = jnp.zeros_like(values)
    return jnp.where(first, values, zero), jnp.where(first, zero, values)


def attend_kernel(bounds_ref, query_ref, key_ref, value_ref, segq_ref, segk_ref, mixed_ref, lse_ref):
    first = lax.broadcasted_iota(jnp.int32, (1, 128), 1) < 64
    for block in range(query_ref.shape[0] // BQ):
        rows = pl.ds(block * BQ, BQ)
        queries = split_pair(query_ref[rows, :] * jnp.asarray(SCALE, BF))
        seg_q = segq_ref[rows, 0:1]

        def body(index, carry):
            keys_at = pl.ds(pl.multiple_of(index * BK, BK), BK)
            keys = key_ref[keys_at, :]
            values = value_ref[keys_at, :]
            live = seg_q == segk_ref[0:1, keys_at]
            made = []
            for head in range(2):
                top, total, acc = carry[head]
                scores = jnp.where(live, dot(queries[head], keys, 1, 1), -1e9)
                new_top = jnp.maximum(top, jnp.max(scores, axis=1, keepdims=True))
                probs = jnp.exp(scores - new_top)
                fade = jnp.exp(top - new_top)
                total = total * fade + jnp.sum(probs, axis=1, keepdims=True)
                acc = acc * fade + dot(probs.astype(BF), values)
                made.append((new_top, total, acc))
            return tuple(made)

        start = tuple(
            (jnp.full((BQ, 1), -2e9, F32), jnp.zeros((BQ, 1), F32), jnp.zeros((BQ, 128), F32)) for _ in range(2)
        )
        done = lax.fori_loop(bounds_ref[block, 0], bounds_ref[block, 1], body, start)
        parts = [acc / total for top, total, acc in done]
        logs = [top + jnp.log(total) for top, total, acc in done]
        mixed_ref[rows, :] = jnp.where(first, parts[0], parts[1]).astype(BF)
        lse_ref[0, rows, :] = jnp.where(first, logs[0], logs[1])


def attend(bounds, queries, keys, values, seg_q, seg_k):
    local, width = queries.shape
    long = keys.shape[0]
    groups = width // 128
    return pl.pallas_call(
        attend_kernel,
        grid_spec=pltpu.PrefetchScalarGridSpec(
            num_scalar_prefetch=1,
            grid=(groups,),
            in_specs=[
                pl.BlockSpec((local, 128), lambda g, b: (0, g)),
                pl.BlockSpec((long, 128), lambda g, b: (0, g)),
                pl.BlockSpec((long, 128), lambda g, b: (0, g)),
                pl.BlockSpec((local, 128), lambda g, b: (0, 0)),
                pl.BlockSpec((8, long), lambda g, b: (0, 0)),
            ],
            out_specs=[
                pl.BlockSpec((local, 128), lambda g, b: (0, g)),
                pl.BlockSpec((1, local, 128), lambda g, b: (g, 0, 0)),
            ],
        ),
        out_shape=[
            jax.ShapeDtypeStruct((local, width), BF),
            jax.ShapeDtypeStruct((groups, local, 128), F32),
        ],
        compiler_params=pltpu.CompilerParams(vmem_limit_bytes=40 * 2**20),
        cost_estimate=pl.CostEstimate(flops=2 * 2**30, bytes_accessed=8 * 2**20, transcendentals=4 * 2**20),
    )(bounds, queries, keys, values, seg_q, seg_k)


def attend_back_kernel(
    bounds_ref, query_ref, key_ref, value_ref, mixed_ref, grad_ref, lse_ref, segq_ref, segk_ref, cos_ref, sin_ref,
    dq_ref, dk_ref, dv_ref, dk_acc, dv_acc,
):
    first = lax.broadcasted_iota(jnp.int32, (1, 128), 1) < 64
    local = query_ref.shape[0]
    dk_acc[...] = jnp.zeros_like(dk_acc)
    dv_acc[...] = jnp.zeros_like(dv_acc)
    for block in range(local // BQ):
        rows = pl.ds(block * BQ, BQ)
        queries = split_pair(query_ref[rows, :] * jnp.asarray(SCALE, BF))
        grads = split_pair(grad_ref[rows, :])
        product = mixed_ref[rows, :].astype(F32) * grad_ref[rows, :].astype(F32)
        deltas = [jnp.sum(part, axis=1, keepdims=True) for part in split_pair(product)]
        logs = (lse_ref[0, rows, 0:1], lse_ref[0, rows, 64:65])
        seg_q = segq_ref[rows, 0:1]

        def body(index, carry):
            keys_at = pl.ds(pl.multiple_of(index * BK, BK), BK)
            keys = key_ref[keys_at, :]
            values = value_ref[keys_at, :]
            live = seg_q == segk_ref[0:1, keys_at]
            made, dk, dv = [], 0.0, 0.0
            for head in range(2):
                scores = jnp.where(live, dot(queries[head], keys, 1, 1), -1e9)
                probs = jnp.exp(scores - logs[head])
                score_low = (probs * (dot(grads[head], values, 1, 1) - deltas[head])).astype(BF)
                made.append(carry[head] + dot(score_low, keys))
                dk = dk + dot(score_low, queries[head], 0, 0)
                dv = dv + dot(probs.astype(BF), grads[head], 0, 0)
            dk_acc[keys_at, :] += dk
            dv_acc[keys_at, :] += dv
            return tuple(made)

        start = (jnp.zeros((BQ, 128), F32),) * 2
        done = lax.fori_loop(bounds_ref[block, 0], bounds_ref[block, 1], body, start)
        at = pl.ds(local + block * BQ, BQ)
        grad = jnp.where(first, done[0], done[1]) * SCALE
        dq_ref[rows, :] = rotate_lanes(grad, cos_ref[at, :], -sin_ref[at, :]).astype(BF)
    dk_ref[...] = rotate_lanes(dk_acc[...], cos_ref[...], -sin_ref[...]).astype(BF)
    dv_ref[...] = dv_acc[...].astype(BF)


def attend_back(bounds, queries, keys, values, mixed, grad, lse, seg_q, seg_k, cosine, sine):
    local, width = queries.shape
    long = keys.shape[0]
    groups = width // 128
    short_spec = pl.BlockSpec((local, 128), lambda g, b: (0, g))
    long_spec = pl.BlockSpec((long, 128), lambda g, b: (0, g))
    return pl.pallas_call(
        attend_back_kernel,
        grid_spec=pltpu.PrefetchScalarGridSpec(
            num_scalar_prefetch=1,
            grid=(groups,),
            in_specs=[
                short_spec,
                long_spec,
                long_spec,
                short_spec,
                short_spec,
                pl.BlockSpec((1, local, 128), lambda g, b: (g, 0, 0)),
                pl.BlockSpec((local, 128), lambda g, b: (0, 0)),
                pl.BlockSpec((8, long), lambda g, b: (0, 0)),
                pl.BlockSpec((long, 128), lambda g, b: (0, 0)),
                pl.BlockSpec((long, 128), lambda g, b: (0, 0)),
            ],
            out_specs=[short_spec, long_spec, long_spec],
            scratch_shapes=[pltpu.VMEM((long, 128), F32)] * 2,
        ),
        out_shape=[
            jax.ShapeDtypeStruct((local, width), BF),
            jax.ShapeDtypeStruct((long, width), BF),
            jax.ShapeDtypeStruct((long, width), BF),
        ],
        compiler_params=pltpu.CompilerParams(vmem_limit_bytes=40 * 2**20),
        cost_estimate=pl.CostEstimate(flops=5 * 2**30, bytes_accessed=16 * 2**20, transcendentals=4 * 2**20),
    )(bounds, queries, keys, values, mixed, grad, lse, seg_q, seg_k, cosine, sine)


CB = 256
HIGH = lax.Precision.HIGHEST


def halves(values):
    high = values.astype(BF)
    return high, (values - high.astype(F32)).astype(BF)


def contrast_kernel(
    info_ref, emb_ref, segc_ref, counts_ref, positive_ref, temp_ref, grad_ref, loss_ref, tgrad_ref,
    unit, docs, marks, ratio, ones_, out,
):
    own0, query_blocks, doc0 = info_ref[0], info_ref[1], info_ref[2]
    blocks = emb_ref.shape[0] // CB
    own_blocks = grad_ref.shape[0] // CB
    lane = lax.broadcasted_iota(jnp.int32, (1, 128), 1)
    loss_scale = temp_ref[0, 1]
    temp_inv = jnp.exp(-temp_ref[0:1, 0:1])
    segs = segc_ref[...]
    docs[...] = jnp.where((segs - NQ == lane) | ((segs == lane) & (lane >= NQ)), 1.0, 0.0).astype(BF)
    marks[...] = jnp.where((segs == lane) & (lane < NQ), 1.0, 0.0)
    out[...] = jnp.zeros_like(out)
    loss = jnp.zeros((1, 1), F32)
    tgrad = jnp.zeros((1, 1), F32)

    def at(index):
        return pl.ds(pl.multiple_of(index * CB, CB), CB)

    def similar(rows, columns):
        return jnp.exp(10.0 * (dot(unit[at(rows), :], unit[at(columns), :], 1, 1) - 1.0))

    for prefix in (EMB, EMB * 3 // 4, EMB // 2):
        emb = jnp.where(lane < prefix, emb_ref[...].astype(F32), 0.0)
        scale_full = lax.rsqrt(jnp.sum(emb * emb, axis=1, keepdims=True) + eps_unit)
        unit[...] = (emb * scale_full).astype(BF)

        def total_rows(index, seg_sum):
            def total_cols(column, total):
                high, low = halves(similar(index, column))
                mask = docs[at(column), :]
                return total + dot(high, mask) + dot(low, mask)

            total = lax.fori_loop(doc0, blocks, total_cols, jnp.zeros((CB, 128), F32))
            total = jnp.where(lane < NQ, total, 1.0)
            ratio[at(index), :] = 1.0 / total
            smooth = jnp.log(total) / 10.0 + 1.0
            return seg_sum + dot(marks[at(index), :], smooth, 0, 0, HIGH)

        seg_sum = lax.fori_loop(0, query_blocks, total_rows, jnp.zeros((128, 128), F32))
        valid = (lax.broadcasted_iota(jnp.int32, (NQ, 128), 1)) < NQ
        inv_counts = 1.0 / counts_ref[0:NQ, :]
        logits = jnp.where(valid, seg_sum[0:NQ, :] * inv_counts * temp_inv, 0.0)
        top = jnp.max(jnp.where(valid, logits, -1e30), axis=1, keepdims=True)
        powers = jnp.where(valid, jnp.exp(logits - top), 0.0)
        power_sum = jnp.sum(powers, axis=1, keepdims=True)
        positive = positive_ref[...]
        term = jnp.log(power_sum) + top - jnp.sum(logits * positive, axis=1, keepdims=True)
        loss = loss + jnp.sum(term, axis=0, keepdims=True) * loss_scale
        dlogits = (powers / power_sum - positive) * loss_scale
        tgrad = tgrad - jnp.sum(jnp.sum(dlogits * logits, axis=1, keepdims=True), axis=0, keepdims=True)
        ones_[...] = jnp.zeros_like(ones_)
        ones_[0:NQ, :] = dlogits * temp_inv * inv_counts

        def weigh(index, unused):
            weight = dot(marks[at(index), :], ones_[...], 1, 0, HIGH) * ratio[at(index), :]
            weight = jnp.where(lane < NQ, weight, 0.0)
            high = weight.astype(BF).astype(F32)
            ratio[at(index), :] = high + pltpu.roll(weight - high, NQ, 1)
            return unused

        lax.fori_loop(0, query_blocks, weigh, 0)

        def sim_grad(rows, columns):
            spread = dot(ratio[at(rows), :].astype(BF), docs[at(columns), :], 1, 1)
            return (similar(rows, columns) * spread).astype(BF)

        for own in range(own_blocks):
            mine = own0 + own

            def as_query(column, total):
                return total + dot(sim_grad(mine, column), unit[at(column), :])

            def as_doc(row, total):
                return total + dot(sim_grad(row, mine), unit[at(row), :], 0, 0)

            grad = jnp.zeros((CB, 128), F32)
            grad = lax.fori_loop(doc0, jnp.where(mine < query_blocks, blocks, doc0), as_query, grad)
            grad = lax.fori_loop(0, jnp.where(mine >= doc0, query_blocks, 0), as_doc, grad)
            part = jnp.where(lane < prefix, emb_ref[at(mine), :].astype(F32), 0.0)
            scale = lax.rsqrt(jnp.sum(part * part, axis=1, keepdims=True) + eps_unit)
            full = part * scale
            back = scale * (grad - full * jnp.sum(full * grad, axis=1, keepdims=True))
            out[pl.ds(own * CB, CB), :] += jnp.where(lane < prefix, back, 0.0)
    grad_ref[...] = out[...].astype(BF)
    loss_ref[...] = jnp.broadcast_to(loss, loss_ref.shape)
    tgrad_ref[...] = jnp.broadcast_to(tgrad, tgrad_ref.shape)


def contrast(info, emb_all, seg_col, counts, positive, temp_row, local):
    rows = emb_all.shape[0]
    return pl.pallas_call(
        contrast_kernel,
        in_specs=[pl.BlockSpec(memory_space=pltpu.SMEM)] + vmem_specs(5),
        out_specs=vmem_specs(3),
        out_shape=[
            jax.ShapeDtypeStruct((local, 128), BF),
            jax.ShapeDtypeStruct((8, 128), F32),
            jax.ShapeDtypeStruct((8, 128), F32),
        ],
        scratch_shapes=[
            pltpu.VMEM((rows, 128), BF),
            pltpu.VMEM((rows, 128), BF),
            pltpu.VMEM((rows, 128), F32),
            pltpu.VMEM((rows, 128), F32),
            pltpu.VMEM((128, 128), F32),
            pltpu.VMEM((local, 128), F32),
        ],
        compiler_params=pltpu.CompilerParams(vmem_limit_bytes=40 * 2**20),
        cost_estimate=pl.CostEstimate(flops=2**30, bytes_accessed=2**22, transcendentals=2**22),
    )(info, emb_all, seg_col, counts, positive, temp_row)


CW = 512
SLOTS_G, SLOTS_S, SLOTS_R, SLOTS_T, SLOTS_K = 3, 3, 4, 4, 6
SMALL_ROWS = 112


def neighbours():
    dp = lax.axis_index("dp")
    low = lax.rem(dp, 8)
    core = lax.rem(low, 2)
    x = lax.rem(low // 2, 2)
    y = low // 4
    return dp, low, core, x, y, dp + 1 - 2 * core, dp + 2 - 4 * x, dp + 4 - 8 * y


def entry_barrier(z, dp, plane, z_count):
    barrier = pltpu.get_barrier_semaphore()
    for other in plane:
        pl.semaphore_signal(barrier, inc=1, device_id={"dp": other, "tensor": z}, device_id_type=MESH)
    for step in range(1, z_count):
        peer = lax.rem(z + step, z_count)
        pl.semaphore_signal(barrier, inc=1, device_id={"dp": dp, "tensor": peer}, device_id_type=MESH)
    pl.semaphore_wait(barrier, len(plane) + z_count - 1)


def remote(src, dst, send_sem, recv_sem, dp, z):
    return pltpu.make_async_remote_copy(
        src_ref=src,
        dst_ref=dst,
        send_sem=send_sem,
        recv_sem=recv_sem,
        device_id={"dp": dp, "tensor": z},
        device_id_type=MESH,
    )


def scatter_kernel(
    window, attn_grad, normed, ffn_grad, dq, dk, dv, mixed, pre_grad, hidden, dxw, small_ref, proj_ref,
    out_qkv, out_attn, out_in, out_out, small_out, proj_out, from_left, from_right,
    xw, xa, xn, xf, gs, gkv, sbuf, rbuf, ta, tb, xra, xrb, s2a, s2b, yra, yrb, keep, zs, zrl, zrr,
    sacc, srec, zsm, pacc, prec, zpw,
    x_sem, g_sem, s_sem, r_sem, t_sem, xr_sem, s2_sem, yr_sem, zs_sem, zr_sem, sm_sem, smz_sem, h_sem, credit,
):
    dp, low, core, x, y, to_core, to_x, to_y = neighbours()
    z = lax.axis_index("tensor")
    nz = 4
    chunks = [("out", i) for i in range(8)] + [("in", i) for i in range(8)] + [("qa", i) for i in range(8)]
    count = len(chunks)
    local = attn_grad.shape[0]
    has_l = z > 0
    has_r = z < nz - 1

    x_loads = [
        pltpu.make_async_copy(src, dst, x_sem.at[index])
        for index, (src, dst) in enumerate(((ffn_grad, xf), (normed, xn), (window, xw), (attn_grad, xa)))
    ]
    for load in x_loads:
        load.start()

    def g_loads(index):
        kind, part = chunks[index]
        slot = index % SLOTS_G
        if kind != "qa":
            source = hidden if kind == "out" else pre_grad
            return [pltpu.make_async_copy(source.at[:, pl.ds(part * CW, CW)], gs.at[slot], g_sem.at[slot, 0])]
        columns = pl.ds((part // 2) * 256, 256)
        one, many = (dq, dk) if part % 2 == 0 else (mixed, dv)
        return [
            pltpu.make_async_copy(one.at[:, columns], gs.at[slot, :, pl.ds(0, 256)], g_sem.at[slot, 0]),
            pltpu.make_async_copy(many.at[:, columns], gkv.at[slot], g_sem.at[slot, 1]),
        ]

    for index in range(2):
        for load in g_loads(index):
            load.start()

    entry_barrier(z, dp, (to_core, to_x, to_y), nz)

    halo_l = remote(dxw.at[pl.ds(0, local)], from_right, h_sem.at[0], h_sem.at[1], dp, z - 1)
    halo_r = remote(dxw.at[pl.ds(2 * local, local)], from_left, h_sem.at[2], h_sem.at[3], dp, z + 1)

    peers = (to_core, to_x, to_y)

    def small_moves(stage):
        return [
            remote(sacc.at[stage], srec.at[stage], sm_sem.at[stage, 0], sm_sem.at[stage, 1], peers[stage], z),
            remote(pacc.at[stage], prec.at[stage], sm_sem.at[stage, 2], sm_sem.at[stage, 3], peers[stage], z),
        ]

    def small_z_moves(step):
        peer = lax.rem(z + step, nz)
        return [
            remote(sacc.at[3], zsm.at[step - 1], smz_sem.at[step - 1, 0], smz_sem.at[step - 1, 1], dp, peer),
            remote(pacc.at[3], zpw.at[step - 1], smz_sem.at[step - 1, 2], smz_sem.at[step - 1, 3], dp, peer),
        ]

    def small_stage(stage):
        if stage == 0:
            sacc[0] = small_ref[...]
            pacc[0] = proj_ref[...].astype(BF)
        if 1 <= stage <= 3:
            for move in small_moves(stage - 1):
                move.wait_recv()
            sacc[stage] = sacc[stage - 1] + srec[stage - 1]
            pacc[stage] = (pacc[stage - 1].astype(F32) + prec[stage - 1].astype(F32)).astype(BF)
        if stage <= 2:
            for move in small_moves(stage):
                move.start()
        if stage == 3:
            for step in range(1, nz):
                for move in small_z_moves(step):
                    move.start()
        if stage == 4:
            for step in range(1, nz):
                for move in small_z_moves(step):
                    move.wait_recv()
            for target, mine, others, low_rows in ((small_out, sacc, zsm, 0), (proj_out, pacc, zpw, 0)):
                total = None
                for owner in range(nz):
                    value = jnp.where(z == owner, mine[3].astype(F32), 0.0)
                    for step in range(1, nz):
                        value = jnp.where(lax.rem(z - step + nz, nz) == owner, others[step - 1].astype(F32), value)
                    total = value if total is None else total + value
                target[...] = total

    def block_columns(j, core_bit):
        xj = lax.rem(j, 2)
        yj = j // 2
        block = core_bit + 2 * (x + xj - 2 * x * xj) + 4 * (y + yj - 2 * y * yj)
        return pl.ds(pl.multiple_of(block * 128, 128), 128)

    def product(index, j, core_bit):
        kind, part = chunks[index]
        slot = index % SLOTS_G
        at = block_columns(j, core_bit)
        if kind == "out":
            return dot(xf[:, at], gs[slot], 0, 0)
        if kind == "in":
            return dot(xn[:, at], gs[slot], 0, 0)
        one = xw[pl.ds(local, local), at] if part % 2 == 0 else xa[:, at]
        return jnp.concatenate(
            [dot(one, gs[slot, :, 0:256], 0, 0), dot(xw[:, at], gkv[slot], 0, 0)], axis=1
        )

    def core_move(index):
        return remote(
            sbuf.at[index % SLOTS_S], rbuf.at[index % SLOTS_R], s_sem.at[index % SLOTS_S], r_sem.at[index % SLOTS_R],
            to_core, z,
        )

    half = CW // 2

    def ta_move(index):
        slot = index % SLOTS_T
        return remote(ta.at[slot, pl.ds(2, 2)], xra.at[index], t_sem.at[slot, 0], xr_sem.at[index, 0], to_x, z)

    def tb_move(index):
        slot = index % SLOTS_T
        return remote(tb.at[slot, pl.ds(2, 2)], xrb.at[index], t_sem.at[slot, 1], xr_sem.at[index, 1], to_y, z)

    def s2a_move(index):
        return remote(s2a.at[index], yra.at[index], s2_sem.at[index, 0], yr_sem.at[index, 0], to_y, z)

    def s2b_move(index):
        return remote(s2b.at[index], yrb.at[index], s2_sem.at[index, 1], yr_sem.at[index, 1], to_x, z)

    def right_move(index):
        return remote(zs.at[index], zrl.at[index], zs_sem.at[index], zr_sem.at[index, 0], dp, z + 1)

    def left_move(index):
        return remote(zs.at[index], zrr.at[index], zs_sem.at[index], zr_sem.at[index, 1], dp, z - 1)

    def stage_one(index):
        kind, part = chunks[index]
        if index == 0:
            x_loads[0].wait()
        if kind == "in" and part == 0:
            x_loads[1].wait()
        if kind == "qa" and part == 0:
            x_loads[2].wait()
            x_loads[3].wait()
        for load in g_loads(index):
            load.wait()
        if index >= SLOTS_S:
            core_move(index - SLOTS_S).wait_send()

        def body(j, unused):
            sbuf[index % SLOTS_S, j] = product(index, j, 1 - core).astype(BF)
            return unused

        lax.fori_loop(0, 4, body, 0)
        if index >= SLOTS_R:
            pl.semaphore_wait(credit, 1)
        core_move(index).start()

    def stage_two(index):
        core_move(index).wait_recv()
        slot = index % SLOTS_T
        if index >= SLOTS_T:
            ta_move(index - SLOTS_T).wait_send()
            tb_move(index - SLOTS_T).wait_send()

        def body(j, unused):
            total = product(index, j, core) + rbuf[index % SLOTS_R, j].astype(F32)
            ta[slot, j // 2 + 2 * lax.rem(j, 2)] = total[:, :half].astype(BF)
            tb[slot, j] = total[:, half:].astype(BF)
            return unused

        lax.fori_loop(0, 4, body, 0)
        if index + SLOTS_R < count:
            pl.semaphore_signal(credit, inc=1, device_id={"dp": to_core, "tensor": z}, device_id_type=MESH)
        ta_move(index).start()
        tb_move(index).start()

    def stage_three(index):
        slot = index % SLOTS_T
        kslot = index % SLOTS_K
        ta_move(index).wait_recv()
        s2a[index] = (ta[slot, 1].astype(F32) + xra[index, 1].astype(F32)).astype(BF)
        s2a_move(index).start()
        keep[kslot, :, :half] = ta[slot, 0].astype(F32) + xra[index, 0].astype(F32)
        tb_move(index).wait_recv()
        s2b[index] = (tb[slot, 1].astype(F32) + xrb[index, 1].astype(F32)).astype(BF)
        s2b_move(index).start()
        keep[kslot, :, half:] = tb[slot, 0].astype(F32) + xrb[index, 0].astype(F32)

    def stage_four(index):
        kslot = index % SLOTS_K
        goal = chunks[index][1] // 2
        s2a_move(index).wait_recv()
        keep[kslot, :, :half] += yra[index].astype(F32)
        s2b_move(index).wait_recv()
        keep[kslot, :, half:] += yrb[index].astype(F32)
        if goal > 0:

            @pl.when(z == 0)
            def _():
                zs[index] = keep[kslot].astype(BF)
                right_move(index).start()

        if goal < nz - 1:

            @pl.when(z == nz - 1)
            def _():
                zs[index] = keep[kslot].astype(BF)
                left_move(index).start()

    def stage_five(index, hop):
        kslot = index % SLOTS_K
        kind, part = chunks[index]
        goal = part // 2
        if hop <= goal:

            @pl.when(z == hop)
            def _():
                right_move(index).wait_recv()
                keep[kslot] += zrl[index].astype(F32)
                if hop < goal:
                    zs[index] = keep[kslot].astype(BF)
                    right_move(index).start()

        if hop <= nz - 1 - goal:

            @pl.when(z == nz - 1 - hop)
            def _():
                left_move(index).wait_recv()
                keep[kslot] += zrr[index].astype(F32)
                if nz - 1 - hop > goal:
                    zs[index] = keep[kslot].astype(BF)
                    left_move(index).start()

        if hop == nz - 1:

            @pl.when(z == goal)
            def _():
                if kind == "qa":
                    if part % 2 == 0:
                        out_qkv[:, 0:512] = keep[kslot]
                    else:
                        out_attn[...] = keep[kslot, :, 0:256]
                        out_qkv[:, 512:768] = keep[kslot, :, 256:512]
                else:
                    target = out_in if kind == "in" else out_out
                    target[:, pl.ds((part % 2) * CW, CW)] = keep[kslot]

    lag_three, lag_four = 3, 4
    for step in range(count + lag_four + nz):
        if step < count:
            stage_one(step)
        if step == 0:
            small_stage(0)
            pl.when(has_l)(lambda: halo_l.start())
            pl.when(has_r)(lambda: halo_r.start())
        if 0 <= step - 1 < count:
            stage_two(step - 1)
        if step + 2 < count:
            for load in g_loads(step + 2):
                load.start()
        if step in (2, 4, 6, 8):
            small_stage(step // 2)
        if 0 <= step - lag_three < count:
            stage_three(step - lag_three)
        if 0 <= step - lag_four < count:
            stage_four(step - lag_four)
        for hop in range(1, nz):
            index = step - lag_four - hop
            if 0 <= index < count:
                stage_five(index, hop)

    for index in range(count):
        goal = chunks[index][1] // 2
        if index >= count - SLOTS_S:
            core_move(index).wait_send()
        if index >= count - SLOTS_T:
            ta_move(index).wait_send()
            tb_move(index).wait_send()
        s2a_move(index).wait_send()
        s2b_move(index).wait_send()
        pl.when(z < goal)(lambda index=index: right_move(index).wait_send())
        pl.when(z > goal)(lambda index=index: left_move(index).wait_send())
    for stage in range(3):
        for move in small_moves(stage):
            move.wait_send()
    for step in range(1, nz):
        for move in small_z_moves(step):
            move.wait_send()

    @pl.when(has_l)
    def _():
        halo_l.wait_send()
        halo_r.wait_recv()

    @pl.when(has_r)
    def _():
        halo_r.wait_send()
        halo_l.wait_recv()


def scatter(window, attn_grad, normed, ffn_grad, dq, dk, dv, mixed, pre_grad, hidden, dxw, small, proj_grad):
    local, width = attn_grad.shape
    long = window.shape[0]
    dma = pltpu.SemaphoreType.DMA
    n = 24
    half = CW // 2
    shape = jax.ShapeDtypeStruct
    return pl.pallas_call(
        scatter_kernel,
        in_specs=hbm_specs(11) + vmem_specs(2),
        out_specs=vmem_specs(6) + hbm_specs(2),
        out_shape=[
            shape((128, 768), F32),
            shape((128, 256), F32),
            shape((128, 1024), F32),
            shape((128, 1024), F32),
            shape(small.shape, F32),
            shape(proj_grad.shape, F32),
            shape((local, width), BF),
            shape((local, width), BF),
        ],
        scratch_shapes=[
            pltpu.VMEM((long, width), BF),
            pltpu.VMEM((local, width), BF),
            pltpu.VMEM((local, width), BF),
            pltpu.VMEM((local, width), BF),
            pltpu.VMEM((SLOTS_G, local, CW), BF),
            pltpu.VMEM((SLOTS_G, long, 256), BF),
            pltpu.VMEM((SLOTS_S, 4, 128, CW), BF),
            pltpu.VMEM((SLOTS_R, 4, 128, CW), BF),
            pltpu.VMEM((SLOTS_T, 4, 128, half), BF),
            pltpu.VMEM((SLOTS_T, 4, 128, half), BF),
            pltpu.VMEM((n, 2, 128, half), BF),
            pltpu.VMEM((n, 2, 128, half), BF),
            pltpu.VMEM((n, 128, half), BF),
            pltpu.VMEM((n, 128, half), BF),
            pltpu.VMEM((n, 128, half), BF),
            pltpu.VMEM((n, 128, half), BF),
            pltpu.VMEM((SLOTS_K, 128, CW), F32),
            pltpu.VMEM((n, 128, CW), BF),
            pltpu.VMEM((n, 128, CW), BF),
            pltpu.VMEM((n, 128, CW), BF),
            pltpu.VMEM((4,) + small.shape, F32),
            pltpu.VMEM((3,) + small.shape, F32),
            pltpu.VMEM((3,) + small.shape, F32),
            pltpu.VMEM((4,) + proj_grad.shape, BF),
            pltpu.VMEM((3,) + proj_grad.shape, BF),
            pltpu.VMEM((3,) + proj_grad.shape, BF),
            dma((4,)),
            dma((SLOTS_G, 2)),
            dma((SLOTS_S,)),
            dma((SLOTS_R,)),
            dma((SLOTS_T, 2)),
            dma((n, 2)),
            dma((n, 2)),
            dma((n, 2)),
            dma((n,)),
            dma((n, 2)),
            dma((3, 4)),
            dma((3, 4)),
            dma((4,)),
            pltpu.SemaphoreType.REGULAR,
        ],
        compiler_params=pltpu.CompilerParams(
            collective_id=2, has_side_effects=True, vmem_limit_bytes=VMEM_BIG
        ),
    )(window, attn_grad, normed, ffn_grad, dq, dk, dv, mixed, pre_grad, hidden, dxw, small, proj_grad)


def source_rows(kind, ref, start, rows):
    return ref.at[:, pl.ds(start, rows), :] if kind == "qkv" else ref.at[pl.ds(start, rows), :]


def gathered_rows(kind, ref, shard, start, rows):
    if kind == "qkv":
        return ref.at[:, pl.ds(start, rows), pl.ds(pl.multiple_of(shard * 256, 256), 256)]
    if kind == "in":
        return ref.at[pl.ds(start, rows), pl.ds(pl.multiple_of(shard * 1024, 1024), 1024)]
    per = ref.shape[0] // 4
    return ref.at[pl.ds(pl.multiple_of(shard * per + start, 16), rows), :]


def shard_rows(kind, ref):
    return ref.shape[1] if kind == "qkv" else ref.shape[0]


def gather_kernel(kinds, with_tokens, *refs):
    n = len(kinds)
    nz = 4
    srcs, refs = refs[:n], refs[n:]
    if with_tokens:
        (tokens, bias), refs = refs[:2], refs[2:]
    outs, refs = refs[:n], refs[n:]
    if with_tokens:
        (window, bias_all), refs = refs[:2], refs[2:]
    z_recv, z_send, p_recv, p_send, l_sem = refs[:5]
    stage, refs = refs[5 : 5 + n], refs[5 + n :]
    if with_tokens:
        h_sem, b_sem, token_stage = refs
    dp, low, core, x, y, to_core, to_x, to_y = neighbours()
    z = lax.axis_index("tensor")
    has_l = z > 0
    has_r = z < nz - 1
    low_x = low + 2 - 4 * x
    low_y = low + 4 - 8 * y
    low_xy = low_x + 4 - 8 * y

    copies_in = [pltpu.make_async_copy(srcs[m], stage[m], l_sem.at[m, 0]) for m in range(n)]
    copies_out = [
        pltpu.make_async_copy(
            stage[m], gathered_rows(kinds[m], outs[m], z, 0, shard_rows(kinds[m], srcs[m])), l_sem.at[m, 1]
        )
        for m in range(n)
    ]
    for copy in copies_in:
        copy.start()
    if with_tokens:
        token_in = pltpu.make_async_copy(tokens, token_stage, h_sem.at[7])
        token_in.start()
        bias_all[pl.ds(z, 1)] = bias[...].reshape(1, *bias.shape)
    entry_barrier(z, dp, (to_core, to_x, to_y), nz)

    def piece(m, shard, index, half=None):
        rows = shard_rows(kinds[m], srcs[m]) // 8
        start = index * rows
        if half is not None:
            rows = rows // 2
            start = start + half * rows
        return gathered_rows(kinds[m], outs[m], shard, pl.multiple_of(start, 16), rows)

    def shard_of(side, distance):
        return z - distance if side == 0 else z + distance

    def onward(side):
        return z + 1 if side == 0 else z - 1

    def can_send(side):
        return has_r if side == 0 else has_l

    def arrives(side, distance):
        return z >= distance if side == 0 else z + distance < nz

    def own_move(m, side):
        rows = shard_rows(kinds[m], srcs[m]) // 8
        src = source_rows(kinds[m], srcs[m], pl.multiple_of(low * rows, 16), rows)
        return remote(src, piece(m, z, low), z_send.at[m, side, 0], z_recv.at[m, side, 0], dp, onward(side))

    def relay_move(m, side, distance):
        at = piece(m, shard_of(side, distance), low)
        return remote(at, at, z_send.at[m, side, distance], z_recv.at[m, side, distance], dp, onward(side))

    def plane_move(m, side, distance, kind):
        shard = shard_of(side, distance)
        at = {
            0: (low, None), 1: (low, None), 4: (low, None), 2: (low_x, 0), 3: (low_y, 1),
            5: (low_x, None), 6: (low_y, None), 7: (low_xy, 0), 8: (low_xy, 1),
        }[kind]
        ref = piece(m, shard, *at)
        to = {0: to_x, 1: to_y, 2: to_y, 3: to_x}.get(kind, to_core)
        slot = side * 3 + distance - 1
        return remote(ref, ref, p_send.at[m, slot, kind], p_recv.at[m, slot, kind], to, z)

    if with_tokens:
        local = tokens.shape[0]
        to_left = remote(tokens, window.at[pl.ds(2 * local, local)], h_sem.at[0], h_sem.at[1], dp, z - 1)
        to_right = remote(tokens, window.at[pl.ds(0, local)], h_sem.at[2], h_sem.at[3], dp, z + 1)
        own_tokens = pltpu.make_async_copy(token_stage, window.at[pl.ds(local, local)], h_sem.at[4])
        fill_left = pltpu.make_async_copy(token_stage, window.at[pl.ds(0, local)], h_sem.at[5])
        fill_right = pltpu.make_async_copy(token_stage, window.at[pl.ds(2 * local, local)], h_sem.at[6])

        def bias_move(step):
            peer = lax.rem(z + step, nz)
            return remote(bias, bias_all.at[z], b_sem.at[0, step - 1], b_sem.at[1, step - 1], dp, peer)

        for step in range(1, nz):
            bias_move(step).start()

    def own_start(m):
        for side in (0, 1):
            pl.when(can_send(side))(lambda side=side: own_move(m, side).start())

    own_start(0)
    if with_tokens:
        token_in.wait()
        own_tokens.start()
        pl.when(jnp.logical_not(has_l))(lambda: fill_left.start())
        pl.when(jnp.logical_not(has_r))(lambda: fill_right.start())
    for copy_in, copy_out in zip(copies_in, copies_out):
        copy_in.wait()
        copy_out.start()

    def stage_z(m, distance, side):
        if side == 0 and distance == 2 and m + 1 < n:
            own_start(m + 1)
        if side == 0 and distance == 3 and with_tokens and m == 0:
            pl.when(has_l)(lambda: to_left.start())
            pl.when(has_r)(lambda: to_right.start())

        @pl.when(arrives(side, distance))
        def _():
            if distance == 1:
                own_move(m, side).wait_recv()
            else:
                relay_move(m, side, distance - 1).wait_recv()
            if distance < 3:
                pl.when(can_send(side))(lambda: relay_move(m, side, distance).start())
            for kind in (0, 1, 4):
                plane_move(m, side, distance, kind).start()

    def stage_xy(m, distance, side):
        @pl.when(arrives(side, distance))
        def _():
            for kind in (0, 1):
                plane_move(m, side, distance, kind).wait_recv()
                plane_move(m, side, distance, kind + 2).start()
                plane_move(m, side, distance, kind + 5).start()

    def stage_diagonal(m, distance, side):
        @pl.when(arrives(side, distance))
        def _():
            for kind in (2, 3):
                plane_move(m, side, distance, kind).wait_recv()
                plane_move(m, side, distance, kind + 5).start()

    events = [(m, distance, side) for m in range(n) for distance in (1, 2, 3) for side in (0, 1)]
    lag = 4
    for step in range(len(events) + 2 * lag):
        if step < len(events):
            stage_z(*events[step])
        if 0 <= step - lag < len(events):
            stage_xy(*events[step - lag])
        if 0 <= step - 2 * lag < len(events):
            stage_diagonal(*events[step - 2 * lag])

    for m, distance, side in events:

        @pl.when(arrives(side, distance))
        def _():
            for kind in (4, 5, 6, 7, 8):
                plane_move(m, side, distance, kind).wait_recv()
            for kind in range(9):
                plane_move(m, side, distance, kind).wait_send()
            if distance < 3:
                pl.when(can_send(side))(lambda: relay_move(m, side, distance).wait_send())

    for m in range(n):
        for side in (0, 1):
            pl.when(can_send(side))(lambda side=side: own_move(m, side).wait_send())
        copies_out[m].wait()
    if with_tokens:
        own_tokens.wait()
        for step in range(1, nz):
            bias_move(step).wait()

        @pl.when(has_l)
        def _():
            to_left.wait_send()
            to_right.wait_recv()

        @pl.when(has_r)
        def _():
            to_right.wait_send()
            to_left.wait_recv()

        pl.when(jnp.logical_not(has_l))(lambda: fill_left.wait())
        pl.when(jnp.logical_not(has_r))(lambda: fill_right.wait())


def gather(kinds, arrays, collective_id, tokens=None, bias=None):
    n = len(kinds)
    with_tokens = tokens is not None
    width = 1024
    shapes = {"qkv": (3, width, width), "attn": (width, width), "in": (width, 4 * width), "out": (4 * width, width)}
    out_shape = [jax.ShapeDtypeStruct(shapes[kind], BF) for kind in kinds]
    in_specs = hbm_specs(n)
    out_specs = hbm_specs(n)
    dma = pltpu.SemaphoreType.DMA
    scratch = [dma((n, 2, 3)), dma((n, 2, 3)), dma((n, 6, 9)), dma((n, 6, 9)), dma((n, 2))]
    scratch += [pltpu.VMEM(array.shape, BF) for array in arrays]
    args = list(arrays)
    if with_tokens:
        args += [tokens, bias]
        in_specs += hbm_specs(1) + vmem_specs(1)
        out_specs += hbm_specs(1) + vmem_specs(1)
        out_shape += [
            jax.ShapeDtypeStruct((3 * tokens.shape[0], width), BF),
            jax.ShapeDtypeStruct((4,) + bias.shape, BF),
        ]
        scratch += [dma((8,)), dma((2, 3)), pltpu.VMEM(tokens.shape, BF)]
    return pl.pallas_call(
        partial(gather_kernel, tuple(kinds), with_tokens),
        in_specs=in_specs,
        out_specs=out_specs,
        out_shape=out_shape,
        scratch_shapes=scratch,
        compiler_params=pltpu.CompilerParams(
            collective_id=collective_id, has_side_effects=True, vmem_limit_bytes=40 * 2**20
        ),
    )(*args)


def norm_forward(values, gain, shift):
    mean_value = jnp.mean(values, axis=-1, keepdims=True)
    centered = values - mean_value
    variance = jnp.mean(centered * centered, axis=-1, keepdims=True)
    scale = lax.rsqrt(variance + eps_norm)
    unit = centered * scale
    return unit * gain + shift, unit, scale


def norm_back(unit, scale, gain, grad):
    dn = grad * gain
    back = scale * (
        dn - jnp.mean(dn, axis=-1, keepdims=True) - unit * jnp.mean(dn * unit, axis=-1, keepdims=True)
    )
    return back, jnp.sum(grad * unit, axis=0), jnp.sum(grad, axis=0)


def per_device(
    tokens, lengths, doc_pairs, qkv_weight, qkv_bias, attn_weight, attn_bias, ffn_in_weight, ffn_in_bias,
    ffn_out_weight, ffn_out_bias, norm_gains, norm_shifts, proj_weight, log_temp,
):
    local, width = tokens.shape
    dp_count = lax.axis_size("dp")
    tensor_count = lax.axis_size("tensor")
    groups = dp_count // 8
    z = lax.axis_index("tensor")
    base = z * local

    row_lengths = lengths[0]
    seg_range = jnp.arange(SEGS, dtype=jnp.int32)
    seg_ends = jnp.sum(jnp.where(seg_range[:, None] >= seg_range[None, :], row_lengths[None, :], 0), axis=1)
    seg_starts = seg_ends - row_lengths
    positions = jnp.arange(SEQ, dtype=jnp.int32)
    seg_ids = jnp.sum((positions[:, None] >= seg_ends[None, :]).astype(jnp.int32), axis=1)
    near = jnp.arange(3 * local, dtype=jnp.int32) + base - local
    near_ids = jnp.sum((near[:, None] >= seg_ends[None, :]).astype(jnp.int32), axis=1)
    near_ids = jnp.where((near >= 0) & (near < SEQ), near_ids, -1)
    near_member = near_ids[:, None] == jnp.arange(SEGS, dtype=jnp.int32)[None, :]
    near_starts = jnp.sum(jnp.where(near_member, seg_starts[None, :], 0), axis=1)
    offsets = jnp.where(near_ids >= 0, near - near_starts, 0)
    half_dim = HDIM // 2
    inv_freq = jnp.exp(jnp.arange(half_dim, dtype=F32) * (-2.0 * math.log(10000.0) / HDIM))
    angles = offsets.astype(F32)[:, None] * inv_freq[None, :]
    cosine, sine = jnp.cos(angles), jnp.sin(angles)
    cosine = jnp.concatenate([cosine] * 4, axis=1)
    sine = jnp.concatenate([-sine, sine] * 2, axis=1)
    seg_q = jnp.broadcast_to(lax.slice_in_dim(near_ids, local, 2 * local)[:, None], (local, 128))
    seg_k = jnp.broadcast_to(near_ids[None, :], (8, 3 * local))
    starts_at = jnp.arange(local // BQ, dtype=jnp.int32) * BQ + base
    first_seg = jnp.sum((starts_at[:, None] >= seg_ends[None, :]).astype(jnp.int32), axis=1)
    last_seg = jnp.sum(((starts_at + BQ - 1)[:, None] >= seg_ends[None, :]).astype(jnp.int32), axis=1)
    first_key = jnp.sum(jnp.where(first_seg[:, None] == seg_range, seg_starts, 0), axis=1) - base + local
    last_key = jnp.sum(jnp.where(last_seg[:, None] == seg_range, seg_ends, 0), axis=1) - base + local
    bounds = jnp.stack([first_key // BK, (last_key + BK - 1) // BK], axis=1)
    query_end = seg_ends[NQ - 1]
    info = jnp.stack([base // CB, (query_end + CB - 1) // CB, query_end // CB])
    seg_col = jnp.broadcast_to(seg_ids[:, None], (SEQ, 128))
    counts = jnp.broadcast_to(row_lengths.astype(F32)[:, None], (SEGS, 128))
    positive = (doc_pairs[0][:, None] == jnp.arange(128, dtype=jnp.int32)[None, :]).astype(F32)
    loss_scale = 1.0 / (NQ * dp_count)
    temp_row = jnp.concatenate([log_temp, jnp.full((127,), loss_scale, F32)]).reshape(1, 128)

    gains = norm_gains.astype(F32)
    shifts = norm_shifts.astype(F32)
    bias = jnp.concatenate([qkv_bias.reshape(6, 128), ffn_in_bias.reshape(8, 128), jnp.zeros((2, 128), BF)])
    qkv_all, window, bias_all = gather(("qkv",), (jnp.transpose(qkv_weight, (1, 0, 2)),), 0, tokens, bias)
    attn_all, in_all, out_all = gather(("attn", "in", "out"), (attn_weight, ffn_in_weight, ffn_out_weight), 1)
    qkv_bias_all = jnp.transpose(bias_all[:, :6].reshape(4, 3, 256), (1, 0, 2)).reshape(3, 1, width)
    in_bias_all = bias_all[:, 6:14].reshape(4 * width).astype(F32)

    queries, keys, values = project(window, qkv_all, qkv_bias_all, cosine, sine)
    mixed, lse = attend(bounds, queries, keys, values, seg_q, seg_k)
    attn_out = dot(mixed, attn_all) + attn_bias.astype(F32)
    normed, unit_one, scale_one = norm_forward(tokens.astype(F32) + attn_out, gains[0], shifts[0])
    normed_low = normed.astype(BF)
    ffn_pre = dot(normed_low, in_all) + in_bias_all
    hidden = jax.nn.gelu(ffn_pre, approximate=False).astype(BF)
    resid_two = normed + dot(hidden, out_all) + ffn_out_bias.astype(F32)
    output, unit_two, scale_two = norm_forward(resid_two, gains[1], shifts[1])
    output_low = output.astype(BF)
    embedded = dot(output_low, proj_weight).astype(BF)
    embedded_all = lax.all_gather(embedded, "tensor", axis=0, tiled=True)
    emb_grad, row_loss, row_temp = contrast(info, embedded_all, seg_col, counts, positive, temp_row, local)

    proj_grad = dot(output_low, emb_grad, 0, 0)
    output_grad = dot(emb_grad, proj_weight, 1, 1)
    resid_two_grad, gain_two_grad, shift_two_grad = norm_back(unit_two, scale_two, gains[1], output_grad)
    ffn_grad = resid_two_grad.astype(BF)
    out_bias_grad = jnp.sum(ffn_grad.astype(F32), axis=0)
    hidden_grad = dot(ffn_grad, out_all, 1, 1)
    unused, gelu_pull = jax.vjp(partial(jax.nn.gelu, approximate=False), ffn_pre)
    pre_grad = gelu_pull(hidden_grad)[0].astype(BF)
    in_bias_grad = jnp.sum(pre_grad.astype(F32), axis=0)
    normed_grad = dot(pre_grad, in_all, 1, 1) + resid_two_grad
    resid_one_grad, gain_one_grad, shift_one_grad = norm_back(unit_one, scale_one, gains[0], normed_grad)
    attn_grad = resid_one_grad.astype(BF)
    attn_bias_grad = jnp.sum(attn_grad.astype(F32), axis=0)
    mixed_grad = dot(attn_grad, attn_all, 1, 1).astype(BF)
    dq, dk, dv = attend_back(bounds, queries, keys, values, mixed, mixed_grad, lse, seg_q, seg_k, cosine, sine)
    window_grad = dot(dk, qkv_all[1], 1, 1) + dot(dv, qkv_all[2], 1, 1)
    window_low = window_grad.astype(BF)
    own_grad = window_grad[local : 2 * local] + dot(dq, qkv_all[0], 1, 1) + resid_one_grad
    qkv_bias_grad = jnp.concatenate([jnp.sum(part.astype(F32), axis=0) for part in (dq, dk, dv)])

    share = 1.0 / tensor_count
    small = jnp.concatenate(
        [
            attn_bias_grad, out_bias_grad, gain_one_grad, gain_two_grad, shift_one_grad, shift_two_grad,
            qkv_bias_grad, in_bias_grad, row_loss[0, :1] * share, row_temp[0, :1] * share,
            jnp.zeros((SMALL_ROWS * 128 - 13 * width - 2,), F32),
        ]
    ).reshape(SMALL_ROWS, 128)

    def arrange(array):
        if groups == 1:
            return array
        rows = array.shape[0]
        return array.reshape(rows, groups, 8, -1).transpose(0, 2, 1, 3).reshape(rows, width)

    qkv_red, attn_red, in_red, out_red, small, proj_red, from_left, from_right = scatter(
        arrange(window), arrange(attn_grad), arrange(normed_low), arrange(ffn_grad),
        dq, dk, dv, mixed, pre_grad, hidden, window_low, small, proj_grad,
    )
    if groups > 1:
        ranks = [[high * 8 + low for high in range(groups)] for low in range(8)]
        qkv_red, attn_red, in_red, out_red = (
            lax.psum_scatter(part, "dp", scatter_dimension=0, axis_index_groups=ranks, tiled=True)
            for part in (qkv_red, attn_red, in_red, out_red)
        )
        small, proj_red = lax.psum((small, proj_red), "dp", axis_index_groups=ranks)
    tokens_grad = (
        own_grad
        + jnp.where(z > 0, from_left.astype(F32), 0.0)
        + jnp.where(z < tensor_count - 1, from_right.astype(F32), 0.0)
    )
    flat = small.reshape(-1)

    def cut(start, length):
        return lax.slice_in_dim(flat, start * width, (start + length) * width)

    qkv_bias_red = lax.dynamic_slice_in_dim(cut(6, 3).reshape(3, width), z * 256, 256, 1)
    in_bias_red = lax.dynamic_slice_in_dim(cut(9, 4), z * width, width, 0)
    return (
        flat[13 * width : 13 * width + 1],
        output_low,
        tokens_grad,
        qkv_red.reshape(-1, 3, 256),
        qkv_bias_red,
        attn_red.T,
        cut(0, 1),
        in_red,
        in_bias_red,
        out_red.T,
        cut(1, 1),
        cut(2, 2).reshape(2, width),
        cut(4, 2).reshape(2, width),
        proj_red,
        flat[13 * width + 1 : 13 * width + 2],
    )


def solution(mesh):
    in_specs = (
        P(("dp", "tensor"), None),
        P("dp", None),
        P("dp", None),
        P(None, None, "tensor"),
        P(None, "tensor"),
        P("tensor", None),
        P(),
        P(None, "tensor"),
        P("tensor"),
        P("tensor", None),
        P(),
        P(),
        P(),
        P(),
        P(),
    )
    out_specs = (
        P(),
        P(("dp", "tensor"), None),
        P(("dp", "tensor"), None),
        P("dp", None, "tensor"),
        P(None, "tensor"),
        P("tensor", "dp"),
        P(),
        P("dp", "tensor"),
        P("tensor"),
        P("tensor", "dp"),
        P(),
        P(),
        P(),
        P(),
        P(),
    )
    return jax.shard_map(
        per_device, mesh=mesh, in_specs=in_specs, out_specs=out_specs, check_vma=False
    )
```

```python
from functools import partial
import math

import jax
import jax.numpy as jnp
from jax import lax
from jax.experimental import pallas as pl
from jax.experimental.pallas import tpu as pltpu
from jax.sharding import PartitionSpec as P

HDIM = 64
EMB = 128
SEQ = 2048
SEGS = 16
NQ = 8
MESH = pl.DeviceIdType.MESH
ANY = pl.ANY
F32 = jnp.float32
BF = jnp.bfloat16
eps_norm = 1e-05
eps_unit = 1e-06
VMEM_BIG = 60 * 1024 * 1024


def dot(left, right, left_dim=1, right_dim=0, precision=None):
    return lax.dot_general(
        left,
        right,
        (((left_dim,), (right_dim,)), ((), ())),
        preferred_element_type=F32,
        precision=precision,
    )


def hbm_specs(count):
    return [pl.BlockSpec(memory_space=ANY)] * count


def vmem_specs(count):
    return [pl.BlockSpec(memory_space=pltpu.VMEM)] * count


def rotate_lanes(values, cosine, sine):
    out = []
    front = lax.rem(lax.broadcasted_iota(jnp.int32, (1, 128), 1), 64) < 32
    for start in range(0, values.shape[1], 128):
        part = values[:, start : start + 128]
        partner = jnp.where(front, pltpu.roll(part, 96, 1), pltpu.roll(part, 32, 1))
        out.append(part * cosine + partner * sine)
    return out[0] if len(out) == 1 else jnp.concatenate(out, axis=1)


FWD_ROWS = 128
BACK_ROWS = 256
BK = 256
FWD_GROUPS = 8
BACK_GROUPS = 4
SCALE = HDIM**-0.5


def split_pair(values, dim=1):
    shape = (1, 128) if dim == 1 else (128, 1)
    first = lax.broadcasted_iota(jnp.int32, shape, dim) < 64
    zero = jnp.zeros_like(values)
    return jnp.where(first, values, zero), jnp.where(first, zero, values)


def turn(values):
    return values.astype(F32).T.astype(BF)


def attend_kernel(bounds_ref, query_ref, key_ref, turned_ref, segq_ref, segk_ref, mixed_ref, lse_ref):
    first = lax.broadcasted_iota(jnp.int32, (128, 1), 0) < 64
    one = jnp.ones((), BF)
    groups = range(0, query_ref.shape[1], 128)
    for block in range(query_ref.shape[0] // FWD_ROWS):
        rows = pl.ds(block * FWD_ROWS, FWD_ROWS)
        queries = [split_pair(turn(query_ref[rows, at : at + 128] * jnp.asarray(SCALE, BF)), 0) for at in groups]
        seg_q = segq_ref[0:1, rows]

        def body(index, carry):
            keys_at = pl.ds(pl.multiple_of(index * BK, BK), BK)
            live = segk_ref[keys_at, 0:1] == seg_q
            made = []
            for group, at in enumerate(groups):
                keys = key_ref[keys_at, at : at + 128]
                values = turned_ref[at : at + 128, keys_at]
                weights = (jnp.where(first, values, one), jnp.where(first, one, values))
                for head in range(2):
                    top, acc = carry[2 * group + head]
                    scores = jnp.where(live, dot(keys, queries[group][head]), -1e9)
                    new_top = jnp.maximum(top, jnp.max(scores, axis=0, keepdims=True))
                    probs = jnp.exp(scores - new_top).astype(BF)
                    acc = acc * jnp.exp(top - new_top) + dot(weights[head], probs)
                    made.append((new_top, acc))
            return tuple(made)

        start = tuple((jnp.full((1, FWD_ROWS), -2e9, F32), jnp.zeros((128, FWD_ROWS), F32)) for _ in range(2 * len(groups)))
        done = lax.fori_loop(bounds_ref[block, 0], bounds_ref[block, 1], body, start)
        for group, at in enumerate(groups):
            (top0, acc0), (top1, acc1) = done[2 * group : 2 * group + 2]
            total0, total1 = acc0[64:65], acc1[0:1]
            mixed = jnp.concatenate([acc0[0:64] / total0, acc1[64:128] / total1], axis=0)
            mixed_ref[rows, at : at + 128] = mixed.T.astype(BF)
            lse_ref[2 * group : 2 * group + 1, rows] = top0 + jnp.log(total0)
            lse_ref[2 * group + 1 : 2 * group + 2, rows] = top1 + jnp.log(total1)


def attend(bounds, queries, keys, turned, seg_q, seg_k):
    local, width = queries.shape
    long = keys.shape[0]
    lanes = FWD_GROUPS * 128
    return pl.pallas_call(
        attend_kernel,
        grid_spec=pltpu.PrefetchScalarGridSpec(
            num_scalar_prefetch=1,
            grid=(width // lanes,),
            in_specs=[
                pl.BlockSpec((local, lanes), lambda g, b: (0, g)),
                pl.BlockSpec((long, lanes), lambda g, b: (0, g)),
                pl.BlockSpec((lanes, long), lambda g, b: (g, 0)),
                pl.BlockSpec((8, local), lambda g, b: (0, 0)),
                pl.BlockSpec((long, 128), lambda g, b: (0, 0)),
            ],
            out_specs=[
                pl.BlockSpec((local, lanes), lambda g, b: (0, g)),
                pl.BlockSpec((2 * FWD_GROUPS, local), lambda g, b: (g, 0)),
            ],
        ),
        out_shape=[
            jax.ShapeDtypeStruct((local, width), BF),
            jax.ShapeDtypeStruct((width // HDIM, local), F32),
        ],
        compiler_params=pltpu.CompilerParams(vmem_limit_bytes=40 * 2**20),
        cost_estimate=pl.CostEstimate(flops=2 * 2**30, bytes_accessed=8 * 2**20, transcendentals=4 * 2**20),
    )(bounds, queries, keys, turned, seg_q, seg_k)


def attend_back_kernel(
    bounds_ref, query_ref, key_ref, turned_ref, value_ref, mixed_ref, grad_ref, lse_ref, segq_ref, segk_ref,
    cos_ref, sin_ref, dq_ref, dk_ref, dv_ref, dk_acc, dv_acc,
):
    local = query_ref.shape[0]
    groups = range(0, query_ref.shape[1], 128)
    dk_acc[...] = jnp.zeros_like(dk_acc)
    dv_acc[...] = jnp.zeros_like(dv_acc)
    head_row = lax.broadcasted_iota(jnp.int32, (8, 128), 0)
    head_lane = lax.broadcasted_iota(jnp.int32, (8, 128), 1) // 64
    chosen = jnp.where(head_row == head_lane, 1.0, 0.0)
    for block in range(local // BACK_ROWS):
        rows = pl.ds(block * BACK_ROWS, BACK_ROWS)
        queries, grads, turned_q, turned_g, deltas, logs = [], [], [], [], [], []
        for group, at in enumerate(groups):
            lanes = slice(at, at + 128)
            queries.append(split_pair(query_ref[rows, lanes] * jnp.asarray(SCALE, BF)))
            grads.append(split_pair(grad_ref[rows, lanes]))
            turned_q.append(split_pair(turn(query_ref[rows, lanes] * jnp.asarray(SCALE, BF)), 0))
            turned_g.append(split_pair(turn(grad_ref[rows, lanes]), 0))
            product = mixed_ref[rows, lanes].astype(F32) * grad_ref[rows, lanes].astype(F32)
            delta = dot(chosen, product, 1, 1, lax.Precision.HIGHEST)
            deltas.append((delta[0:1], delta[1:2]))
            logs.append((lse_ref[2 * group : 2 * group + 1, rows], lse_ref[2 * group + 1 : 2 * group + 2, rows]))
        seg_q = segq_ref[0:1, rows]

        def body(index, carry):
            keys_at = pl.ds(pl.multiple_of(index * BK, BK), BK)
            live = segk_ref[keys_at, 0:1] == seg_q
            made = []
            for group, at in enumerate(groups):
                lanes = slice(at, at + 128)
                keys = key_ref[keys_at, lanes]
                values = value_ref[keys_at, lanes]
                turned = turned_ref[lanes, keys_at]
                dk, dv = 0.0, 0.0
                for head in range(2):
                    scores = jnp.where(live, dot(keys, turned_q[group][head]), -1e9)
                    probs = jnp.exp(scores - logs[group][head])
                    score_low = (probs * (dot(values, turned_g[group][head]) - deltas[group][head])).astype(BF)
                    made.append(carry[2 * group + head] + dot(turned, score_low))
                    dk = dk + dot(score_low, queries[group][head])
                    dv = dv + dot(probs.astype(BF), grads[group][head])
                dk_acc[keys_at, lanes] += dk
                dv_acc[keys_at, lanes] += dv
            return tuple(made)

        start = (jnp.zeros((128, BACK_ROWS), F32),) * (2 * len(groups))
        done = lax.fori_loop(bounds_ref[block, 0], bounds_ref[block, 1], body, start)
        at_window = pl.ds(local + block * BACK_ROWS, BACK_ROWS)
        for group, at in enumerate(groups):
            grad = jnp.concatenate([done[2 * group][0:64], done[2 * group + 1][64:128]], axis=0).T * SCALE
            back = rotate_lanes(grad, cos_ref[at_window, :], -sin_ref[at_window, :])
            dq_ref[rows, at : at + 128] = back.astype(BF)
    dk_ref[...] = rotate_lanes(dk_acc[...], cos_ref[...], -sin_ref[...]).astype(BF)
    dv_ref[...] = dv_acc[...].astype(BF)


def attend_back(bounds, queries, keys, turned, values, mixed, grad, lse, seg_q, seg_k, cosine, sine):
    local, width = queries.shape
    long = keys.shape[0]
    lanes = BACK_GROUPS * 128
    short_spec = pl.BlockSpec((local, lanes), lambda g, b: (0, g))
    long_spec = pl.BlockSpec((long, lanes), lambda g, b: (0, g))
    return pl.pallas_call(
        attend_back_kernel,
        grid_spec=pltpu.PrefetchScalarGridSpec(
            num_scalar_prefetch=1,
            grid=(width // lanes,),
            in_specs=[
                short_spec,
                long_spec,
                pl.BlockSpec((lanes, long), lambda g, b: (g, 0)),
                long_spec,
                short_spec,
                short_spec,
                pl.BlockSpec((2 * BACK_GROUPS, local), lambda g, b: (g, 0)),
                pl.BlockSpec((8, local), lambda g, b: (0, 0)),
                pl.BlockSpec((long, 128), lambda g, b: (0, 0)),
                pl.BlockSpec((long, 128), lambda g, b: (0, 0)),
                pl.BlockSpec((long, 128), lambda g, b: (0, 0)),
            ],
            out_specs=[short_spec, long_spec, long_spec],
            scratch_shapes=[pltpu.VMEM((long, lanes), F32)] * 2,
        ),
        out_shape=[
            jax.ShapeDtypeStruct((local, width), BF),
            jax.ShapeDtypeStruct((long, width), BF),
            jax.ShapeDtypeStruct((long, width), BF),
        ],
        compiler_params=pltpu.CompilerParams(vmem_limit_bytes=48 * 2**20),
        cost_estimate=pl.CostEstimate(flops=5 * 2**30, bytes_accessed=16 * 2**20, transcendentals=4 * 2**20),
    )(bounds, queries, keys, turned, values, mixed, grad, lse, seg_q, seg_k, cosine, sine)


CB = 512
HIGH = lax.Precision.HIGHEST


def halves(values):
    high = values.astype(BF)
    return high, (values - high.astype(F32)).astype(BF)


def contrast_kernel(
    info_ref, emb_ref, segc_ref, segr_ref, counts_ref, positive_ref, temp_ref, grad_ref, loss_ref, tgrad_ref,
    unit, docs, docs_t, marks, marks_row, ratio, ratio_t, weights,
):
    own0, query_blocks, doc0 = info_ref[0], info_ref[1], info_ref[2]
    blocks = emb_ref.shape[0] // CB
    own_blocks = grad_ref.shape[0] // CB
    lane = lax.broadcasted_iota(jnp.int32, (1, 128), 1)
    widths = (EMB, EMB * 3 // 4, EMB // 2)
    loss_scale = temp_ref[0:1, 1:2]
    temp_inv = jnp.exp(-temp_ref[0:1, 0:1])
    segs = segc_ref[...]
    docs[...] = jnp.where((segs - NQ == lane) | ((segs == lane) & (lane >= NQ)), 1.0, 0.0).astype(BF)
    marks[...] = jnp.where((segs == lane) & (lane < NQ), 1.0, 0.0)
    down = lax.broadcasted_iota(jnp.int32, (128, 1), 0)
    across = segr_ref[0:1, :]
    docs_t[...] = jnp.where((across - NQ == down) | ((across == down) & (down >= NQ)), 1.0, 0.0).astype(BF)
    marks_row[...] = jnp.where(segr_ref[...] == lax.broadcasted_iota(jnp.int32, (NQ, 1), 0), 1.0, 0.0)
    for index, prefix in enumerate(widths):
        emb = jnp.where(lane < prefix, emb_ref[...].astype(F32), 0.0)
        unit[index] = (emb * lax.rsqrt(jnp.sum(emb * emb, axis=1, keepdims=True) + eps_unit)).astype(BF)

    def at(index):
        return pl.ds(pl.multiple_of(index * CB, CB), CB)

    def similar(index, rows, columns):
        return jnp.exp(10.0 * dot(unit[index, at(rows), :], unit[index, at(columns), :], 1, 1) - 10.0)

    def total_rows(row, seg_sums):
        def total_cols(column, totals):
            mask = docs[at(column), :]
            made = []
            for index in range(3):
                high, low = halves(similar(index, row, column))
                made.append(totals[index] + dot(high, mask) + dot(low, mask))
            return tuple(made)

        totals = lax.fori_loop(doc0, blocks, total_cols, (jnp.zeros((CB, 128), F32),) * 3)
        made = []
        for index in range(3):
            total = jnp.where(lane < NQ, totals[index], 1.0)
            ratio[index, at(row), :] = 1.0 / total
            smooth = jnp.log(total) / 10.0 + 1.0
            made.append(seg_sums[index] + dot(marks_row[:, at(row)], smooth, 1, 0, HIGH))
        return tuple(made)

    seg_sums = lax.fori_loop(0, query_blocks, total_rows, (jnp.zeros((NQ, 128), F32),) * 3)
    valid = lax.broadcasted_iota(jnp.int32, (NQ, 128), 1) < NQ
    inv_counts = 1.0 / counts_ref[0:NQ, :]
    positive = positive_ref[...]
    loss = jnp.zeros((1, 1), F32)
    tgrad = jnp.zeros((1, 1), F32)
    weights[...] = jnp.zeros_like(weights)
    for index in range(3):
        logits = jnp.where(valid, seg_sums[index] * inv_counts * temp_inv, 0.0)
        top = jnp.max(jnp.where(valid, logits, -1e30), axis=1, keepdims=True)
        powers = jnp.where(valid, jnp.exp(logits - top), 0.0)
        power_sum = jnp.sum(powers, axis=1, keepdims=True)
        term = jnp.log(power_sum) + top - jnp.sum(logits * positive, axis=1, keepdims=True)
        loss = loss + jnp.sum(term, axis=0, keepdims=True) * loss_scale
        dlogits = (powers / power_sum - positive) * loss_scale
        tgrad = tgrad - jnp.sum(jnp.sum(dlogits * logits, axis=1, keepdims=True), axis=0, keepdims=True)
        weights[index, 0:NQ, :] = dlogits * temp_inv * inv_counts

    def weigh(row, unused):
        for index in range(3):
            weight = dot(marks[at(row), :], weights[index], 1, 0, HIGH) * ratio[index, at(row), :]
            weight = jnp.where(lane < NQ, weight, 0.0)
            high = weight.astype(BF).astype(F32)
            both = high + pltpu.roll(weight - high, NQ, 1)
            ratio[index, at(row), :] = both
            ratio_t[index, :, at(row)] = both.T.astype(BF)
        return unused

    lax.fori_loop(0, query_blocks, weigh, 0)

    for own in range(own_blocks):
        mine = own0 + own

        def as_query(column, grads):
            mask = docs_t[:, at(column)]
            made = []
            for index in range(3):
                spread = dot(ratio[index, at(mine), :].astype(BF), mask)
                sim_grad = (similar(index, mine, column) * spread).astype(BF)
                made.append(grads[index] + dot(sim_grad, unit[index, at(column), :]))
            return tuple(made)

        def as_doc(row, grads):
            mask = docs[at(mine), :]
            made = []
            for index in range(3):
                spread = dot(mask, ratio_t[index, :, at(row)])
                sim_grad = (similar(index, mine, row) * spread).astype(BF)
                made.append(grads[index] + dot(sim_grad, unit[index, at(row), :]))
            return tuple(made)

        grads = (jnp.zeros((CB, 128), F32),) * 3
        grads = lax.fori_loop(doc0, jnp.where(mine < query_blocks, blocks, doc0), as_query, grads)
        grads = lax.fori_loop(0, jnp.where(mine >= doc0, query_blocks, 0), as_doc, grads)
        total = jnp.zeros((CB, 128), F32)
        for index, prefix in enumerate(widths):
            part = jnp.where(lane < prefix, emb_ref[at(mine), :].astype(F32), 0.0)
            scale = lax.rsqrt(jnp.sum(part * part, axis=1, keepdims=True) + eps_unit)
            full = part * scale
            back = scale * (grads[index] - full * jnp.sum(full * grads[index], axis=1, keepdims=True))
            total = total + jnp.where(lane < prefix, back, 0.0)
        grad_ref[pl.ds(own * CB, CB), :] = total.astype(BF)
    loss_ref[...] = jnp.broadcast_to(loss, loss_ref.shape)
    tgrad_ref[...] = jnp.broadcast_to(tgrad, tgrad_ref.shape)


def contrast(info, emb_all, seg_col, seg_row, counts, positive, temp_row, local):
    rows = emb_all.shape[0]
    return pl.pallas_call(
        contrast_kernel,
        in_specs=[pl.BlockSpec(memory_space=pltpu.SMEM)] + vmem_specs(6),
        out_specs=vmem_specs(3),
        out_shape=[
            jax.ShapeDtypeStruct((local, 128), BF),
            jax.ShapeDtypeStruct((8, 128), F32),
            jax.ShapeDtypeStruct((8, 128), F32),
        ],
        scratch_shapes=[
            pltpu.VMEM((3, rows, 128), BF),
            pltpu.VMEM((rows, 128), BF),
            pltpu.VMEM((128, rows), BF),
            pltpu.VMEM((rows, 128), F32),
            pltpu.VMEM((NQ, rows), F32),
            pltpu.VMEM((3, rows, 128), F32),
            pltpu.VMEM((3, 128, rows), BF),
            pltpu.VMEM((3, 128, 128), F32),
        ],
        compiler_params=pltpu.CompilerParams(vmem_limit_bytes=40 * 2**20),
        cost_estimate=pl.CostEstimate(flops=2**30, bytes_accessed=2**22, transcendentals=2**22),
    )(info, emb_all, seg_col, seg_row, counts, positive, temp_row)


CW = 512
SLOTS_G, SLOTS_S, SLOTS_R, SLOTS_T, SLOTS_K = 3, 3, 4, 6, 14
SMALL_ROWS = 112
LAGS = (4, 7, 2)


def neighbours():
    dp = lax.axis_index("dp")
    low = lax.rem(dp, 8)
    core = lax.rem(low, 2)
    x = lax.rem(low // 2, 2)
    y = low // 4
    return dp, low, core, x, y, dp + 1 - 2 * core, dp + 2 - 4 * x, dp + 4 - 8 * y


def entry_barrier(z, dp, plane, z_count):
    barrier = pltpu.get_barrier_semaphore()
    for other in plane:
        pl.semaphore_signal(barrier, inc=1, device_id={"dp": other, "tensor": z}, device_id_type=MESH)
    for step in range(1, z_count):
        peer = lax.rem(z + step, z_count)
        pl.semaphore_signal(barrier, inc=1, device_id={"dp": dp, "tensor": peer}, device_id_type=MESH)
    pl.semaphore_wait(barrier, len(plane) + z_count - 1)


def remote(src, dst, send_sem, recv_sem, dp, z):
    return pltpu.make_async_remote_copy(
        src_ref=src,
        dst_ref=dst,
        send_sem=send_sem,
        recv_sem=recv_sem,
        device_id={"dp": dp, "tensor": z},
        device_id_type=MESH,
    )


def scatter_kernel(
    window, attn_grad, normed, ffn_grad, dq, dk, dv, mixed, pre_grad, hidden, dxw, small_ref,
    out_qkv, out_attn, out_in, out_out, small_out, from_left, from_right,
    xw, xa, xn, xf, gs, gkv, sbuf, rbuf, ta, tb, xra, xrb, s2a, s2b, yra, yrb, keep, zs, zrl, zrr,
    sacc, srec, zsm,
    x_sem, g_sem, s_sem, r_sem, t_sem, xr_sem, s2_sem, yr_sem, zs_sem, zr_sem, sm_sem, smz_sem, h_sem, credit,
):
    dp, low, core, x, y, to_core, to_x, to_y = neighbours()
    z = lax.axis_index("tensor")
    nz = 4
    chunks = [("out", i) for i in range(8)] + [("in", i) for i in range(8)] + [("qa", i) for i in range(8)]
    count = len(chunks)
    local = attn_grad.shape[0]
    has_l = z > 0
    has_r = z < nz - 1

    x_loads = [
        pltpu.make_async_copy(src, dst, x_sem.at[index])
        for index, (src, dst) in enumerate(((ffn_grad, xf), (normed, xn), (window, xw), (attn_grad, xa)))
    ]
    for load in x_loads:
        load.start()

    def g_loads(index):
        kind, part = chunks[index]
        slot = index % SLOTS_G
        if kind != "qa":
            source = hidden if kind == "out" else pre_grad
            return [pltpu.make_async_copy(source.at[:, pl.ds(part * CW, CW)], gs.at[slot], g_sem.at[slot, 0])]
        columns = pl.ds((part // 2) * 256, 256)
        one, many = (dq, dk) if part % 2 == 0 else (mixed, dv)
        return [
            pltpu.make_async_copy(one.at[:, columns], gs.at[slot, :, pl.ds(0, 256)], g_sem.at[slot, 0]),
            pltpu.make_async_copy(many.at[:, columns], gkv.at[slot], g_sem.at[slot, 1]),
        ]

    for index in range(2):
        for load in g_loads(index):
            load.start()

    entry_barrier(z, dp, (to_core, to_x, to_y), nz)

    halo_l = remote(dxw.at[pl.ds(0, local)], from_right, h_sem.at[0], h_sem.at[1], dp, z - 1)
    halo_r = remote(dxw.at[pl.ds(2 * local, local)], from_left, h_sem.at[2], h_sem.at[3], dp, z + 1)

    peers = (to_core, to_x, to_y)

    def small_moves(stage):
        return [
            remote(sacc.at[stage], srec.at[stage], sm_sem.at[stage, 0], sm_sem.at[stage, 1], peers[stage], z),
        ]

    def small_z_moves(step):
        peer = lax.rem(z + step, nz)
        return [
            remote(sacc.at[3], zsm.at[step - 1], smz_sem.at[step - 1, 0], smz_sem.at[step - 1, 1], dp, peer),
        ]

    def small_stage(stage):
        if stage == 0:
            sacc[0] = small_ref[...]
        if 1 <= stage <= 3:
            for move in small_moves(stage - 1):
                move.wait_recv()
            sacc[stage] = sacc[stage - 1] + srec[stage - 1]
        if stage <= 2:
            for move in small_moves(stage):
                move.start()
        if stage == 3:
            for step in range(1, nz):
                for move in small_z_moves(step):
                    move.start()
        if stage == 4:
            for step in range(1, nz):
                for move in small_z_moves(step):
                    move.wait_recv()
            total = None
            for owner in range(nz):
                value = jnp.where(z == owner, sacc[3], 0.0)
                for step in range(1, nz):
                    value = jnp.where(lax.rem(z - step + nz, nz) == owner, zsm[step - 1], value)
                total = value if total is None else total + value
            small_out[...] = total

    def block_columns(j, core_bit):
        xj = lax.rem(j, 2)
        yj = j // 2
        block = core_bit + 2 * (x + xj - 2 * x * xj) + 4 * (y + yj - 2 * y * yj)
        return pl.ds(pl.multiple_of(block * 128, 128), 128)

    def product(index, j, core_bit):
        kind, part = chunks[index]
        slot = index % SLOTS_G
        at = block_columns(j, core_bit)
        if kind == "out":
            return dot(xf[:, at], gs[slot], 0, 0)
        if kind == "in":
            return dot(xn[:, at], gs[slot], 0, 0)
        one = xw[pl.ds(local, local), at] if part % 2 == 0 else xa[:, at]
        return jnp.concatenate(
            [dot(one, gs[slot, :, 0:256], 0, 0), dot(xw[:, at], gkv[slot], 0, 0)], axis=1
        )

    def core_move(index):
        return remote(
            sbuf.at[index % SLOTS_S], rbuf.at[index % SLOTS_R], s_sem.at[index % SLOTS_S], r_sem.at[index % SLOTS_R],
            to_core, z,
        )

    half = CW // 2

    def ta_move(index):
        slot = index % SLOTS_T
        return remote(ta.at[slot, pl.ds(2, 2)], xra.at[index], t_sem.at[slot, 0], xr_sem.at[index, 0], to_x, z)

    def tb_move(index):
        slot = index % SLOTS_T
        return remote(tb.at[slot, pl.ds(2, 2)], xrb.at[index], t_sem.at[slot, 1], xr_sem.at[index, 1], to_y, z)

    def s2a_move(index):
        return remote(s2a.at[index], yra.at[index], s2_sem.at[index, 0], yr_sem.at[index, 0], to_y, z)

    def s2b_move(index):
        return remote(s2b.at[index], yrb.at[index], s2_sem.at[index, 1], yr_sem.at[index, 1], to_x, z)

    def right_move(index):
        return remote(zs.at[index], zrl.at[index], zs_sem.at[index], zr_sem.at[index, 0], dp, z + 1)

    def left_move(index):
        return remote(zs.at[index], zrr.at[index], zs_sem.at[index], zr_sem.at[index, 1], dp, z - 1)

    def stage_one(index):
        kind, part = chunks[index]
        if index == 0:
            x_loads[0].wait()
        if kind == "in" and part == 0:
            x_loads[1].wait()
        if kind == "qa" and part == 0:
            x_loads[2].wait()
            x_loads[3].wait()
        for load in g_loads(index):
            load.wait()
        if index >= SLOTS_S:
            core_move(index - SLOTS_S).wait_send()

        def body(j, unused):
            sbuf[index % SLOTS_S, j] = product(index, j, 1 - core).astype(BF)
            return unused

        lax.fori_loop(0, 4, body, 0)
        if index >= SLOTS_R:
            pl.semaphore_wait(credit, 1)
        core_move(index).start()

    def stage_two(index):
        core_move(index).wait_recv()
        slot = index % SLOTS_T
        if index >= SLOTS_T:
            ta_move(index - SLOTS_T).wait_send()
            tb_move(index - SLOTS_T).wait_send()

        def body(j, unused):
            total = product(index, j, core) + rbuf[index % SLOTS_R, j].astype(F32)
            ta[slot, j // 2 + 2 * lax.rem(j, 2)] = total[:, :half].astype(BF)
            tb[slot, j] = total[:, half:].astype(BF)
            return unused

        lax.fori_loop(0, 4, body, 0)
        if index + SLOTS_R < count:
            pl.semaphore_signal(credit, inc=1, device_id={"dp": to_core, "tensor": z}, device_id_type=MESH)
        ta_move(index).start()
        tb_move(index).start()

    def stage_three(index):
        slot = index % SLOTS_T
        kslot = index % SLOTS_K
        ta_move(index).wait_recv()
        s2a[index] = (ta[slot, 1].astype(F32) + xra[index, 1].astype(F32)).astype(BF)
        s2a_move(index).start()
        keep[kslot, :, :half] = ta[slot, 0].astype(F32) + xra[index, 0].astype(F32)
        tb_move(index).wait_recv()
        s2b[index] = (tb[slot, 1].astype(F32) + xrb[index, 1].astype(F32)).astype(BF)
        s2b_move(index).start()
        keep[kslot, :, half:] = tb[slot, 0].astype(F32) + xrb[index, 0].astype(F32)

    def stage_four(index):
        kslot = index % SLOTS_K
        goal = chunks[index][1] // 2
        s2a_move(index).wait_recv()
        keep[kslot, :, :half] += yra[index].astype(F32)
        s2b_move(index).wait_recv()
        keep[kslot, :, half:] += yrb[index].astype(F32)
        if goal > 0:

            @pl.when(z == 0)
            def _():
                zs[index] = keep[kslot].astype(BF)
                right_move(index).start()

        if goal < nz - 1:

            @pl.when(z == nz - 1)
            def _():
                zs[index] = keep[kslot].astype(BF)
                left_move(index).start()

    def stage_five(index, hop):
        kslot = index % SLOTS_K
        kind, part = chunks[index]
        goal = part // 2
        if hop <= goal:

            @pl.when(z == hop)
            def _():
                right_move(index).wait_recv()
                keep[kslot] += zrl[index].astype(F32)
                if hop < goal:
                    zs[index] = keep[kslot].astype(BF)
                    right_move(index).start()

        if hop <= nz - 1 - goal:

            @pl.when(z == nz - 1 - hop)
            def _():
                left_move(index).wait_recv()
                keep[kslot] += zrr[index].astype(F32)
                if nz - 1 - hop > goal:
                    zs[index] = keep[kslot].astype(BF)
                    left_move(index).start()

        if hop == nz - 1:

            @pl.when(z == goal)
            def _():
                if kind == "qa":
                    if part % 2 == 0:
                        out_qkv[:, 0:512] = keep[kslot]
                    else:
                        out_attn[...] = keep[kslot, :, 0:256]
                        out_qkv[:, 512:768] = keep[kslot, :, 256:512]
                else:
                    target = out_in if kind == "in" else out_out
                    target[:, pl.ds((part % 2) * CW, CW)] = keep[kslot]

    lag_three, lag_four, spacing = LAGS
    for step in range(count + lag_four + spacing * (nz - 1) + 1):
        if step < count:
            stage_one(step)
        if step == 0:
            small_stage(0)
            pl.when(has_l)(lambda: halo_l.start())
            pl.when(has_r)(lambda: halo_r.start())
        if 0 <= step - 1 < count:
            stage_two(step - 1)
        if step + 2 < count:
            for load in g_loads(step + 2):
                load.start()
        if step in (2, 4, 6, 8):
            small_stage(step // 2)
        if 0 <= step - lag_three < count:
            stage_three(step - lag_three)
        if 0 <= step - lag_four < count:
            stage_four(step - lag_four)
        for hop in range(1, nz):
            index = step - lag_four - spacing * hop
            if 0 <= index < count:
                stage_five(index, hop)

    for index in range(count):
        goal = chunks[index][1] // 2
        if index >= count - SLOTS_S:
            core_move(index).wait_send()
        if index >= count - SLOTS_T:
            ta_move(index).wait_send()
            tb_move(index).wait_send()
        s2a_move(index).wait_send()
        s2b_move(index).wait_send()
        pl.when(z < goal)(lambda index=index: right_move(index).wait_send())
        pl.when(z > goal)(lambda index=index: left_move(index).wait_send())
    for stage in range(3):
        for move in small_moves(stage):
            move.wait_send()
    for step in range(1, nz):
        for move in small_z_moves(step):
            move.wait_send()

    @pl.when(has_l)
    def _():
        halo_l.wait_send()
        halo_r.wait_recv()

    @pl.when(has_r)
    def _():
        halo_r.wait_send()
        halo_l.wait_recv()


def scatter(window, attn_grad, normed, ffn_grad, dq, dk, dv, mixed, pre_grad, hidden, dxw, small):
    local, width = attn_grad.shape
    long = window.shape[0]
    dma = pltpu.SemaphoreType.DMA
    n = 24
    half = CW // 2
    shape = jax.ShapeDtypeStruct
    return pl.pallas_call(
        scatter_kernel,
        in_specs=hbm_specs(11) + vmem_specs(1),
        out_specs=vmem_specs(5) + hbm_specs(2),
        out_shape=[
            shape((128, 768), F32),
            shape((128, 256), F32),
            shape((128, 1024), F32),
            shape((128, 1024), F32),
            shape(small.shape, F32),
            shape((local, width), BF),
            shape((local, width), BF),
        ],
        scratch_shapes=[
            pltpu.VMEM((long, width), BF),
            pltpu.VMEM((local, width), BF),
            pltpu.VMEM((local, width), BF),
            pltpu.VMEM((local, width), BF),
            pltpu.VMEM((SLOTS_G, local, CW), BF),
            pltpu.VMEM((SLOTS_G, long, 256), BF),
            pltpu.VMEM((SLOTS_S, 4, 128, CW), BF),
            pltpu.VMEM((SLOTS_R, 4, 128, CW), BF),
            pltpu.VMEM((SLOTS_T, 4, 128, half), BF),
            pltpu.VMEM((SLOTS_T, 4, 128, half), BF),
            pltpu.VMEM((n, 2, 128, half), BF),
            pltpu.VMEM((n, 2, 128, half), BF),
            pltpu.VMEM((n, 128, half), BF),
            pltpu.VMEM((n, 128, half), BF),
            pltpu.VMEM((n, 128, half), BF),
            pltpu.VMEM((n, 128, half), BF),
            pltpu.VMEM((SLOTS_K, 128, CW), F32),
            pltpu.VMEM((n, 128, CW), BF),
            pltpu.VMEM((n, 128, CW), BF),
            pltpu.VMEM((n, 128, CW), BF),
            pltpu.VMEM((4,) + small.shape, F32),
            pltpu.VMEM((3,) + small.shape, F32),
            pltpu.VMEM((3,) + small.shape, F32),
            dma((4,)),
            dma((SLOTS_G, 2)),
            dma((SLOTS_S,)),
            dma((SLOTS_R,)),
            dma((SLOTS_T, 2)),
            dma((n, 2)),
            dma((n, 2)),
            dma((n, 2)),
            dma((n,)),
            dma((n, 2)),
            dma((3, 2)),
            dma((3, 2)),
            dma((4,)),
            pltpu.SemaphoreType.REGULAR,
        ],
        compiler_params=pltpu.CompilerParams(
            collective_id=2, has_side_effects=True, vmem_limit_bytes=VMEM_BIG
        ),
    )(window, attn_grad, normed, ffn_grad, dq, dk, dv, mixed, pre_grad, hidden, dxw, small)


def shard_rows(kind, ref):
    return ref.shape[1] if kind == "qkv" else (512 if kind in ("out0", "out1") else ref.shape[0])


def source_rows(kind, ref, start, rows):
    if kind == "qkv":
        return ref.at[:, pl.ds(start, rows), :]
    if kind == "out1":
        start = pl.multiple_of(start + 512, 16)
    return ref.at[pl.ds(start, rows), :]


def gathered_rows(kind, ref, shard, start, rows):
    if kind == "qkv":
        return ref.at[:, pl.ds(start, rows), pl.ds(pl.multiple_of(shard * 256, 256), 256)]
    if kind == "in":
        return ref.at[pl.ds(start, rows), pl.ds(pl.multiple_of(shard * 1024, 1024), 1024)]
    per = ref.shape[0] // 4
    if kind == "out1":
        start = start + 512
    return ref.at[pl.ds(pl.multiple_of(shard * per + start, 16), rows), :]


class Gather:
    def __init__(self, kinds, srcs, outs, z_send, z_recv, p_send, p_recv, lag):
        self.kinds, self.srcs, self.outs = kinds, srcs, outs
        self.z_send, self.z_recv, self.p_send, self.p_recv = z_send, z_recv, p_send, p_recv
        self.dp, low, core, x, y, self.to_core, self.to_x, self.to_y = neighbours()
        self.z = lax.axis_index("tensor")
        self.nz = 4
        self.has_l, self.has_r = self.z > 0, self.z < self.nz - 1
        low_x, low_y = low + 2 - 4 * x, low + 4 - 8 * y
        low_xy = low_x + 4 - 8 * y
        self.low = low
        self.places = {
            0: (low, None), 1: (low, None), 4: (low, None), 2: (low_x, 0), 3: (low_y, 1),
            5: (low_x, None), 6: (low_y, None), 7: (low_xy, 0), 8: (low_xy, 1),
        }
        self.events = [(m, distance, side) for m in range(len(kinds)) for distance in (1, 2, 3) for side in (0, 1)]
        self.lag = lag
        self.steps = len(self.events) + 2 * lag

    def barrier(self):
        entry_barrier(self.z, self.dp, (self.to_core, self.to_x, self.to_y), self.nz)

    def piece(self, m, shard, index, half=None):
        rows = shard_rows(self.kinds[m], self.srcs[m]) // 8
        start = index * rows
        if half is not None:
            rows = rows // 2
            start = start + half * rows
        return gathered_rows(self.kinds[m], self.outs[m], shard, pl.multiple_of(start, 16), rows)

    def shard_of(self, side, distance):
        return self.z - distance if side == 0 else self.z + distance

    def onward(self, side):
        return self.z + 1 if side == 0 else self.z - 1

    def can_send(self, side):
        return self.has_r if side == 0 else self.has_l

    def arrives(self, side, distance):
        return self.z >= distance if side == 0 else self.z + distance < self.nz

    def own_move(self, m, side):
        rows = shard_rows(self.kinds[m], self.srcs[m]) // 8
        src = source_rows(self.kinds[m], self.srcs[m], pl.multiple_of(self.low * rows, 16), rows)
        sems = self.z_send.at[m, side, 0], self.z_recv.at[m, side, 0]
        return remote(src, self.piece(m, self.z, self.low), *sems, self.dp, self.onward(side))

    def relay_move(self, m, side, distance):
        at = self.piece(m, self.shard_of(side, distance), self.low)
        sems = self.z_send.at[m, side, distance], self.z_recv.at[m, side, distance]
        return remote(at, at, *sems, self.dp, self.onward(side))

    def plane_move(self, m, side, distance, kind):
        ref = self.piece(m, self.shard_of(side, distance), *self.places[kind])
        to = {0: self.to_x, 1: self.to_y, 2: self.to_y, 3: self.to_x}.get(kind, self.to_core)
        slot = side * 3 + distance - 1
        return remote(ref, ref, self.p_send.at[m, slot, kind], self.p_recv.at[m, slot, kind], to, self.z)

    def own_start(self, m):
        for side in (0, 1):
            pl.when(self.can_send(side))(lambda side=side: self.own_move(m, side).start())

    def stage_z(self, m, distance, side):
        if side == 0 and distance == 2 and m + 1 < len(self.kinds):
            self.own_start(m + 1)

        @pl.when(self.arrives(side, distance))
        def _():
            if distance == 1:
                self.own_move(m, side).wait_recv()
            else:
                self.relay_move(m, side, distance - 1).wait_recv()
            if distance < 3:
                pl.when(self.can_send(side))(lambda: self.relay_move(m, side, distance).start())
            for kind in (0, 1, 4):
                self.plane_move(m, side, distance, kind).start()

    def stage_plane(self, m, distance, side, waits, shift):
        @pl.when(self.arrives(side, distance))
        def _():
            for kind in waits:
                self.plane_move(m, side, distance, kind).wait_recv()
                for more in shift:
                    self.plane_move(m, side, distance, kind + more).start()

    def step(self, step):
        count = len(self.events)
        if step < count:
            self.stage_z(*self.events[step])
        if 0 <= step - self.lag < count:
            self.stage_plane(*self.events[step - self.lag], (0, 1), (2, 5))
        if 0 <= step - 2 * self.lag < count:
            self.stage_plane(*self.events[step - 2 * self.lag], (2, 3), (5,))

    def arrived(self, m, distance, side):
        self.stage_plane(m, distance, side, (4, 5, 6, 7, 8), ())

    def arrived_all(self, m):
        for distance in (1, 2, 3):
            for side in (0, 1):
                self.arrived(m, distance, side)

    def drain(self):
        for m, distance, side in self.events:

            @pl.when(self.arrives(side, distance))
            def _():
                for kind in range(9):
                    self.plane_move(m, side, distance, kind).wait_send()
                if distance < 3:
                    pl.when(self.can_send(side))(lambda: self.relay_move(m, side, distance).wait_send())

        for m in range(len(self.kinds)):
            for side in (0, 1):
                pl.when(self.can_send(side))(lambda side=side: self.own_move(m, side).wait_send())


def gather_sems(n):
    dma = pltpu.SemaphoreType.DMA
    return [dma((n, 2, 3)), dma((n, 2, 3)), dma((n, 6, 9)), dma((n, 6, 9))]


def first_kernel(
    qkv_src, attn_src, in_src, tokens, bias, cos_ref, sin_ref,
    qkv_out, attn_out, in_out, window_out, bias_all, query_out, key_out, key_t_out, value_out, value_t_out,
    weight, xw, query, key, key_t, value, value_t, stage_a, stage_i,
    z_send, z_recv, p_send, p_recv, l_sem, h_sem, b_sem, o_sem,
):
    plan = Gather(
        ("qkv", "attn", "in"), (qkv_src, attn_src, in_src), (weight, attn_out, in_out), z_send, z_recv, p_send, p_recv, 4
    )
    z, dp, nz = plan.z, plan.dp, plan.nz
    local = tokens.shape[0]
    own_qkv = pltpu.make_async_copy(qkv_src, gathered_rows("qkv", weight, z, 0, qkv_src.shape[1]), l_sem.at[0])
    a_in = pltpu.make_async_copy(attn_src, stage_a, l_sem.at[1])
    i_in = pltpu.make_async_copy(in_src, stage_i, l_sem.at[2])
    a_out = pltpu.make_async_copy(stage_a, gathered_rows("attn", attn_out, z, 0, attn_src.shape[0]), l_sem.at[3])
    i_out = pltpu.make_async_copy(stage_i, gathered_rows("in", in_out, z, 0, in_src.shape[0]), l_sem.at[4])
    own_tokens = pltpu.make_async_copy(tokens, xw.at[pl.ds(local, local)], h_sem.at[4])
    fill_l = pltpu.make_async_copy(tokens, xw.at[pl.ds(0, local)], h_sem.at[5])
    fill_r = pltpu.make_async_copy(tokens, xw.at[pl.ds(2 * local, local)], h_sem.at[6])
    for copy in (own_qkv, a_in, i_in, own_tokens):
        copy.start()
    pl.when(jnp.logical_not(plan.has_l))(lambda: fill_l.start())
    pl.when(jnp.logical_not(plan.has_r))(lambda: fill_r.start())
    bias_all[pl.ds(z, 1)] = bias[...].reshape(1, *bias.shape)
    plan.barrier()
    to_left = remote(tokens, xw.at[pl.ds(2 * local, local)], h_sem.at[0], h_sem.at[1], dp, z - 1)
    to_right = remote(tokens, xw.at[pl.ds(0, local)], h_sem.at[2], h_sem.at[3], dp, z + 1)

    def bias_move(step):
        return remote(bias, bias_all.at[z], b_sem.at[0, step - 1], b_sem.at[1, step - 1], dp, lax.rem(z + step, nz))

    plan.own_start(0)
    for step in range(1, nz):
        bias_move(step).start()
    a_in.wait()
    a_out.start()
    i_in.wait()
    i_out.start()

    weight_out = pltpu.make_async_copy(weight, qkv_out, o_sem.at[0])
    window_copy = pltpu.make_async_copy(xw, window_out, o_sem.at[1])

    def outputs(shard):
        columns = pl.ds(shard * 256, 256)
        return [
            pltpu.make_async_copy(query.at[:, columns], query_out.at[:, columns], o_sem.at[2 + 5 * shard]),
            pltpu.make_async_copy(key.at[:, columns], key_out.at[:, columns], o_sem.at[3 + 5 * shard]),
            pltpu.make_async_copy(key_t.at[columns, :], key_t_out.at[columns, :], o_sem.at[4 + 5 * shard]),
            pltpu.make_async_copy(value.at[:, columns], value_out.at[:, columns], o_sem.at[5 + 5 * shard]),
            pltpu.make_async_copy(value_t.at[columns, :], value_t_out.at[columns, :], o_sem.at[6 + 5 * shard]),
        ]

    def ready():
        plan.arrived_all(0)
        own_qkv.wait()
        own_tokens.wait()
        weight_out.start()
        for step in range(1, nz):
            bias_move(step).wait_recv()

    def halo_ready():
        pl.when(plan.has_l)(lambda: to_right.wait_recv())
        pl.when(plan.has_r)(lambda: to_left.wait_recv())
        pl.when(jnp.logical_not(plan.has_l))(lambda: fill_l.wait())
        pl.when(jnp.logical_not(plan.has_r))(lambda: fill_r.wait())
        window_copy.start()

    def compute(shard, part):
        columns = slice(shard * 256, shard * 256 + 256)
        rows = slice(part * local, part * local + local)
        window = xw[rows, :]
        cosine, sine = cos_ref[rows, :], sin_ref[rows, :]

        def made(kind):
            add = [bias_all[shard, 2 * kind + i : 2 * kind + i + 1, :].astype(F32) for i in range(2)]
            return dot(window, weight[kind, :, columns]) + jnp.concatenate(add, axis=1)

        if part == 1:
            query[:, columns] = rotate_lanes(made(0), cosine, sine).astype(BF)
        keys = rotate_lanes(made(1), cosine, sine)
        key[rows, columns] = keys.astype(BF)
        key_t[columns, rows] = keys.T.astype(BF)
        values = made(2)
        value[rows, columns] = values.astype(BF)
        value_t[columns, rows] = values.T.astype(BF)

    pieces = [ready]
    pieces += [partial(compute, shard, 1) for shard in range(4)]
    pieces += [halo_ready]
    for shard in range(4):
        pieces += [partial(compute, shard, 0), partial(compute, shard, 2)]
        pieces += [lambda shard=shard: [copy.start() for copy in outputs(shard)]]
    first_piece = 6 + 2 * plan.lag
    for step in range(max(plan.steps, first_piece + len(pieces))):
        if step < plan.steps:
            plan.step(step)
        if step == 5:
            pl.when(plan.has_l)(lambda: to_left.start())
            pl.when(plan.has_r)(lambda: to_right.start())
        if step >= first_piece and pieces:
            pieces.pop(0)()
    for m in (1, 2):
        plan.arrived_all(m)
    plan.drain()
    a_out.wait()
    i_out.wait()
    for step in range(1, nz):
        bias_move(step).wait_send()
    pl.when(plan.has_l)(lambda: to_left.wait_send())
    pl.when(plan.has_r)(lambda: to_right.wait_send())
    weight_out.wait()
    window_copy.wait()
    for shard in range(4):
        for copy in outputs(shard):
            copy.wait()


def first(qkv_weight, attn_weight, in_weight, tokens, bias, cosine, sine):
    local, width = tokens.shape
    long = 3 * local
    shape = jax.ShapeDtypeStruct
    dma = pltpu.SemaphoreType.DMA
    return pl.pallas_call(
        first_kernel,
        in_specs=hbm_specs(4) + vmem_specs(3),
        out_specs=hbm_specs(4) + vmem_specs(1) + hbm_specs(5),
        out_shape=[
            shape((3, width, width), BF),
            shape((width, width), BF),
            shape((width, 4 * width), BF),
            shape((long, width), BF),
            shape((4,) + bias.shape, BF),
            shape((local, width), BF),
            shape((long, width), BF),
            shape((width, long), BF),
            shape((long, width), BF),
            shape((width, long), BF),
        ],
        scratch_shapes=[
            pltpu.VMEM((3, width, width), BF),
            pltpu.VMEM((long, width), BF),
            pltpu.VMEM((local, width), BF),
            pltpu.VMEM((long, width), BF),
            pltpu.VMEM((width, long), BF),
            pltpu.VMEM((long, width), BF),
            pltpu.VMEM((width, long), BF),
            pltpu.VMEM(attn_weight.shape, BF),
            pltpu.VMEM(in_weight.shape, BF),
        ]
        + gather_sems(3)
        + [dma((5,)), dma((7,)), dma((2, 3)), dma((22,))],
        compiler_params=pltpu.CompilerParams(collective_id=0, has_side_effects=True, vmem_limit_bytes=VMEM_BIG),
    )(qkv_weight, attn_weight, in_weight, tokens, bias, cosine, sine)


def normalise(values):
    mean_value = jnp.mean(values, axis=1, keepdims=True)
    centered = values - mean_value
    variance = jnp.mean(centered * centered, axis=1, keepdims=True)
    scale = lax.rsqrt(variance + eps_norm)
    return centered * scale, scale


FF_STEP = 512
ROOT_HALF = math.sqrt(0.5)
ROOT_TURN = 1.0 / math.sqrt(2.0 * math.pi)


def second_kernel(
    out_src, mixed, tokens, attn_all, in_all, in_bias, vectors, proj_weight,
    out_all, hidden_out, slope_out, normed_out, unit_one_out, scale_one, output_out, unit_two_out, scale_two, emb_all,
    weight, mixed_v, tokens_v, attn_v, in_v, hidden, slope, normed, normed_low, total, unit, output_low, unit_two, emb,
    z_send, z_recv, p_send, p_recv, l_sem, i_sem, o_sem, e_sem,
):
    plan = Gather(("out0", "out1"), (out_src, out_src), (weight, weight), z_send, z_recv, p_send, p_recv, 4)
    z, dp, nz = plan.z, plan.dp, plan.nz
    local = tokens.shape[0]
    per = out_src.shape[0]
    own = pltpu.make_async_copy(out_src, weight.at[pl.ds(pl.multiple_of(z * per, 16), per)], l_sem.at[0])
    loads = [
        pltpu.make_async_copy(src, dst, l_sem.at[1 + index])
        for index, (src, dst) in enumerate(((mixed, mixed_v), (attn_all, attn_v), (tokens, tokens_v)))
    ]
    ff = in_all.shape[1]
    ff_steps = ff // FF_STEP

    def in_load(index):
        return pltpu.make_async_copy(
            in_all.at[:, pl.ds(index * FF_STEP, FF_STEP)], in_v.at[index % 2], i_sem.at[index % 2]
        )

    for copy in (*loads, own, in_load(0), in_load(1)):
        copy.start()
    plan.barrier()
    plan.own_start(0)

    saves = [
        pltpu.make_async_copy(src, dst, o_sem.at[index])
        for index, (src, dst) in enumerate(
            ((hidden, hidden_out), (slope, slope_out), (normed_low, normed_out), (unit, unit_one_out),
             (output_low, output_out), (unit_two, unit_two_out), (weight, out_all))
        )
    ]

    def attn_half(half):
        if half == 0:
            for load in loads:
                load.wait()
        rows = slice(half * (local // 2), (half + 1) * (local // 2))
        attn_out = dot(mixed_v[rows, :], attn_v[...]) + vectors[0:1, :]
        made, scale = normalise(tokens_v[rows, :].astype(F32) + attn_out)
        unit[rows, :] = made
        scale_one[rows, :] = jnp.broadcast_to(scale, (local // 2, 128))
        full = made * vectors[2:3, :] + vectors[4:5, :]
        normed[rows, :] = full
        normed_low[rows, :] = full.astype(BF)
        if half == 1:
            saves[2].start()
            saves[3].start()

    def ff_one(index):
        in_load(index).wait()
        columns = slice(index * FF_STEP, (index + 1) * FF_STEP)

        def body(part, unused):
            rows = pl.ds(pl.multiple_of(part * 128, 128), 128)
            pre = dot(normed_low[rows, :], in_v[index % 2]) + in_bias[0:1, columns]
            spread = 0.5 + 0.5 * lax.erf(pre * ROOT_HALF)
            hidden[rows, columns] = (pre * spread).astype(BF)
            slope[rows, columns] = (spread + pre * (ROOT_TURN * jnp.exp(-0.5 * pre * pre))).astype(BF)
            return unused

        lax.fori_loop(0, local // 128, body, 0)
        if index + 2 < ff_steps:
            in_load(index + 2).start()
        if index == ff_steps - 1:
            saves[0].start()
            saves[1].start()

    def out_own():
        own.wait()
        at = pl.ds(pl.multiple_of(z * per, 128), per)
        total[...] = dot(hidden[:, at], weight[at, :]) + normed[...] + vectors[1:2, :]

    def out_shard(half, distance, side):
        plan.arrived(half, distance, side)

        @pl.when(plan.arrives(side, distance))
        def _():
            at = pl.ds(pl.multiple_of(plan.shard_of(side, distance) * per + half * 512, 128), 512)
            total[...] += dot(hidden[:, at], weight[at, :])

    pieces = [partial(attn_half, 0), partial(attn_half, 1)]
    pieces += [partial(ff_one, index) for index in range(ff_steps)]
    pieces += [out_own]
    pieces += [partial(out_shard, *event) for event in plan.events]
    for step in range(max(plan.steps, len(pieces))):
        if step < plan.steps:
            plan.step(step)
        if step < len(pieces):
            pieces[step]()
    saves[6].start()

    made, scale = normalise(total[...])
    unit_two[...] = made
    saves[5].start()
    scale_two[...] = jnp.broadcast_to(scale, (local, 128))
    output_low[...] = (made * vectors[3:4, :] + vectors[5:6, :]).astype(BF)
    saves[4].start()
    emb[...] = dot(output_low[...], proj_weight[...]).astype(BF)
    emb_all[pl.ds(z, 1)] = emb[...].reshape(1, local, 128)

    def emb_move(step):
        return remote(emb, emb_all.at[z], e_sem.at[0, step - 1], e_sem.at[1, step - 1], dp, lax.rem(z + step, nz))

    for step in range(1, nz):
        emb_move(step).start()
    plan.drain()
    for save in saves:
        save.wait()
    for step in range(1, nz):
        emb_move(step).wait()


def second(out_weight, mixed, tokens, attn_all, in_all, in_bias, vectors, proj_weight):
    local, width = tokens.shape
    ff = in_all.shape[1]
    shape = jax.ShapeDtypeStruct
    dma = pltpu.SemaphoreType.DMA
    return pl.pallas_call(
        second_kernel,
        in_specs=hbm_specs(5) + vmem_specs(3),
        out_specs=hbm_specs(5) + vmem_specs(1) + hbm_specs(2) + vmem_specs(2),
        out_shape=[
            shape((ff, width), BF),
            shape((local, ff), BF),
            shape((local, ff), BF),
            shape((local, width), BF),
            shape((local, width), F32),
            shape((local, 128), F32),
            shape((local, width), BF),
            shape((local, width), F32),
            shape((local, 128), F32),
            shape((4, local, 128), BF),
        ],
        scratch_shapes=[
            pltpu.VMEM((ff, width), BF),
            pltpu.VMEM((local, width), BF),
            pltpu.VMEM((local, width), BF),
            pltpu.VMEM((width, width), BF),
            pltpu.VMEM((2, width, FF_STEP), BF),
            pltpu.VMEM((local, ff), BF),
            pltpu.VMEM((local, ff), BF),
            pltpu.VMEM((local, width), F32),
            pltpu.VMEM((local, width), BF),
            pltpu.VMEM((local, width), F32),
            pltpu.VMEM((local, width), F32),
            pltpu.VMEM((local, width), BF),
            pltpu.VMEM((local, width), F32),
            pltpu.VMEM((local, 128), BF),
        ]
        + gather_sems(2)
        + [dma((4,)), dma((2,)), dma((7,)), dma((2, 3))],
        compiler_params=pltpu.CompilerParams(collective_id=1, has_side_effects=True, vmem_limit_bytes=VMEM_BIG),
    )(out_weight, mixed, tokens, attn_all, in_all, in_bias, vectors, proj_weight)


def norm_back(unit, scale, gain, grad):
    dn = grad * gain
    back = scale * (
        dn - jnp.mean(dn, axis=-1, keepdims=True) - unit * jnp.mean(dn * unit, axis=-1, keepdims=True)
    )
    return back, jnp.sum(grad * unit, axis=0), jnp.sum(grad, axis=0)


def segment_facts(lengths, doc_pairs, log_temp, local, z, dp_count):
    base = z * local
    row_lengths = lengths[0]
    seg_range = jnp.arange(SEGS, dtype=jnp.int32)
    seg_ends = jnp.sum(jnp.where(seg_range[:, None] >= seg_range[None, :], row_lengths[None, :], 0), axis=1)
    seg_starts = seg_ends - row_lengths
    positions = jnp.arange(SEQ, dtype=jnp.int32)
    seg_ids = jnp.sum((positions[:, None] >= seg_ends[None, :]).astype(jnp.int32), axis=1)
    near = jnp.arange(3 * local, dtype=jnp.int32) + base - local
    near_ids = jnp.sum((near[:, None] >= seg_ends[None, :]).astype(jnp.int32), axis=1)
    near_ids = jnp.where((near >= 0) & (near < SEQ), near_ids, -1)
    near_member = near_ids[:, None] == jnp.arange(SEGS, dtype=jnp.int32)[None, :]
    near_starts = jnp.sum(jnp.where(near_member, seg_starts[None, :], 0), axis=1)
    offsets = jnp.where(near_ids >= 0, near - near_starts, 0)
    half_dim = HDIM // 2
    inv_freq = jnp.exp(jnp.arange(half_dim, dtype=F32) * (-2.0 * math.log(10000.0) / HDIM))
    angles = offsets.astype(F32)[:, None] * inv_freq[None, :]
    cosine, sine = jnp.cos(angles), jnp.sin(angles)
    cosine = jnp.concatenate([cosine] * 4, axis=1)
    sine = jnp.concatenate([-sine, sine] * 2, axis=1)
    seg_q = jnp.broadcast_to(lax.slice_in_dim(near_ids, local, 2 * local)[None, :], (8, local))
    seg_k = jnp.broadcast_to(near_ids[:, None], (3 * local, 128))
    key_starts = jnp.where(near_ids >= 0, near_starts - base + local, 0)
    near_ends = jnp.sum(jnp.where(near_member, seg_ends[None, :], 0), axis=1)
    key_ends = jnp.where(near_ids >= 0, near_ends - base + local, 0)

    def live_blocks(rows):
        first_key = key_starts[local : 2 * local : rows]
        last_key = key_ends[local + rows - 1 : 2 * local : rows]
        return jnp.stack([first_key // BK, (last_key + BK - 1) // BK], axis=1)

    bounds = jnp.concatenate([live_blocks(FWD_ROWS), live_blocks(BACK_ROWS)])
    query_end = seg_ends[NQ - 1]
    info = jnp.stack([base // CB, (query_end + CB - 1) // CB, query_end // CB])
    seg_col = jnp.broadcast_to(seg_ids[:, None], (SEQ, 128))
    seg_row = jnp.broadcast_to(seg_ids[None, :], (8, SEQ))
    counts = jnp.broadcast_to(row_lengths.astype(F32)[:, None], (SEGS, 128))
    positive = (doc_pairs[0][:, None] == jnp.arange(128, dtype=jnp.int32)[None, :]).astype(F32)
    loss_scale = 1.0 / (NQ * dp_count)
    temp_row = jnp.concatenate([log_temp, jnp.full((127,), loss_scale, F32)]).reshape(1, 128)

    return bounds, seg_q, seg_k, cosine, sine, info, seg_col, seg_row, counts, positive, temp_row


def per_device(
    tokens, lengths, doc_pairs, qkv_weight, qkv_bias, attn_weight, attn_bias, ffn_in_weight, ffn_in_bias,
    ffn_out_weight, ffn_out_bias, norm_gains, norm_shifts, proj_weight, log_temp,
):
    local, width = tokens.shape
    dp_count = lax.axis_size("dp")
    tensor_count = lax.axis_size("tensor")
    groups = dp_count // 8
    z = lax.axis_index("tensor")
    bounds, seg_q, seg_k, cosine, sine, info, seg_col, seg_row, counts, positive, temp_row = segment_facts(
        lengths, doc_pairs, log_temp, local, z, dp_count
    )
    gains = norm_gains.astype(F32)
    shifts = norm_shifts.astype(F32)
    bias = jnp.concatenate([qkv_bias.reshape(6, 128), ffn_in_bias.reshape(8, 128), jnp.zeros((2, 128), BF)])
    qkv_all, attn_all, in_all, window, bias_all, queries, keys, keys_t, values, values_t = first(
        jnp.transpose(qkv_weight, (1, 0, 2)), attn_weight, ffn_in_weight, tokens, bias, cosine, sine
    )
    in_bias_all = bias_all[:, 6:14].reshape(1, 4 * width).astype(F32)
    vectors = jnp.concatenate(
        [attn_bias.astype(F32)[None], ffn_out_bias.astype(F32)[None], gains, shifts, jnp.zeros((2, width), F32)]
    )
    mixed, lse = attend(bounds[: local // FWD_ROWS], queries, keys, values_t, seg_q, seg_k)
    out_all, hidden, slope, normed_low, unit_one, scale_one, output_low, unit_two, scale_two, embedded_all = second(
        ffn_out_weight, mixed, tokens, attn_all, in_all, in_bias_all, vectors, proj_weight
    )
    embedded_all = embedded_all.reshape(-1, EMB)
    scale_one, scale_two = scale_one[:, :1], scale_two[:, :1]
    emb_grad, row_loss, row_temp = contrast(info, embedded_all, seg_col, seg_row, counts, positive, temp_row, local)

    proj_grad = dot(output_low, emb_grad, 0, 0)
    output_grad = dot(emb_grad, proj_weight, 1, 1)
    resid_two_grad, gain_two_grad, shift_two_grad = norm_back(unit_two, scale_two, gains[1], output_grad)
    ffn_grad = resid_two_grad.astype(BF)
    out_bias_grad = jnp.sum(ffn_grad.astype(F32), axis=0)
    hidden_grad = dot(ffn_grad, out_all, 1, 1)
    pre_grad = (hidden_grad * slope.astype(F32)).astype(BF)
    in_bias_grad = jnp.sum(pre_grad.astype(F32), axis=0)
    normed_grad = dot(pre_grad, in_all, 1, 1) + resid_two_grad
    resid_one_grad, gain_one_grad, shift_one_grad = norm_back(unit_one, scale_one, gains[0], normed_grad)
    attn_grad = resid_one_grad.astype(BF)
    attn_bias_grad = jnp.sum(attn_grad.astype(F32), axis=0)
    mixed_grad = dot(attn_grad, attn_all, 1, 1).astype(BF)
    dq, dk, dv = attend_back(bounds[local // FWD_ROWS :], queries, keys, keys_t, values, mixed, mixed_grad, lse, seg_q, seg_k, cosine, sine)
    window_grad = dot(dk, qkv_all[1], 1, 1) + dot(dv, qkv_all[2], 1, 1)
    window_low = window_grad.astype(BF)
    own_grad = window_grad[local : 2 * local] + dot(dq, qkv_all[0], 1, 1) + resid_one_grad
    qkv_bias_grad = jnp.concatenate([jnp.sum(part.astype(F32), axis=0) for part in (dq, dk, dv)])

    share = 1.0 / tensor_count
    proj_red = lax.psum(proj_grad, ("dp", "tensor"))
    small = jnp.concatenate(
        [
            attn_bias_grad, out_bias_grad, gain_one_grad, gain_two_grad, shift_one_grad, shift_two_grad,
            qkv_bias_grad, in_bias_grad, row_loss[0, :1] * share, row_temp[0, :1] * share,
            jnp.zeros((SMALL_ROWS * 128 - 13 * width - 2,), F32),
        ]
    ).reshape(SMALL_ROWS, 128)

    def arrange(array):
        if groups == 1:
            return array
        rows = array.shape[0]
        return array.reshape(rows, groups, 8, -1).transpose(0, 2, 1, 3).reshape(rows, width)

    qkv_red, attn_red, in_red, out_red, small, from_left, from_right = scatter(
        arrange(window), arrange(attn_grad), arrange(normed_low), arrange(ffn_grad),
        dq, dk, dv, mixed, pre_grad, hidden, window_low, small,
    )
    if groups > 1:
        ranks = [[high * 8 + low for high in range(groups)] for low in range(8)]
        qkv_red, attn_red, in_red, out_red = (
            lax.psum_scatter(part, "dp", scatter_dimension=0, axis_index_groups=ranks, tiled=True)
            for part in (qkv_red, attn_red, in_red, out_red)
        )
        small = lax.psum(small, "dp", axis_index_groups=ranks)
    tokens_grad = (
        own_grad
        + jnp.where(z > 0, from_left.astype(F32), 0.0)
        + jnp.where(z < tensor_count - 1, from_right.astype(F32), 0.0)
    )
    flat = small.reshape(-1)

    def cut(start, length):
        return lax.slice_in_dim(flat, start * width, (start + length) * width)

    qkv_bias_red = lax.dynamic_slice_in_dim(cut(6, 3).reshape(3, width), z * 256, 256, 1)
    in_bias_red = lax.dynamic_slice_in_dim(cut(9, 4), z * width, width, 0)
    return (
        flat[13 * width : 13 * width + 1],
        output_low,
        tokens_grad,
        qkv_red.reshape(-1, 3, 256),
        qkv_bias_red,
        attn_red.T,
        cut(0, 1),
        in_red,
        in_bias_red,
        out_red.T,
        cut(1, 1),
        cut(2, 2).reshape(2, width),
        cut(4, 2).reshape(2, width),
        proj_red,
        flat[13 * width + 1 : 13 * width + 2],
    )


def solution(mesh):
    in_specs = (
        P(("dp", "tensor"), None),
        P("dp", None),
        P("dp", None),
        P(None, None, "tensor"),
        P(None, "tensor"),
        P("tensor", None),
        P(),
        P(None, "tensor"),
        P("tensor"),
        P("tensor", None),
        P(),
        P(),
        P(),
        P(),
        P(),
    )
    out_specs = (
        P(),
        P(("dp", "tensor"), None),
        P(("dp", "tensor"), None),
        P("dp", None, "tensor"),
        P(None, "tensor"),
        P("tensor", "dp"),
        P(),
        P("dp", "tensor"),
        P("tensor"),
        P("tensor", "dp"),
        P(),
        P(),
        P(),
        P(),
        P(),
    )
    return jax.shard_map(
        per_device, mesh=mesh, in_specs=in_specs, out_specs=out_specs, check_vma=False
    )
```

```python
from functools import partial
import math

import jax
import jax.numpy as jnp
from jax import lax
from jax.experimental import pallas as pl
from jax.experimental.pallas import tpu as pltpu
from jax.sharding import PartitionSpec as P

HDIM = 64
EMB = 128
SEQ = 2048
SEGS = 16
NQ = 8
MESH = pl.DeviceIdType.MESH
ANY = pl.ANY
F32 = jnp.float32
BF = jnp.bfloat16
eps_norm = 1e-05
eps_unit = 1e-06
VMEM_BIG = 60 * 1024 * 1024


def dot(left, right, left_dim=1, right_dim=0, precision=None):
    return lax.dot_general(
        left,
        right,
        (((left_dim,), (right_dim,)), ((), ())),
        preferred_element_type=F32,
        precision=precision,
    )


def hbm_specs(count):
    return [pl.BlockSpec(memory_space=ANY)] * count


def vmem_specs(count):
    return [pl.BlockSpec(memory_space=pltpu.VMEM)] * count


def rotate_lanes(values, cosine, sine):
    out = []
    front = lax.rem(lax.broadcasted_iota(jnp.int32, (1, 128), 1), 64) < 32
    for start in range(0, values.shape[1], 128):
        part = values[:, start : start + 128]
        partner = jnp.where(front, pltpu.roll(part, 96, 1), pltpu.roll(part, 32, 1))
        out.append(part * cosine + partner * sine)
    return out[0] if len(out) == 1 else jnp.concatenate(out, axis=1)


FWD_ROWS = 128
BACK_ROWS = 256
BK = 256
FWD_GROUPS = 8
SCALE = HDIM**-0.5


def split_pair(values, dim=1):
    shape = (1, 128) if dim == 1 else (128, 1)
    first = lax.broadcasted_iota(jnp.int32, shape, dim) < 64
    zero = jnp.zeros_like(values)
    return jnp.where(first, values, zero), jnp.where(first, zero, values)


def turn(values):
    return values.astype(F32).T.astype(BF)


def attend_kernel(bounds_ref, query_ref, key_ref, turned_ref, segq_ref, segk_ref, mixed_ref, lse_ref):
    first = lax.broadcasted_iota(jnp.int32, (128, 1), 0) < 64
    one = jnp.ones((), BF)
    groups = range(0, query_ref.shape[1], 128)
    for block in range(query_ref.shape[0] // FWD_ROWS):
        rows = pl.ds(block * FWD_ROWS, FWD_ROWS)
        queries = [split_pair(turn(query_ref[rows, at : at + 128] * jnp.asarray(SCALE, BF)), 0) for at in groups]
        seg_q = segq_ref[0:1, rows]

        def body(index, carry):
            keys_at = pl.ds(pl.multiple_of(index * BK, BK), BK)
            live = segk_ref[keys_at, 0:1] == seg_q
            made = []
            for group, at in enumerate(groups):
                keys = key_ref[keys_at, at : at + 128]
                values = turned_ref[at : at + 128, keys_at]
                weights = (jnp.where(first, values, one), jnp.where(first, one, values))
                for head in range(2):
                    top, acc = carry[2 * group + head]
                    scores = jnp.where(live, dot(keys, queries[group][head]), -1e9)
                    new_top = jnp.maximum(top, jnp.max(scores, axis=0, keepdims=True))
                    probs = jnp.exp(scores - new_top).astype(BF)
                    acc = acc * jnp.exp(top - new_top) + dot(weights[head], probs)
                    made.append((new_top, acc))
            return tuple(made)

        start = tuple((jnp.full((1, FWD_ROWS), -2e9, F32), jnp.zeros((128, FWD_ROWS), F32)) for _ in range(2 * len(groups)))
        done = lax.fori_loop(bounds_ref[block, 0], bounds_ref[block, 1], body, start)
        for group, at in enumerate(groups):
            (top0, acc0), (top1, acc1) = done[2 * group : 2 * group + 2]
            total0, total1 = acc0[64:65], acc1[0:1]
            mixed = jnp.concatenate([acc0[0:64] / total0, acc1[64:128] / total1], axis=0)
            mixed_ref[rows, at : at + 128] = mixed.T.astype(BF)
            lse_ref[2 * group : 2 * group + 1, rows] = top0 + jnp.log(total0)
            lse_ref[2 * group + 1 : 2 * group + 2, rows] = top1 + jnp.log(total1)


def attend(bounds, queries, keys, turned, seg_q, seg_k):
    local, width = queries.shape
    long = keys.shape[0]
    lanes = FWD_GROUPS * 128
    return pl.pallas_call(
        attend_kernel,
        grid_spec=pltpu.PrefetchScalarGridSpec(
            num_scalar_prefetch=1,
            grid=(width // lanes,),
            in_specs=[
                pl.BlockSpec((local, lanes), lambda g, b: (0, g)),
                pl.BlockSpec((long, lanes), lambda g, b: (0, g)),
                pl.BlockSpec((lanes, long), lambda g, b: (g, 0)),
                pl.BlockSpec((8, local), lambda g, b: (0, 0)),
                pl.BlockSpec((long, 128), lambda g, b: (0, 0)),
            ],
            out_specs=[
                pl.BlockSpec((local, lanes), lambda g, b: (0, g)),
                pl.BlockSpec((2 * FWD_GROUPS, local), lambda g, b: (g, 0)),
            ],
        ),
        out_shape=[
            jax.ShapeDtypeStruct((local, width), BF),
            jax.ShapeDtypeStruct((width // HDIM, local), F32),
        ],
        compiler_params=pltpu.CompilerParams(vmem_limit_bytes=40 * 2**20),
        cost_estimate=pl.CostEstimate(flops=2 * 2**30, bytes_accessed=8 * 2**20, transcendentals=4 * 2**20),
    )(bounds, queries, keys, turned, seg_q, seg_k)


CB = 512
HIGH = lax.Precision.HIGHEST


def halves(values):
    high = values.astype(BF)
    return high, (values - high.astype(F32)).astype(BF)


def contrast_kernel(
    info_ref, emb_ref, segc_ref, segr_ref, counts_ref, positive_ref, temp_ref, grad_ref, loss_ref, tgrad_ref,
    unit, docs, docs_t, marks, marks_row, ratio, ratio_t, weights,
):
    own0, query_blocks, doc0 = info_ref[0], info_ref[1], info_ref[2]
    blocks = emb_ref.shape[0] // CB
    own_blocks = grad_ref.shape[0] // CB
    lane = lax.broadcasted_iota(jnp.int32, (1, 128), 1)
    widths = (EMB, EMB * 3 // 4, EMB // 2)
    loss_scale = temp_ref[0:1, 1:2]
    temp_inv = jnp.exp(-temp_ref[0:1, 0:1])
    segs = segc_ref[...]
    docs[...] = jnp.where((segs - NQ == lane) | ((segs == lane) & (lane >= NQ)), 1.0, 0.0).astype(BF)
    marks[...] = jnp.where((segs == lane) & (lane < NQ), 1.0, 0.0)
    down = lax.broadcasted_iota(jnp.int32, (128, 1), 0)
    across = segr_ref[0:1, :]
    docs_t[...] = jnp.where((across - NQ == down) | ((across == down) & (down >= NQ)), 1.0, 0.0).astype(BF)
    marks_row[...] = jnp.where(segr_ref[...] == lax.broadcasted_iota(jnp.int32, (NQ, 1), 0), 1.0, 0.0)
    for index, prefix in enumerate(widths):
        emb = jnp.where(lane < prefix, emb_ref[...].astype(F32), 0.0)
        unit[index] = (emb * lax.rsqrt(jnp.sum(emb * emb, axis=1, keepdims=True) + eps_unit)).astype(BF)

    def at(index):
        return pl.ds(pl.multiple_of(index * CB, CB), CB)

    def similar(index, rows, columns):
        return jnp.exp(10.0 * dot(unit[index, at(rows), :], unit[index, at(columns), :], 1, 1) - 10.0)

    def total_rows(row, seg_sums):
        def total_cols(column, totals):
            mask = docs[at(column), :]
            made = []
            for index in range(3):
                high, low = halves(similar(index, row, column))
                made.append(totals[index] + dot(high, mask) + dot(low, mask))
            return tuple(made)

        totals = lax.fori_loop(doc0, blocks, total_cols, (jnp.zeros((CB, 128), F32),) * 3)
        made = []
        for index in range(3):
            total = jnp.where(lane < NQ, totals[index], 1.0)
            ratio[index, at(row), :] = 1.0 / total
            smooth = jnp.log(total) / 10.0 + 1.0
            made.append(seg_sums[index] + dot(marks_row[:, at(row)], smooth, 1, 0, HIGH))
        return tuple(made)

    seg_sums = lax.fori_loop(0, query_blocks, total_rows, (jnp.zeros((NQ, 128), F32),) * 3)
    valid = lax.broadcasted_iota(jnp.int32, (NQ, 128), 1) < NQ
    inv_counts = 1.0 / counts_ref[0:NQ, :]
    positive = positive_ref[...]
    loss = jnp.zeros((1, 1), F32)
    tgrad = jnp.zeros((1, 1), F32)
    weights[...] = jnp.zeros_like(weights)
    for index in range(3):
        logits = jnp.where(valid, seg_sums[index] * inv_counts * temp_inv, 0.0)
        top = jnp.max(jnp.where(valid, logits, -1e30), axis=1, keepdims=True)
        powers = jnp.where(valid, jnp.exp(logits - top), 0.0)
        power_sum = jnp.sum(powers, axis=1, keepdims=True)
        term = jnp.log(power_sum) + top - jnp.sum(logits * positive, axis=1, keepdims=True)
        loss = loss + jnp.sum(term, axis=0, keepdims=True) * loss_scale
        dlogits = (powers / power_sum - positive) * loss_scale
        tgrad = tgrad - jnp.sum(jnp.sum(dlogits * logits, axis=1, keepdims=True), axis=0, keepdims=True)
        weights[index, 0:NQ, :] = dlogits * temp_inv * inv_counts

    def weigh(row, unused):
        for index in range(3):
            weight = dot(marks[at(row), :], weights[index], 1, 0, HIGH) * ratio[index, at(row), :]
            weight = jnp.where(lane < NQ, weight, 0.0)
            high = weight.astype(BF).astype(F32)
            both = high + pltpu.roll(weight - high, NQ, 1)
            ratio[index, at(row), :] = both
            ratio_t[index, :, at(row)] = both.T.astype(BF)
        return unused

    lax.fori_loop(0, query_blocks, weigh, 0)

    for own in range(own_blocks):
        mine = own0 + own

        def as_query(column, grads):
            mask = docs_t[:, at(column)]
            made = []
            for index in range(3):
                spread = dot(ratio[index, at(mine), :].astype(BF), mask)
                sim_grad = (similar(index, mine, column) * spread).astype(BF)
                made.append(grads[index] + dot(sim_grad, unit[index, at(column), :]))
            return tuple(made)

        def as_doc(row, grads):
            mask = docs[at(mine), :]
            made = []
            for index in range(3):
                spread = dot(mask, ratio_t[index, :, at(row)])
                sim_grad = (similar(index, mine, row) * spread).astype(BF)
                made.append(grads[index] + dot(sim_grad, unit[index, at(row), :]))
            return tuple(made)

        grads = (jnp.zeros((CB, 128), F32),) * 3
        grads = lax.fori_loop(doc0, jnp.where(mine < query_blocks, blocks, doc0), as_query, grads)
        grads = lax.fori_loop(0, jnp.where(mine >= doc0, query_blocks, 0), as_doc, grads)
        total = jnp.zeros((CB, 128), F32)
        for index, prefix in enumerate(widths):
            part = jnp.where(lane < prefix, emb_ref[at(mine), :].astype(F32), 0.0)
            scale = lax.rsqrt(jnp.sum(part * part, axis=1, keepdims=True) + eps_unit)
            full = part * scale
            back = scale * (grads[index] - full * jnp.sum(full * grads[index], axis=1, keepdims=True))
            total = total + jnp.where(lane < prefix, back, 0.0)
        grad_ref[pl.ds(own * CB, CB), :] = total.astype(BF)
    loss_ref[...] = jnp.broadcast_to(loss, loss_ref.shape)
    tgrad_ref[...] = jnp.broadcast_to(tgrad, tgrad_ref.shape)


def contrast(info, emb_all, seg_col, seg_row, counts, positive, temp_row, local):
    rows = emb_all.shape[0]
    return pl.pallas_call(
        contrast_kernel,
        in_specs=[pl.BlockSpec(memory_space=pltpu.SMEM)] + vmem_specs(6),
        out_specs=vmem_specs(3),
        out_shape=[
            jax.ShapeDtypeStruct((local, 128), BF),
            jax.ShapeDtypeStruct((8, 128), F32),
            jax.ShapeDtypeStruct((8, 128), F32),
        ],
        scratch_shapes=[
            pltpu.VMEM((3, rows, 128), BF),
            pltpu.VMEM((rows, 128), BF),
            pltpu.VMEM((128, rows), BF),
            pltpu.VMEM((rows, 128), F32),
            pltpu.VMEM((NQ, rows), F32),
            pltpu.VMEM((3, rows, 128), F32),
            pltpu.VMEM((3, 128, rows), BF),
            pltpu.VMEM((3, 128, 128), F32),
        ],
        compiler_params=pltpu.CompilerParams(vmem_limit_bytes=40 * 2**20),
        cost_estimate=pl.CostEstimate(flops=2**30, bytes_accessed=2**22, transcendentals=2**22),
    )(info, emb_all, seg_col, seg_row, counts, positive, temp_row)


CW = 512
HALF = CW // 2
SLOTS_S, SLOTS_R, SLOTS_T, SLOTS_K = 3, 4, 6, 14
SMALL_ROWS = 112
QKV_ROW = 48
LAGS = (4, 7, 2)
RING = 12


def neighbours():
    dp = lax.axis_index("dp")
    low = lax.rem(dp, 8)
    core = lax.rem(low, 2)
    x = lax.rem(low // 2, 2)
    y = low // 4
    return dp, low, core, x, y, dp + 1 - 2 * core, dp + 2 - 4 * x, dp + 4 - 8 * y


def entry_barrier(z, dp, plane, z_count):
    barrier = pltpu.get_barrier_semaphore()
    for other in plane:
        pl.semaphore_signal(barrier, inc=1, device_id={"dp": other, "tensor": z}, device_id_type=MESH)
    for step in range(1, z_count):
        peer = lax.rem(z + step, z_count)
        pl.semaphore_signal(barrier, inc=1, device_id={"dp": dp, "tensor": peer}, device_id_type=MESH)
    pl.semaphore_wait(barrier, len(plane) + z_count - 1)


def remote(src, dst, send_sem, recv_sem, dp, z):
    return pltpu.make_async_remote_copy(
        src_ref=src,
        dst_ref=dst,
        send_sem=send_sem,
        recv_sem=recv_sem,
        device_id={"dp": dp, "tensor": z},
        device_id_type=MESH,
    )


class Scatter:
    def __init__(self, goals, product, finish, refs):
        (self.sbuf, self.rbuf, self.ta, self.tb, self.xra, self.xrb, self.s2a, self.s2b, self.yra, self.yrb, self.keep,
         self.zs, self.zrl, self.zrr, self.s_sem, self.r_sem, self.t_sem, self.xr_sem, self.s2_sem, self.yr_sem,
         self.zs_sem, self.zr_sem, self.credit) = refs
        self.goals, self.product, self.finish = goals, product, finish
        self.count = len(goals)
        self.dp, low, self.core, self.x, self.y, self.to_core, self.to_x, self.to_y = neighbours()
        self.z = lax.axis_index("tensor")
        self.nz = 4
        self.steps = self.count + LAGS[1] + LAGS[2] * (self.nz - 1) + 1

    def barrier(self):
        entry_barrier(self.z, self.dp, (self.to_core, self.to_x, self.to_y), self.nz)

    def block(self, index):
        other, xj, yj = index // 4, index % 2, index % 4 // 2
        core, x, y = (bit + flip - 2 * bit * flip for bit, flip in ((self.core, other), (self.x, xj), (self.y, yj)))
        return pl.ds(pl.multiple_of((core + 2 * x + 4 * y) * 128, 128), 128)

    def core_move(self, i):
        s, r = i % SLOTS_S, i % SLOTS_R
        return remote(self.sbuf.at[s], self.rbuf.at[r], self.s_sem.at[s], self.r_sem.at[r], self.to_core, self.z)

    def ta_move(self, i):
        t, r = i % SLOTS_T, i % RING
        src = self.ta.at[t, pl.ds(2, 2)]
        return remote(src, self.xra.at[r], self.t_sem.at[t, 0], self.xr_sem.at[r, 0], self.to_x, self.z)

    def tb_move(self, i):
        t, r = i % SLOTS_T, i % RING
        src = self.tb.at[t, pl.ds(2, 2)]
        return remote(src, self.xrb.at[r], self.t_sem.at[t, 1], self.xr_sem.at[r, 1], self.to_y, self.z)

    def s2a_move(self, i):
        r = i % RING
        return remote(self.s2a.at[r], self.yra.at[r], self.s2_sem.at[r, 0], self.yr_sem.at[r, 0], self.to_y, self.z)

    def s2b_move(self, i):
        r = i % RING
        return remote(self.s2b.at[r], self.yrb.at[r], self.s2_sem.at[r, 1], self.yr_sem.at[r, 1], self.to_x, self.z)

    def right_move(self, i):
        return remote(self.zs.at[i], self.zrl.at[i], self.zs_sem.at[i], self.zr_sem.at[i, 0], self.dp, self.z + 1)

    def left_move(self, i):
        return remote(self.zs.at[i], self.zrr.at[i], self.zs_sem.at[i], self.zr_sem.at[i, 1], self.dp, self.z - 1)

    def stage_one(self, i):
        if i >= SLOTS_S:
            self.core_move(i - SLOTS_S).wait_send()

        self.sbuf[i % SLOTS_S] = self.product(i, 4).reshape(4, 128, CW).astype(BF)
        if i >= SLOTS_R:
            pl.semaphore_wait(self.credit, 1)
        self.core_move(i).start()

    def stage_two(self, i):
        self.core_move(i).wait_recv()
        slot = i % SLOTS_T
        if i >= SLOTS_T:
            self.ta_move(i - SLOTS_T).wait_send()
            self.tb_move(i - SLOTS_T).wait_send()

        total = self.product(i, 0).reshape(4, 128, CW) + self.rbuf[i % SLOTS_R].astype(F32)
        for j in range(4):
            self.ta[slot, j // 2 + 2 * (j % 2)] = total[j, :, :HALF].astype(BF)
            self.tb[slot, j] = total[j, :, HALF:].astype(BF)
        if i + SLOTS_R < self.count:
            where = {"dp": self.to_core, "tensor": self.z}
            pl.semaphore_signal(self.credit, inc=1, device_id=where, device_id_type=MESH)
        self.ta_move(i).start()
        self.tb_move(i).start()

    def stage_three(self, i):
        slot, k, r = i % SLOTS_T, i % SLOTS_K, i % RING
        if i >= RING:
            self.s2a_move(i - RING).wait_send()
            self.s2b_move(i - RING).wait_send()
        self.ta_move(i).wait_recv()
        self.s2a[r] = (self.ta[slot, 1].astype(F32) + self.xra[r, 1].astype(F32)).astype(BF)
        self.s2a_move(i).start()
        self.keep[k, :, :HALF] = self.ta[slot, 0].astype(F32) + self.xra[r, 0].astype(F32)
        self.tb_move(i).wait_recv()
        self.s2b[r] = (self.tb[slot, 1].astype(F32) + self.xrb[r, 1].astype(F32)).astype(BF)
        self.s2b_move(i).start()
        self.keep[k, :, HALF:] = self.tb[slot, 0].astype(F32) + self.xrb[r, 0].astype(F32)

    def pass_on(self, i, right):
        self.zs[i] = self.keep[i % SLOTS_K].astype(BF)
        (self.right_move(i) if right else self.left_move(i)).start()

    def stage_four(self, i):
        k = i % SLOTS_K
        self.s2a_move(i).wait_recv()
        self.keep[k, :, :HALF] += self.yra[i % RING].astype(F32)
        self.s2b_move(i).wait_recv()
        self.keep[k, :, HALF:] += self.yrb[i % RING].astype(F32)
        if self.goals[i] > 0:
            pl.when(self.z == 0)(lambda: self.pass_on(i, True))
        if self.goals[i] < self.nz - 1:
            pl.when(self.z == self.nz - 1)(lambda: self.pass_on(i, False))

    def stage_five(self, i, hop):
        k = i % SLOTS_K
        goal, last = self.goals[i], self.nz - 1
        if hop <= goal:

            @pl.when(self.z == hop)
            def _():
                self.right_move(i).wait_recv()
                self.keep[k] += self.zrl[i].astype(F32)
                if hop < goal:
                    self.pass_on(i, True)

        if hop <= last - goal:

            @pl.when(self.z == last - hop)
            def _():
                self.left_move(i).wait_recv()
                self.keep[k] += self.zrr[i].astype(F32)
                if last - hop > goal:
                    self.pass_on(i, False)

        if hop == last:
            pl.when(self.z == goal)(lambda: self.finish(i, self.keep.at[k]))

    def late_stages(self, step):
        lag_three, lag_four, spacing = LAGS
        if 0 <= step - lag_three < self.count:
            self.stage_three(step - lag_three)
        if 0 <= step - lag_four < self.count:
            self.stage_four(step - lag_four)
        for hop in range(1, self.nz):
            i = step - lag_four - spacing * hop
            if 0 <= i < self.count:
                self.stage_five(i, hop)

    def drain(self):
        for i in range(self.count):
            if i >= self.count - SLOTS_S:
                self.core_move(i).wait_send()
            if i >= self.count - SLOTS_T:
                self.ta_move(i).wait_send()
                self.tb_move(i).wait_send()
            if i >= self.count - RING:
                self.s2a_move(i).wait_send()
                self.s2b_move(i).wait_send()
            pl.when(self.z < self.goals[i])(lambda i=i: self.right_move(i).wait_send())
            pl.when(self.z > self.goals[i])(lambda i=i: self.left_move(i).wait_send())


def scatter_scratch(n):
    dma = pltpu.SemaphoreType.DMA
    slots_k = min(SLOTS_K, n)
    return [
        pltpu.VMEM((SLOTS_S, 4, 128, CW), BF),
        pltpu.VMEM((SLOTS_R, 4, 128, CW), BF),
        pltpu.VMEM((SLOTS_T, 4, 128, HALF), BF),
        pltpu.VMEM((SLOTS_T, 4, 128, HALF), BF),
        pltpu.VMEM((RING, 2, 128, HALF), BF),
        pltpu.VMEM((RING, 2, 128, HALF), BF),
        pltpu.VMEM((RING, 128, HALF), BF),
        pltpu.VMEM((RING, 128, HALF), BF),
        pltpu.VMEM((RING, 128, HALF), BF),
        pltpu.VMEM((RING, 128, HALF), BF),
        pltpu.VMEM((slots_k, 128, CW), F32),
        pltpu.VMEM((n, 128, CW), BF),
        pltpu.VMEM((n, 128, CW), BF),
        pltpu.VMEM((n, 128, CW), BF),
        dma((SLOTS_S,)),
        dma((SLOTS_R,)),
        dma((SLOTS_T, 2)),
        dma((RING, 2)),
        dma((RING, 2)),
        dma((RING, 2)),
        dma((n,)),
        dma((n, 2)),
        pltpu.SemaphoreType.REGULAR,
    ]


CHUNKS = (
    [("out", i) for i in range(4)] + [("qk", 0), ("vm", 0)] + [("out", i) for i in range(4, 8)] + [("qk", 1), ("vm", 1)]
    + [("in", i) for i in range(3)] + [("qk", 2), ("vm", 2)] + [("in", i) for i in range(3, 6)] + [("qk", 3), ("vm", 3)]
    + [("in", i) for i in range(6, 8)]
)
ATTEND_AT = {0: (0, 0), 3: (0, 1), 6: (1, 0), 9: (1, 1), 12: (2, 0), 14: (2, 1), 17: (3, 0), 19: (3, 1)}
TOKENS_AT = {
    4: ((0, 1),), 7: ((0, 0),), 8: ((0, 2),), 10: ((1, 1),), 12: ((1, 0),), 13: ((1, 2),), 15: ((2, 1),),
    17: ((2, 0),), 18: ((2, 2),), 20: ((3, 0), (3, 2)), 22: ((3, 1),),
}
HALO_AT = {21: 0, 23: 1, 25: 2, 27: 3}
HEADS_AT = {2: 1, 7: 2, 13: 3}
SMALL_AT = {20: 0, 22: 1, 24: 2, 26: 3, 30: 4}
INPUTS_AT = {0: 0, 4: 1, 5: 2, 12: 3}
WIDE = [i for i, (kind, part) in enumerate(CHUNKS) if kind in ("out", "in")]


def last_kernel(
    window, attn_grad, normed, ffn_grad, hidden, pre_grad, query, key, value, mixed, mixed_grad, qkv_all, resid_grad,
    lse_ref, segq_ref, segk_ref, cos_ref, sin_ref, small_ref,
    out_qkv, out_attn, out_in, out_out, small_out, token_grad,
    xw, xa, xn, xf, gs, q_v, g_v, m_v, k_v, v_v, weight, dk_acc, dv_acc, dq_b, dk_b, dv_b, send_l, send_r, from_l, from_r,
    sums, sacc, srec, zsm, x_sem, g_sem, h_sem, w_sem, sm_sem, smz_sem, e_sem, *refs,
):
    local = attn_grad.shape[1]
    turned = ((ffn_grad, xf), (window, xw), (attn_grad, xa), (normed, xn))
    resid_load = pltpu.make_async_copy(resid_grad, token_grad, x_sem.at[4, 0])

    def x_loads(which):
        source, target = turned[which]
        return [
            pltpu.make_async_copy(source.at[plan.block(index), :], target.at[index], x_sem.at[which, index])
            for index in range(8)
        ]

    def g_load(order):
        kind, part = CHUNKS[WIDE[order]]
        source = hidden if kind == "out" else pre_grad
        return pltpu.make_async_copy(source.at[:, pl.ds(part * CW, CW)], gs.at[order % 3], g_sem.at[order % 3])

    def head_loads(shard):
        columns, slot = pl.ds(shard * 256, 256), shard % 2
        pairs = ((query, q_v), (mixed_grad, g_v), (mixed, m_v), (key, k_v), (value, v_v))
        return [
            pltpu.make_async_copy(source.at[:, columns], target.at[slot], h_sem.at[slot, index])
            for index, (source, target) in enumerate(pairs)
        ]

    def weight_load(shard):
        columns = pl.ds(shard * 256, 256)
        return pltpu.make_async_copy(qkv_all.at[:, :, columns], weight.at[shard % 2], w_sem.at[shard % 2])

    def product(i, start):
        kind, part = CHUNKS[i]
        four = slice(start, start + 4)
        if kind in ("out", "in"):
            left = (xf if kind == "out" else xn)[four].reshape(512, local)
            return dot(left, gs[WIDE.index(i) % 3])
        wide = xw[four].reshape(512, 3 * local)
        if kind == "qk":
            parts = dot(wide[:, local : 2 * local], dq_b[...]), dot(wide, dk_b[...])
        else:
            parts = dot(wide, dv_b[...]), dot(xa[four].reshape(512, local), m_v[part % 2])
        return jnp.concatenate(parts, axis=1)

    def finish(i, kept):
        kind, part = CHUNKS[i]
        if kind == "qk":
            out_qkv[:, 0:512] = kept[...]
        elif kind == "vm":
            out_qkv[:, 512:768] = kept[:, 0:256]
            out_attn[...] = kept[:, 256:512].T
        elif kind == "in":
            out_in[:, pl.ds((part % 2) * CW, CW)] = kept[...]
        else:
            out_out[pl.ds((part % 2) * CW, CW), :] = kept[...].T

    goals = [part if kind in ("qk", "vm") else part // 2 for kind, part in CHUNKS]
    plan = Scatter(goals, product, finish, refs)
    z, dp, nz = plan.z, plan.dp, plan.nz
    has_l, has_r = z > 0, z < nz - 1
    for copy in (
        *x_loads(0), g_load(0), *head_loads(0), g_load(1), *x_loads(1), g_load(2), *x_loads(2), *x_loads(3), resid_load
    ):
        copy.start()
    weight_load(0).start()
    plan.barrier()

    def to_left(piece):
        at = pl.ds(piece * 128, 128)
        return remote(send_l.at[at], from_r.at[at], e_sem.at[piece, 0], e_sem.at[piece, 1], dp, z - 1)

    def to_right(piece):
        at = pl.ds(piece * 128, 128)
        return remote(send_r.at[at], from_l.at[at], e_sem.at[piece, 2], e_sem.at[piece, 3], dp, z + 1)

    peers = (plan.to_core, plan.to_x, plan.to_y)

    def small_move(stage):
        return remote(sacc.at[stage], srec.at[stage], sm_sem.at[stage, 0], sm_sem.at[stage, 1], peers[stage], z)

    def small_z_move(step):
        sems = smz_sem.at[step - 1, 0], smz_sem.at[step - 1, 1]
        return remote(sacc.at[3], zsm.at[step - 1], *sems, dp, lax.rem(z + step, nz))

    def small_stage(stage):
        if stage == 0:
            sacc[0] = small_ref[...]
            sacc[0, QKV_ROW : QKV_ROW + 24, :] = sums[...]
        if 1 <= stage <= 3:
            small_move(stage - 1).wait_recv()
            sacc[stage] = sacc[stage - 1] + srec[stage - 1]
        if stage <= 2:
            small_move(stage).start()
        if stage == 3:
            for step in range(1, nz):
                small_z_move(step).start()
        if stage == 4:
            for step in range(1, nz):
                small_z_move(step).wait_recv()
            total = None
            for owner in range(nz):
                made = jnp.where(z == owner, sacc[3], 0.0)
                for step in range(1, nz):
                    made = jnp.where(lax.rem(z - step + nz, nz) == owner, zsm[step - 1], made)
                total = made if total is None else total + made
            small_out[...] = total

    head_row = lax.broadcasted_iota(jnp.int32, (8, 128), 0)
    head_lane = lax.broadcasted_iota(jnp.int32, (8, 128), 1) // 64
    chosen = jnp.where(head_row == head_lane, 1.0, 0.0)
    groups = (0, 128)

    def attend_part(shard, block):
        slot = shard % 2
        if block == 0:
            for load in head_loads(shard):
                load.wait()
            dk_acc[...] = jnp.zeros_like(dk_acc)
            dv_acc[...] = jnp.zeros_like(dv_acc)
        rows = slice(block * BACK_ROWS, (block + 1) * BACK_ROWS)
        queries, grads, turned_q, turned_g, deltas, logs = [], [], [], [], [], []
        for group, at in enumerate(groups):
            lanes = slice(at, at + 128)
            scaled = q_v[slot, rows, lanes] * jnp.asarray(SCALE, BF)
            grad = g_v[slot, rows, lanes]
            queries.append(split_pair(scaled))
            grads.append(split_pair(grad))
            turned_q.append(split_pair(turn(scaled), 0))
            turned_g.append(split_pair(turn(grad), 0))
            delta = dot(chosen, m_v[slot, rows, lanes].astype(F32) * grad.astype(F32), 1, 1, lax.Precision.HIGHEST)
            deltas.append((delta[0:1], delta[1:2]))
            first_head = 4 * shard + 2 * group
            logs.append([lse_ref[first_head + head : first_head + head + 1, rows] for head in range(2)])
        seg_q = segq_ref[0:1, rows]

        def body(index, carry):
            keys_at = pl.ds(pl.multiple_of(index * BK, BK), BK)
            live = segk_ref[keys_at, 0:1] == seg_q
            made = []
            for group, at in enumerate(groups):
                lanes = slice(at, at + 128)
                keys = k_v[slot, keys_at, lanes]
                values = v_v[slot, keys_at, lanes]
                turned = turn(keys)
                dk, dv = 0.0, 0.0
                for head in range(2):
                    scores = jnp.where(live, dot(keys, turned_q[group][head]), -1e9)
                    probs = jnp.exp(scores - logs[group][head])
                    score_low = (probs * (dot(values, turned_g[group][head]) - deltas[group][head])).astype(BF)
                    made.append(carry[2 * group + head] + dot(turned, score_low))
                    dk = dk + dot(score_low, queries[group][head])
                    dv = dv + dot(probs.astype(BF), grads[group][head])
                dk_acc[keys_at, lanes] += dk
                dv_acc[keys_at, lanes] += dv
            return tuple(made)

        reach = local // BK * 2 + 1
        start = (jnp.zeros((128, BACK_ROWS), F32),) * 4
        done = lax.fori_loop(block, block + reach, body, start)
        at_window = slice(local + block * BACK_ROWS, local + (block + 1) * BACK_ROWS)
        for group, at in enumerate(groups):
            grad = jnp.concatenate([done[2 * group][0:64], done[2 * group + 1][64:128]], axis=0).T * SCALE
            back = rotate_lanes(grad, cos_ref[at_window, :], -sin_ref[at_window, :])
            dq_b[rows, at : at + 128] = back.astype(BF)
        if block == local // BACK_ROWS - 1:
            dk_b[...] = rotate_lanes(dk_acc[...], cos_ref[...], -sin_ref[...]).astype(BF)
            dv_b[...] = dv_acc[...].astype(BF)
            for kind, ref in enumerate((dq_b, dk_b, dv_b)):
                total = jnp.sum(ref[...].astype(F32), axis=0, keepdims=True)
                row = 8 * kind + 2 * shard
                sums[row : row + 1, :] = total[:, 0:128]
                sums[row + 1 : row + 2, :] = total[:, 128:256]

    def token_part(shard, part):
        slot = shard % 2
        if part == (0 if shard == 3 else 1):
            weight_load(shard).wait()
            if shard + 1 < 4:
                weight_load(shard + 1).start()
        if part == 1 and shard == 0:
            resid_load.wait()

        rows = slice(part * local, part * local + local)

        def body(index, unused):
            at = pl.ds(pl.multiple_of(index * 256, 256), 256)
            grad = dot(dk_b[rows, :], weight[slot, 1, at, :], 1, 1) + dot(dv_b[rows, :], weight[slot, 2, at, :], 1, 1)
            if part == 1:
                token_grad[:, at] += grad + dot(dq_b[...], weight[slot, 0, at, :], 1, 1)
            else:
                target = send_l if part == 0 else send_r
                target[:, at] = (grad if shard == 0 else grad + target[:, at].astype(F32)).astype(BF)
            return unused

        lax.fori_loop(0, weight.shape[2] // 256, body, 0)

    def add_halo(copy, there, source):
        @pl.when(there)
        def _():
            for piece in range(local // 128):
                copy(piece).wait_recv()
                rows = slice(piece * 128, piece * 128 + 128)
                token_grad[rows, :] += source[rows, :].astype(F32)

    for step in range(plan.steps):
        if step in INPUTS_AT:
            for load in x_loads(INPUTS_AT[step]):
                load.wait()
        if step < plan.count:
            if step in WIDE:
                g_load(WIDE.index(step)).wait()
            plan.stage_one(step)
        if 0 <= step - 1 < plan.count:
            plan.stage_two(step - 1)
            if step - 1 in WIDE and WIDE.index(step - 1) + 3 < len(WIDE):
                g_load(WIDE.index(step - 1) + 3).start()
        if step in HEADS_AT:
            for load in head_loads(HEADS_AT[step]):
                load.start()
        plan.late_stages(step)
        if step in ATTEND_AT:
            attend_part(*ATTEND_AT[step])
        for piece in TOKENS_AT.get(step, ()):
            token_part(*piece)
        if step in HALO_AT:
            pl.when(has_l)(lambda step=step: to_left(HALO_AT[step]).start())
            pl.when(has_r)(lambda step=step: to_right(HALO_AT[step]).start())
        if step in SMALL_AT:
            small_stage(SMALL_AT[step])
    add_halo(to_right, has_l, from_l)
    add_halo(to_left, has_r, from_r)
    plan.drain()
    for stage in range(3):
        small_move(stage).wait_send()
    for step in range(1, nz):
        small_z_move(step).wait_send()
    for piece in range(local // 128):
        pl.when(has_l)(lambda piece=piece: to_left(piece).wait_send())
        pl.when(has_r)(lambda piece=piece: to_right(piece).wait_send())


def last(
    window, attn_grad, normed, ffn_grad, hidden, pre_grad, query, key, value, mixed, mixed_grad, qkv_all, resid_grad,
    lse, seg_q, seg_k, cosine, sine, small,
):
    width, local = attn_grad.shape
    long = window.shape[1]
    shape = jax.ShapeDtypeStruct
    dma = pltpu.SemaphoreType.DMA
    return pl.pallas_call(
        last_kernel,
        in_specs=hbm_specs(13) + vmem_specs(6),
        out_specs=vmem_specs(6),
        out_shape=[
            shape((128, 768), F32),
            shape((256, 128), F32),
            shape((128, 1024), F32),
            shape((1024, 128), F32),
            shape(small.shape, F32),
            shape((local, width), F32),
        ],
        scratch_shapes=[
            pltpu.VMEM((8, 128, long), BF),
            pltpu.VMEM((8, 128, local), BF),
            pltpu.VMEM((8, 128, local), BF),
            pltpu.VMEM((8, 128, local), BF),
            pltpu.VMEM((3, local, CW), BF),
            pltpu.VMEM((2, local, 256), BF),
            pltpu.VMEM((2, local, 256), BF),
            pltpu.VMEM((2, local, 256), BF),
            pltpu.VMEM((2, long, 256), BF),
            pltpu.VMEM((2, long, 256), BF),
            pltpu.VMEM((2, 3, width, 256), BF),
            pltpu.VMEM((long, 256), F32),
            pltpu.VMEM((long, 256), F32),
            pltpu.VMEM((local, 256), BF),
            pltpu.VMEM((long, 256), BF),
            pltpu.VMEM((long, 256), BF),
            pltpu.VMEM((local, width), BF),
            pltpu.VMEM((local, width), BF),
            pltpu.VMEM((local, width), BF),
            pltpu.VMEM((local, width), BF),
            pltpu.VMEM((24, 128), F32),
            pltpu.VMEM((4,) + small.shape, F32),
            pltpu.VMEM((3,) + small.shape, F32),
            pltpu.VMEM((3,) + small.shape, F32),
            dma((5, 8)),
            dma((3,)),
            dma((2, 5)),
            dma((2,)),
            dma((3, 2)),
            dma((3, 2)),
            dma((4, 4)),
        ]
        + scatter_scratch(len(CHUNKS)),
        compiler_params=pltpu.CompilerParams(
            collective_id=2, has_side_effects=True, vmem_limit_bytes=62 * 2**20
        ),
    )(
        window, attn_grad, normed, ffn_grad, hidden, pre_grad, query, key, value, mixed, mixed_grad, qkv_all, resid_grad,
        lse, seg_q, seg_k, cosine, sine, small,
    )


def shard_rows(kind, ref):
    return ref.shape[1] if kind == "qkv" else (512 if kind in ("out0", "out1") else ref.shape[0])


def source_rows(kind, ref, start, rows):
    if kind == "qkv":
        return ref.at[:, pl.ds(start, rows), :]
    if kind == "out1":
        start = pl.multiple_of(start + 512, 16)
    return ref.at[pl.ds(start, rows), :]


def gathered_rows(kind, ref, shard, start, rows):
    if kind == "qkv":
        return ref.at[:, pl.ds(start, rows), pl.ds(pl.multiple_of(shard * 256, 256), 256)]
    if kind == "in":
        return ref.at[pl.ds(start, rows), pl.ds(pl.multiple_of(shard * 1024, 1024), 1024)]
    per = ref.shape[0] // 4
    if kind == "out1":
        start = start + 512
    return ref.at[pl.ds(pl.multiple_of(shard * per + start, 16), rows), :]


class Gather:
    def __init__(self, kinds, srcs, outs, z_send, z_recv, p_send, p_recv, lag):
        self.kinds, self.srcs, self.outs = kinds, srcs, outs
        self.z_send, self.z_recv, self.p_send, self.p_recv = z_send, z_recv, p_send, p_recv
        self.dp, low, core, x, y, self.to_core, self.to_x, self.to_y = neighbours()
        self.z = lax.axis_index("tensor")
        self.nz = 4
        self.has_l, self.has_r = self.z > 0, self.z < self.nz - 1
        low_x, low_y = low + 2 - 4 * x, low + 4 - 8 * y
        low_xy = low_x + 4 - 8 * y
        self.low = low
        self.places = {
            0: (low, None), 1: (low, None), 4: (low, None), 2: (low_x, 0), 3: (low_y, 1),
            5: (low_x, None), 6: (low_y, None), 7: (low_xy, 0), 8: (low_xy, 1),
        }
        self.events = [(m, distance, side) for m in range(len(kinds)) for distance in (1, 2, 3) for side in (0, 1)]
        self.lag = lag
        self.steps = len(self.events) + 2 * lag

    def barrier(self):
        entry_barrier(self.z, self.dp, (self.to_core, self.to_x, self.to_y), self.nz)

    def piece(self, m, shard, index, half=None):
        rows = shard_rows(self.kinds[m], self.srcs[m]) // 8
        start = index * rows
        if half is not None:
            rows = rows // 2
            start = start + half * rows
        return gathered_rows(self.kinds[m], self.outs[m], shard, pl.multiple_of(start, 16), rows)

    def shard_of(self, side, distance):
        return self.z - distance if side == 0 else self.z + distance

    def onward(self, side):
        return self.z + 1 if side == 0 else self.z - 1

    def can_send(self, side):
        return self.has_r if side == 0 else self.has_l

    def arrives(self, side, distance):
        return self.z >= distance if side == 0 else self.z + distance < self.nz

    def own_move(self, m, side):
        rows = shard_rows(self.kinds[m], self.srcs[m]) // 8
        src = source_rows(self.kinds[m], self.srcs[m], pl.multiple_of(self.low * rows, 16), rows)
        sems = self.z_send.at[m, side, 0], self.z_recv.at[m, side, 0]
        return remote(src, self.piece(m, self.z, self.low), *sems, self.dp, self.onward(side))

    def relay_move(self, m, side, distance):
        at = self.piece(m, self.shard_of(side, distance), self.low)
        sems = self.z_send.at[m, side, distance], self.z_recv.at[m, side, distance]
        return remote(at, at, *sems, self.dp, self.onward(side))

    def plane_move(self, m, side, distance, kind):
        ref = self.piece(m, self.shard_of(side, distance), *self.places[kind])
        to = {0: self.to_x, 1: self.to_y, 2: self.to_y, 3: self.to_x}.get(kind, self.to_core)
        slot = side * 3 + distance - 1
        return remote(ref, ref, self.p_send.at[m, slot, kind], self.p_recv.at[m, slot, kind], to, self.z)

    def own_start(self, m):
        for side in (0, 1):
            pl.when(self.can_send(side))(lambda side=side: self.own_move(m, side).start())

    def stage_z(self, m, distance, side):
        if side == 0 and distance == 2 and m + 1 < len(self.kinds):
            self.own_start(m + 1)

        @pl.when(self.arrives(side, distance))
        def _():
            if distance == 1:
                self.own_move(m, side).wait_recv()
            else:
                self.relay_move(m, side, distance - 1).wait_recv()
            if distance < 3:
                pl.when(self.can_send(side))(lambda: self.relay_move(m, side, distance).start())
            for kind in (0, 1, 4):
                self.plane_move(m, side, distance, kind).start()

    def stage_plane(self, m, distance, side, waits, shift):
        @pl.when(self.arrives(side, distance))
        def _():
            for kind in waits:
                self.plane_move(m, side, distance, kind).wait_recv()
                for more in shift:
                    self.plane_move(m, side, distance, kind + more).start()

    def step(self, step):
        count = len(self.events)
        if step < count:
            self.stage_z(*self.events[step])
        if 0 <= step - self.lag < count:
            self.stage_plane(*self.events[step - self.lag], (0, 1), (2, 5))
        if 0 <= step - 2 * self.lag < count:
            self.stage_plane(*self.events[step - 2 * self.lag], (2, 3), (5,))

    def arrived(self, m, distance, side):
        self.stage_plane(m, distance, side, (4, 5, 6, 7, 8), ())

    def arrived_all(self, m):
        for distance in (1, 2, 3):
            for side in (0, 1):
                self.arrived(m, distance, side)

    def drain(self):
        for m, distance, side in self.events:

            @pl.when(self.arrives(side, distance))
            def _():
                for kind in range(9):
                    self.plane_move(m, side, distance, kind).wait_send()
                if distance < 3:
                    pl.when(self.can_send(side))(lambda: self.relay_move(m, side, distance).wait_send())

        for m in range(len(self.kinds)):
            for side in (0, 1):
                pl.when(self.can_send(side))(lambda side=side: self.own_move(m, side).wait_send())


def gather_sems(n):
    dma = pltpu.SemaphoreType.DMA
    return [dma((n, 2, 3)), dma((n, 2, 3)), dma((n, 6, 9)), dma((n, 6, 9))]


def first_kernel(
    qkv_src, attn_src, in_src, tokens, bias, cos_ref, sin_ref,
    qkv_out, attn_out, in_out, window_out, bias_all, query_out, key_out, value_out, value_t_out,
    weight, xw, turned, query, key, value, value_t, stage_a, stage_i,
    z_send, z_recv, p_send, p_recv, l_sem, h_sem, b_sem, o_sem,
):
    plan = Gather(
        ("qkv", "attn", "in"), (qkv_src, attn_src, in_src), (weight, attn_out, in_out), z_send, z_recv, p_send, p_recv, 4
    )
    z, dp, nz = plan.z, plan.dp, plan.nz
    local = tokens.shape[0]
    own_qkv = pltpu.make_async_copy(qkv_src, gathered_rows("qkv", weight, z, 0, qkv_src.shape[1]), l_sem.at[0])
    a_in = pltpu.make_async_copy(attn_src, stage_a, l_sem.at[1])
    i_in = pltpu.make_async_copy(in_src, stage_i, l_sem.at[2])
    a_out = pltpu.make_async_copy(stage_a, gathered_rows("attn", attn_out, z, 0, attn_src.shape[0]), l_sem.at[3])
    i_out = pltpu.make_async_copy(stage_i, gathered_rows("in", in_out, z, 0, in_src.shape[0]), l_sem.at[4])
    own_tokens = pltpu.make_async_copy(tokens, xw.at[pl.ds(local, local)], h_sem.at[4])
    fill_l = pltpu.make_async_copy(tokens, xw.at[pl.ds(0, local)], h_sem.at[5])
    fill_r = pltpu.make_async_copy(tokens, xw.at[pl.ds(2 * local, local)], h_sem.at[6])
    for copy in (own_qkv, a_in, i_in, own_tokens):
        copy.start()
    pl.when(jnp.logical_not(plan.has_l))(lambda: fill_l.start())
    pl.when(jnp.logical_not(plan.has_r))(lambda: fill_r.start())
    bias_all[pl.ds(z, 1)] = bias[...].reshape(1, *bias.shape)
    plan.barrier()
    to_left = remote(tokens, xw.at[pl.ds(2 * local, local)], h_sem.at[0], h_sem.at[1], dp, z - 1)
    to_right = remote(tokens, xw.at[pl.ds(0, local)], h_sem.at[2], h_sem.at[3], dp, z + 1)

    def bias_move(step):
        return remote(bias, bias_all.at[z], b_sem.at[0, step - 1], b_sem.at[1, step - 1], dp, lax.rem(z + step, nz))

    plan.own_start(0)
    for step in range(1, nz):
        bias_move(step).start()
    a_in.wait()
    a_out.start()
    i_in.wait()
    i_out.start()

    weight_out = pltpu.make_async_copy(weight, qkv_out, o_sem.at[0])

    def outputs(shard):
        columns = pl.ds(shard * 256, 256)
        return [
            pltpu.make_async_copy(turned.at[columns, :], window_out.at[columns, :], o_sem.at[1 + 5 * shard]),
            pltpu.make_async_copy(query.at[:, columns], query_out.at[:, columns], o_sem.at[2 + 5 * shard]),
            pltpu.make_async_copy(key.at[:, columns], key_out.at[:, columns], o_sem.at[3 + 5 * shard]),
            pltpu.make_async_copy(value.at[:, columns], value_out.at[:, columns], o_sem.at[4 + 5 * shard]),
            pltpu.make_async_copy(value_t.at[columns, :], value_t_out.at[columns, :], o_sem.at[5 + 5 * shard]),
        ]

    def ready():
        plan.arrived_all(0)
        own_qkv.wait()
        own_tokens.wait()
        weight_out.start()
        for step in range(1, nz):
            bias_move(step).wait_recv()

    def halo_ready():
        pl.when(plan.has_l)(lambda: to_right.wait_recv())
        pl.when(plan.has_r)(lambda: to_left.wait_recv())
        pl.when(jnp.logical_not(plan.has_l))(lambda: fill_l.wait())
        pl.when(jnp.logical_not(plan.has_r))(lambda: fill_r.wait())

    def compute(shard, part):
        columns = slice(shard * 256, shard * 256 + 256)
        rows = slice(part * local, part * local + local)
        window = xw[rows, :]
        cosine, sine = cos_ref[rows, :], sin_ref[rows, :]

        def made(kind):
            add = [bias_all[shard, 2 * kind + i : 2 * kind + i + 1, :].astype(F32) for i in range(2)]
            return dot(window, weight[kind, :, columns]) + jnp.concatenate(add, axis=1)

        turned[columns, rows] = turn(window[:, columns])
        if part == 1:
            query[:, columns] = rotate_lanes(made(0), cosine, sine).astype(BF)
        keys = rotate_lanes(made(1), cosine, sine)
        key[rows, columns] = keys.astype(BF)
        values = made(2)
        value[rows, columns] = values.astype(BF)
        value_t[columns, rows] = values.T.astype(BF)

    pieces = [ready]
    pieces += [partial(compute, shard, 1) for shard in range(4)]
    pieces += [halo_ready]
    for shard in range(4):
        pieces += [partial(compute, shard, 0), partial(compute, shard, 2)]
        pieces += [lambda shard=shard: [copy.start() for copy in outputs(shard)]]
    first_piece = 6 + 2 * plan.lag
    for step in range(max(plan.steps, first_piece + len(pieces))):
        if step < plan.steps:
            plan.step(step)
        if step == 5:
            pl.when(plan.has_l)(lambda: to_left.start())
            pl.when(plan.has_r)(lambda: to_right.start())
        if step >= first_piece and pieces:
            pieces.pop(0)()
    for m in (1, 2):
        plan.arrived_all(m)
    plan.drain()
    a_out.wait()
    i_out.wait()
    for step in range(1, nz):
        bias_move(step).wait_send()
    pl.when(plan.has_l)(lambda: to_left.wait_send())
    pl.when(plan.has_r)(lambda: to_right.wait_send())
    weight_out.wait()
    for shard in range(4):
        for copy in outputs(shard):
            copy.wait()


def first(qkv_weight, attn_weight, in_weight, tokens, bias, cosine, sine):
    local, width = tokens.shape
    long = 3 * local
    shape = jax.ShapeDtypeStruct
    dma = pltpu.SemaphoreType.DMA
    return pl.pallas_call(
        first_kernel,
        in_specs=hbm_specs(4) + vmem_specs(3),
        out_specs=hbm_specs(4) + vmem_specs(1) + hbm_specs(4),
        out_shape=[
            shape((3, width, width), BF),
            shape((width, width), BF),
            shape((width, 4 * width), BF),
            shape((width, long), BF),
            shape((4,) + bias.shape, BF),
            shape((local, width), BF),
            shape((long, width), BF),
            shape((long, width), BF),
            shape((width, long), BF),
        ],
        scratch_shapes=[
            pltpu.VMEM((3, width, width), BF),
            pltpu.VMEM((long, width), BF),
            pltpu.VMEM((width, long), BF),
            pltpu.VMEM((local, width), BF),
            pltpu.VMEM((long, width), BF),
            pltpu.VMEM((long, width), BF),
            pltpu.VMEM((width, long), BF),
            pltpu.VMEM(attn_weight.shape, BF),
            pltpu.VMEM(in_weight.shape, BF),
        ]
        + gather_sems(3)
        + [dma((5,)), dma((7,)), dma((2, 3)), dma((21,))],
        compiler_params=pltpu.CompilerParams(collective_id=0, has_side_effects=True, vmem_limit_bytes=VMEM_BIG),
    )(qkv_weight, attn_weight, in_weight, tokens, bias, cosine, sine)


def normalise(values):
    mean_value = jnp.mean(values, axis=1, keepdims=True)
    centered = values - mean_value
    variance = jnp.mean(centered * centered, axis=1, keepdims=True)
    scale = lax.rsqrt(variance + eps_norm)
    return centered * scale, scale


FF_STEP = 512
ROOT_HALF = math.sqrt(0.5)
ROOT_TURN = 1.0 / math.sqrt(2.0 * math.pi)


def second_kernel(
    out_src, mixed, tokens, attn_all, in_all, in_bias, vectors, proj_weight,
    out_all, hidden_out, slope_out, normed_out, unit_one_out, scale_one, output_out, unit_two_out, scale_two, emb_all,
    weight, mixed_v, tokens_v, attn_v, in_v, hidden, slope, normed, normed_low, normed_t, total, unit, output_low, unit_two, emb,
    z_send, z_recv, p_send, p_recv, l_sem, i_sem, o_sem, e_sem,
):
    plan = Gather(("out0", "out1"), (out_src, out_src), (weight, weight), z_send, z_recv, p_send, p_recv, 4)
    z, dp, nz = plan.z, plan.dp, plan.nz
    local = tokens.shape[0]
    per = out_src.shape[0]
    own = pltpu.make_async_copy(out_src, weight.at[pl.ds(pl.multiple_of(z * per, 16), per)], l_sem.at[0])
    loads = [
        pltpu.make_async_copy(src, dst, l_sem.at[1 + index])
        for index, (src, dst) in enumerate(((mixed, mixed_v), (attn_all, attn_v), (tokens, tokens_v)))
    ]
    ff = in_all.shape[1]
    ff_steps = ff // FF_STEP

    def in_load(index):
        return pltpu.make_async_copy(
            in_all.at[:, pl.ds(index * FF_STEP, FF_STEP)], in_v.at[index % 2], i_sem.at[index % 2]
        )

    for copy in (*loads, own, in_load(0), in_load(1)):
        copy.start()
    plan.barrier()
    plan.own_start(0)

    saves = [
        pltpu.make_async_copy(src, dst, o_sem.at[index])
        for index, (src, dst) in enumerate(
            ((hidden, hidden_out), (slope, slope_out), (normed_t, normed_out), (unit, unit_one_out),
             (output_low, output_out), (unit_two, unit_two_out), (weight, out_all))
        )
    ]

    def attn_half(half):
        if half == 0:
            for load in loads:
                load.wait()
        rows = slice(half * (local // 2), (half + 1) * (local // 2))
        attn_out = dot(mixed_v[rows, :], attn_v[...]) + vectors[0:1, :]
        made, scale = normalise(tokens_v[rows, :].astype(F32) + attn_out)
        unit[rows, :] = made
        scale_one[rows, :] = jnp.broadcast_to(scale, (local // 2, 128))
        full = made * vectors[2:3, :] + vectors[4:5, :]
        normed[rows, :] = full
        normed_low[rows, :] = full.astype(BF)
        normed_t[:, rows] = full.T.astype(BF)
        if half == 1:
            saves[2].start()
            saves[3].start()

    def ff_one(index):
        in_load(index).wait()
        columns = slice(index * FF_STEP, (index + 1) * FF_STEP)

        def body(part, unused):
            rows = pl.ds(pl.multiple_of(part * 128, 128), 128)
            pre = dot(normed_low[rows, :], in_v[index % 2]) + in_bias[0:1, columns]
            spread = 0.5 + 0.5 * lax.erf(pre * ROOT_HALF)
            hidden[rows, columns] = (pre * spread).astype(BF)
            slope[rows, columns] = (spread + pre * (ROOT_TURN * jnp.exp(-0.5 * pre * pre))).astype(BF)
            return unused

        lax.fori_loop(0, local // 128, body, 0)
        if index + 2 < ff_steps:
            in_load(index + 2).start()
        if index == ff_steps - 1:
            saves[0].start()
            saves[1].start()

    def out_own():
        own.wait()
        at = pl.ds(pl.multiple_of(z * per, 128), per)
        total[...] = dot(hidden[:, at], weight[at, :]) + normed[...] + vectors[1:2, :]

    def out_shard(half, distance, side):
        plan.arrived(half, distance, side)

        @pl.when(plan.arrives(side, distance))
        def _():
            at = pl.ds(pl.multiple_of(plan.shard_of(side, distance) * per + half * 512, 128), 512)
            total[...] += dot(hidden[:, at], weight[at, :])

    pieces = [partial(attn_half, 0), partial(attn_half, 1)]
    pieces += [partial(ff_one, index) for index in range(ff_steps)]
    pieces += [out_own]
    pieces += [partial(out_shard, *event) for event in plan.events]
    for step in range(max(plan.steps, len(pieces))):
        if step < plan.steps:
            plan.step(step)
        if step < len(pieces):
            pieces[step]()
    saves[6].start()

    made, scale = normalise(total[...])
    unit_two[...] = made
    saves[5].start()
    scale_two[...] = jnp.broadcast_to(scale, (local, 128))
    output_low[...] = (made * vectors[3:4, :] + vectors[5:6, :]).astype(BF)
    saves[4].start()
    emb[...] = dot(output_low[...], proj_weight[...]).astype(BF)
    emb_all[pl.ds(z, 1)] = emb[...].reshape(1, local, 128)

    def emb_move(step):
        return remote(emb, emb_all.at[z], e_sem.at[0, step - 1], e_sem.at[1, step - 1], dp, lax.rem(z + step, nz))

    for step in range(1, nz):
        emb_move(step).start()
    plan.drain()
    for save in saves:
        save.wait()
    for step in range(1, nz):
        emb_move(step).wait()


def second(out_weight, mixed, tokens, attn_all, in_all, in_bias, vectors, proj_weight):
    local, width = tokens.shape
    ff = in_all.shape[1]
    shape = jax.ShapeDtypeStruct
    dma = pltpu.SemaphoreType.DMA
    return pl.pallas_call(
        second_kernel,
        in_specs=hbm_specs(5) + vmem_specs(3),
        out_specs=hbm_specs(5) + vmem_specs(1) + hbm_specs(2) + vmem_specs(2),
        out_shape=[
            shape((ff, width), BF),
            shape((local, ff), BF),
            shape((local, ff), BF),
            shape((width, local), BF),
            shape((local, width), F32),
            shape((local, 128), F32),
            shape((local, width), BF),
            shape((local, width), F32),
            shape((local, 128), F32),
            shape((4, local, 128), BF),
        ],
        scratch_shapes=[
            pltpu.VMEM((ff, width), BF),
            pltpu.VMEM((local, width), BF),
            pltpu.VMEM((local, width), BF),
            pltpu.VMEM((width, width), BF),
            pltpu.VMEM((2, width, FF_STEP), BF),
            pltpu.VMEM((local, ff), BF),
            pltpu.VMEM((local, ff), BF),
            pltpu.VMEM((local, width), F32),
            pltpu.VMEM((local, width), BF),
            pltpu.VMEM((width, local), BF),
            pltpu.VMEM((local, width), F32),
            pltpu.VMEM((local, width), F32),
            pltpu.VMEM((local, width), BF),
            pltpu.VMEM((local, width), F32),
            pltpu.VMEM((local, 128), BF),
        ]
        + gather_sems(2)
        + [dma((4,)), dma((2,)), dma((7,)), dma((2, 3))],
        compiler_params=pltpu.CompilerParams(collective_id=1, has_side_effects=True, vmem_limit_bytes=VMEM_BIG),
    )(out_weight, mixed, tokens, attn_all, in_all, in_bias, vectors, proj_weight)


def norm_back(unit, scale, gain, grad):
    dn = grad * gain
    back = scale * (
        dn - jnp.mean(dn, axis=-1, keepdims=True) - unit * jnp.mean(dn * unit, axis=-1, keepdims=True)
    )
    return back, jnp.sum(grad * unit, axis=0), jnp.sum(grad, axis=0)


def segment_facts(lengths, doc_pairs, log_temp, local, z, dp_count):
    base = z * local
    row_lengths = lengths[0]
    seg_range = jnp.arange(SEGS, dtype=jnp.int32)
    seg_ends = jnp.sum(jnp.where(seg_range[:, None] >= seg_range[None, :], row_lengths[None, :], 0), axis=1)
    seg_starts = seg_ends - row_lengths
    positions = jnp.arange(SEQ, dtype=jnp.int32)
    seg_ids = jnp.sum((positions[:, None] >= seg_ends[None, :]).astype(jnp.int32), axis=1)
    near = jnp.arange(3 * local, dtype=jnp.int32) + base - local
    near_ids = jnp.sum((near[:, None] >= seg_ends[None, :]).astype(jnp.int32), axis=1)
    near_ids = jnp.where((near >= 0) & (near < SEQ), near_ids, -1)
    near_member = near_ids[:, None] == jnp.arange(SEGS, dtype=jnp.int32)[None, :]
    near_starts = jnp.sum(jnp.where(near_member, seg_starts[None, :], 0), axis=1)
    offsets = jnp.where(near_ids >= 0, near - near_starts, 0)
    half_dim = HDIM // 2
    inv_freq = jnp.exp(jnp.arange(half_dim, dtype=F32) * (-2.0 * math.log(10000.0) / HDIM))
    angles = offsets.astype(F32)[:, None] * inv_freq[None, :]
    cosine, sine = jnp.cos(angles), jnp.sin(angles)
    cosine = jnp.concatenate([cosine] * 4, axis=1)
    sine = jnp.concatenate([-sine, sine] * 2, axis=1)
    seg_q = jnp.broadcast_to(lax.slice_in_dim(near_ids, local, 2 * local)[None, :], (8, local))
    seg_k = jnp.broadcast_to(near_ids[:, None], (3 * local, 128))
    key_starts = jnp.where(near_ids >= 0, near_starts - base + local, 0)
    near_ends = jnp.sum(jnp.where(near_member, seg_ends[None, :], 0), axis=1)
    key_ends = jnp.where(near_ids >= 0, near_ends - base + local, 0)

    def live_blocks(rows):
        first_key = key_starts[local : 2 * local : rows]
        last_key = key_ends[local + rows - 1 : 2 * local : rows]
        return jnp.stack([first_key // BK, (last_key + BK - 1) // BK], axis=1)

    bounds = live_blocks(FWD_ROWS)
    query_end = seg_ends[NQ - 1]
    info = jnp.stack([base // CB, (query_end + CB - 1) // CB, query_end // CB])
    seg_col = jnp.broadcast_to(seg_ids[:, None], (SEQ, 128))
    seg_row = jnp.broadcast_to(seg_ids[None, :], (8, SEQ))
    counts = jnp.broadcast_to(row_lengths.astype(F32)[:, None], (SEGS, 128))
    positive = (doc_pairs[0][:, None] == jnp.arange(128, dtype=jnp.int32)[None, :]).astype(F32)
    loss_scale = 1.0 / (NQ * dp_count)
    temp_row = jnp.concatenate([log_temp, jnp.full((127,), loss_scale, F32)]).reshape(1, 128)

    return bounds, seg_q, seg_k, cosine, sine, info, seg_col, seg_row, counts, positive, temp_row


def per_device(
    tokens, lengths, doc_pairs, qkv_weight, qkv_bias, attn_weight, attn_bias, ffn_in_weight, ffn_in_bias,
    ffn_out_weight, ffn_out_bias, norm_gains, norm_shifts, proj_weight, log_temp,
):
    local, width = tokens.shape
    dp_count = lax.axis_size("dp")
    tensor_count = lax.axis_size("tensor")
    groups = dp_count // 8
    z = lax.axis_index("tensor")
    bounds, seg_q, seg_k, cosine, sine, info, seg_col, seg_row, counts, positive, temp_row = segment_facts(
        lengths, doc_pairs, log_temp, local, z, dp_count
    )
    gains = norm_gains.astype(F32)
    shifts = norm_shifts.astype(F32)
    bias = jnp.concatenate([qkv_bias.reshape(6, 128), ffn_in_bias.reshape(8, 128), jnp.zeros((2, 128), BF)])
    qkv_all, attn_all, in_all, window_t, bias_all, queries, keys, values, values_t = first(
        jnp.transpose(qkv_weight, (1, 0, 2)), attn_weight, ffn_in_weight, tokens, bias, cosine, sine
    )
    in_bias_all = bias_all[:, 6:14].reshape(1, 4 * width).astype(F32)
    vectors = jnp.concatenate(
        [attn_bias.astype(F32)[None], ffn_out_bias.astype(F32)[None], gains, shifts, jnp.zeros((2, width), F32)]
    )
    mixed, lse = attend(bounds, queries, keys, values_t, seg_q, seg_k)
    out_all, hidden, slope, normed_t, unit_one, scale_one, output_low, unit_two, scale_two, embedded_all = second(
        ffn_out_weight, mixed, tokens, attn_all, in_all, in_bias_all, vectors, proj_weight
    )
    embedded_all = embedded_all.reshape(-1, EMB)
    scale_one, scale_two = scale_one[:, :1], scale_two[:, :1]
    emb_grad, row_loss, row_temp = contrast(info, embedded_all, seg_col, seg_row, counts, positive, temp_row, local)

    proj_grad = dot(output_low, emb_grad, 0, 0)
    output_grad = dot(emb_grad, proj_weight, 1, 1)
    resid_two_grad, gain_two_grad, shift_two_grad = norm_back(unit_two, scale_two, gains[1], output_grad)
    ffn_grad = resid_two_grad.astype(BF)
    out_bias_grad = jnp.sum(ffn_grad.astype(F32), axis=0)
    hidden_grad = dot(ffn_grad, out_all, 1, 1)
    pre_grad = (hidden_grad * slope.astype(F32)).astype(BF)
    in_bias_grad = jnp.sum(pre_grad.astype(F32), axis=0)
    normed_grad = dot(pre_grad, in_all, 1, 1) + resid_two_grad
    resid_one_grad, gain_one_grad, shift_one_grad = norm_back(unit_one, scale_one, gains[0], normed_grad)
    attn_grad = resid_one_grad.astype(BF)
    attn_bias_grad = jnp.sum(attn_grad.astype(F32), axis=0)
    mixed_grad = dot(attn_grad, attn_all, 1, 1).astype(BF)
    share = 1.0 / tensor_count
    proj_red = lax.psum(proj_grad, ("dp", "tensor"))
    small = jnp.concatenate(
        [
            attn_bias_grad, out_bias_grad, gain_one_grad, gain_two_grad, shift_one_grad, shift_two_grad,
            jnp.zeros((3 * width,), F32), in_bias_grad, row_loss[0, :1] * share, row_temp[0, :1] * share,
            jnp.zeros((SMALL_ROWS * 128 - 13 * width - 2,), F32),
        ]
    ).reshape(SMALL_ROWS, 128)

    def arrange(array):
        if groups == 1:
            return array
        columns = array.shape[1]
        return array.reshape(groups, 8, -1, columns).transpose(1, 0, 2, 3).reshape(width, columns)

    qkv_red, attn_red, in_red, out_red, small, tokens_grad = last(
        arrange(window_t), arrange(attn_grad.T), arrange(normed_t), arrange(ffn_grad.T), hidden, pre_grad,
        queries, keys, values, mixed, mixed_grad, qkv_all, resid_one_grad, lse, seg_q, seg_k, cosine, sine, small,
    )
    if groups > 1:
        ranks = [[high * 8 + low for high in range(groups)] for low in range(8)]
        qkv_red, attn_red, in_red, out_red = (
            lax.psum_scatter(part, "dp", scatter_dimension=dim, axis_index_groups=ranks, tiled=True)
            for part, dim in ((qkv_red, 0), (attn_red, 1), (in_red, 0), (out_red, 1))
        )
        small = lax.psum(small, "dp", axis_index_groups=ranks)
    flat = small.reshape(-1)

    def cut(start, length):
        return lax.slice_in_dim(flat, start * width, (start + length) * width)

    qkv_bias_red = lax.dynamic_slice_in_dim(cut(6, 3).reshape(3, width), z * 256, 256, 1)
    in_bias_red = lax.dynamic_slice_in_dim(cut(9, 4), z * width, width, 0)
    return (
        flat[13 * width : 13 * width + 1],
        output_low,
        tokens_grad,
        qkv_red.reshape(-1, 3, 256),
        qkv_bias_red,
        attn_red,
        cut(0, 1),
        in_red,
        in_bias_red,
        out_red,
        cut(1, 1),
        cut(2, 2).reshape(2, width),
        cut(4, 2).reshape(2, width),
        proj_red,
        flat[13 * width + 1 : 13 * width + 2],
    )


def solution(mesh):
    in_specs = (
        P(("dp", "tensor"), None),
        P("dp", None),
        P("dp", None),
        P(None, None, "tensor"),
        P(None, "tensor"),
        P("tensor", None),
        P(),
        P(None, "tensor"),
        P("tensor"),
        P("tensor", None),
        P(),
        P(),
        P(),
        P(),
        P(),
    )
    out_specs = (
        P(),
        P(("dp", "tensor"), None),
        P(("dp", "tensor"), None),
        P("dp", None, "tensor"),
        P(None, "tensor"),
        P("tensor", "dp"),
        P(),
        P("dp", "tensor"),
        P("tensor"),
        P("tensor", "dp"),
        P(),
        P(),
        P(),
        P(),
        P(),
    )
    return jax.shard_map(
        per_device, mesh=mesh, in_specs=in_specs, out_specs=out_specs, check_vma=False
    )
```

```python
from functools import partial
import math

import jax
import jax.numpy as jnp
from jax import lax
from jax.experimental import pallas as pl
from jax.experimental.pallas import tpu as pltpu
from jax.sharding import PartitionSpec as P

HDIM = 64
EMB = 128
SEQ = 2048
SEGS = 16
NQ = 8
MESH = pl.DeviceIdType.MESH
ANY = pl.ANY
F32 = jnp.float32
BF = jnp.bfloat16
eps_norm = 1e-05
eps_unit = 1e-06
VMEM_BIG = 60 * 1024 * 1024


def dot(left, right, left_dim=1, right_dim=0, precision=None):
    return lax.dot_general(
        left,
        right,
        (((left_dim,), (right_dim,)), ((), ())),
        preferred_element_type=F32,
        precision=precision,
    )


def hbm_specs(count):
    return [pl.BlockSpec(memory_space=ANY)] * count


def vmem_specs(count):
    return [pl.BlockSpec(memory_space=pltpu.VMEM)] * count


def rotate_lanes(values, cosine, sine):
    out = []
    front = lax.rem(lax.broadcasted_iota(jnp.int32, (1, 128), 1), 64) < 32
    for start in range(0, values.shape[1], 128):
        part = values[:, start : start + 128]
        partner = jnp.where(front, pltpu.roll(part, 96, 1), pltpu.roll(part, 32, 1))
        out.append(part * cosine + partner * sine)
    return out[0] if len(out) == 1 else jnp.concatenate(out, axis=1)


FWD_ROWS = 128
BACK_ROWS = 256
BK = 256
FWD_GROUPS = 8
SCALE = HDIM**-0.5


def split_pair(values, dim=1):
    shape = (1, 128) if dim == 1 else (128, 1)
    first = lax.broadcasted_iota(jnp.int32, shape, dim) < 64
    zero = jnp.zeros_like(values)
    return jnp.where(first, values, zero), jnp.where(first, zero, values)


def turn(values):
    return values.T


def attend_kernel(bounds_ref, query_ref, key_ref, turned_ref, segq_ref, segk_ref, mixed_ref, lse_ref):
    first = lax.broadcasted_iota(jnp.int32, (128, 1), 0) < 64
    one = jnp.ones((), BF)
    groups = range(0, query_ref.shape[1], 128)
    for block in range(query_ref.shape[0] // FWD_ROWS):
        rows = pl.ds(block * FWD_ROWS, FWD_ROWS)
        queries = [split_pair(turn(query_ref[rows, at : at + 128] * jnp.asarray(SCALE, BF)), 0) for at in groups]
        seg_q = segq_ref[0:1, rows]

        def body(index, carry):
            keys_at = pl.ds(pl.multiple_of(index * BK, BK), BK)
            live = segk_ref[keys_at, 0:1] == seg_q
            made = []
            for group, at in enumerate(groups):
                keys = key_ref[keys_at, at : at + 128]
                values = turned_ref[at : at + 128, keys_at]
                weights = (jnp.where(first, values, one), jnp.where(first, one, values))
                for head in range(2):
                    top, acc = carry[2 * group + head]
                    scores = jnp.where(live, dot(keys, queries[group][head]), -1e9)
                    new_top = jnp.maximum(top, jnp.max(scores, axis=0, keepdims=True))
                    probs = jnp.exp(scores - new_top).astype(BF)
                    acc = acc * jnp.exp(top - new_top) + dot(weights[head], probs)
                    made.append((new_top, acc))
            return tuple(made)

        start = tuple((jnp.full((1, FWD_ROWS), -2e9, F32), jnp.zeros((128, FWD_ROWS), F32)) for _ in range(2 * len(groups)))
        done = lax.fori_loop(bounds_ref[block, 0], bounds_ref[block, 1], body, start)
        for group, at in enumerate(groups):
            (top0, acc0), (top1, acc1) = done[2 * group : 2 * group + 2]
            total0, total1 = acc0[64:65], acc1[0:1]
            mixed = jnp.concatenate([acc0[0:64] / total0, acc1[64:128] / total1], axis=0)
            mixed_ref[rows, at : at + 128] = mixed.T.astype(BF)
            lse_ref[2 * group : 2 * group + 1, rows] = top0 + jnp.log(total0)
            lse_ref[2 * group + 1 : 2 * group + 2, rows] = top1 + jnp.log(total1)


def attend(bounds, queries, keys, turned, seg_q, seg_k):
    local, width = queries.shape
    long = keys.shape[0]
    lanes = FWD_GROUPS * 128
    return pl.pallas_call(
        attend_kernel,
        grid_spec=pltpu.PrefetchScalarGridSpec(
            num_scalar_prefetch=1,
            grid=(width // lanes,),
            in_specs=[
                pl.BlockSpec((local, lanes), lambda g, b: (0, g)),
                pl.BlockSpec((long, lanes), lambda g, b: (0, g)),
                pl.BlockSpec((lanes, long), lambda g, b: (g, 0)),
                pl.BlockSpec((8, local), lambda g, b: (0, 0)),
                pl.BlockSpec((long, 128), lambda g, b: (0, 0)),
            ],
            out_specs=[
                pl.BlockSpec((local, lanes), lambda g, b: (0, g)),
                pl.BlockSpec((2 * FWD_GROUPS, local), lambda g, b: (g, 0)),
            ],
        ),
        out_shape=[
            jax.ShapeDtypeStruct((local, width), BF),
            jax.ShapeDtypeStruct((width // HDIM, local), F32),
        ],
        compiler_params=pltpu.CompilerParams(vmem_limit_bytes=40 * 2**20),
        cost_estimate=pl.CostEstimate(flops=2 * 2**30, bytes_accessed=8 * 2**20, transcendentals=4 * 2**20),
    )(bounds, queries, keys, turned, seg_q, seg_k)


CB = 512
HIGH = lax.Precision.HIGHEST


def halves(values):
    high = values.astype(BF)
    return high, (values - high.astype(F32)).astype(BF)


def contrast_kernel(
    info_ref, emb_ref, segc_ref, segr_ref, counts_ref, positive_ref, temp_ref, grad_ref, loss_ref, tgrad_ref,
    unit, docs, docs_t, marks, marks_row, ratio, ratio_t, weights,
):
    own0, query_blocks, doc0 = info_ref[0], info_ref[1], info_ref[2]
    blocks = emb_ref.shape[0] // CB
    own_blocks = grad_ref.shape[0] // CB
    lane = lax.broadcasted_iota(jnp.int32, (1, 128), 1)
    widths = (EMB, EMB * 3 // 4, EMB // 2)
    loss_scale = temp_ref[0:1, 1:2]
    temp_inv = jnp.exp(-temp_ref[0:1, 0:1])
    segs = segc_ref[...]
    docs[...] = jnp.where((segs - NQ == lane) | ((segs == lane) & (lane >= NQ)), 1.0, 0.0).astype(BF)
    marks[...] = jnp.where((segs == lane) & (lane < NQ), 1.0, 0.0)
    down = lax.broadcasted_iota(jnp.int32, (128, 1), 0)
    across = segr_ref[0:1, :]
    docs_t[...] = jnp.where((across - NQ == down) | ((across == down) & (down >= NQ)), 1.0, 0.0).astype(BF)
    marks_row[...] = jnp.where(segr_ref[...] == lax.broadcasted_iota(jnp.int32, (NQ, 1), 0), 1.0, 0.0)
    for index, prefix in enumerate(widths):
        emb = jnp.where(lane < prefix, emb_ref[...].astype(F32), 0.0)
        unit[index] = (emb * lax.rsqrt(jnp.sum(emb * emb, axis=1, keepdims=True) + eps_unit)).astype(BF)

    def at(index):
        return pl.ds(pl.multiple_of(index * CB, CB), CB)

    def similar(index, rows, columns):
        return jnp.exp(10.0 * dot(unit[index, at(rows), :], unit[index, at(columns), :], 1, 1) - 10.0)

    def total_rows(row, seg_sums):
        def total_cols(column, totals):
            mask = docs[at(column), :]
            made = []
            for index in range(3):
                high, low = halves(similar(index, row, column))
                made.append(totals[index] + dot(high, mask) + dot(low, mask))
            return tuple(made)

        totals = lax.fori_loop(doc0, blocks, total_cols, (jnp.zeros((CB, 128), F32),) * 3)
        made = []
        for index in range(3):
            total = jnp.where(lane < NQ, totals[index], 1.0)
            ratio[index, at(row), :] = 1.0 / total
            smooth = jnp.log(total) / 10.0 + 1.0
            made.append(seg_sums[index] + dot(marks_row[:, at(row)], smooth, 1, 0, HIGH))
        return tuple(made)

    seg_sums = lax.fori_loop(0, query_blocks, total_rows, (jnp.zeros((NQ, 128), F32),) * 3)
    valid = lax.broadcasted_iota(jnp.int32, (NQ, 128), 1) < NQ
    inv_counts = 1.0 / counts_ref[0:NQ, :]
    positive = positive_ref[...]
    loss = jnp.zeros((1, 1), F32)
    tgrad = jnp.zeros((1, 1), F32)
    weights[...] = jnp.zeros_like(weights)
    for index in range(3):
        logits = jnp.where(valid, seg_sums[index] * inv_counts * temp_inv, 0.0)
        top = jnp.max(jnp.where(valid, logits, -1e30), axis=1, keepdims=True)
        powers = jnp.where(valid, jnp.exp(logits - top), 0.0)
        power_sum = jnp.sum(powers, axis=1, keepdims=True)
        term = jnp.log(power_sum) + top - jnp.sum(logits * positive, axis=1, keepdims=True)
        loss = loss + jnp.sum(term, axis=0, keepdims=True) * loss_scale
        dlogits = (powers / power_sum - positive) * loss_scale
        tgrad = tgrad - jnp.sum(jnp.sum(dlogits * logits, axis=1, keepdims=True), axis=0, keepdims=True)
        weights[index, 0:NQ, :] = dlogits * temp_inv * inv_counts

    def weigh(row, unused):
        for index in range(3):
            weight = dot(marks[at(row), :], weights[index], 1, 0, HIGH) * ratio[index, at(row), :]
            weight = jnp.where(lane < NQ, weight, 0.0)
            high = weight.astype(BF).astype(F32)
            both = high + pltpu.roll(weight - high, NQ, 1)
            ratio[index, at(row), :] = both
            ratio_t[index, :, at(row)] = both.T.astype(BF)
        return unused

    lax.fori_loop(0, query_blocks, weigh, 0)

    for own in range(own_blocks):
        mine = own0 + own

        def as_query(column, grads):
            mask = docs_t[:, at(column)]
            made = []
            for index in range(3):
                spread = dot(ratio[index, at(mine), :].astype(BF), mask)
                sim_grad = (similar(index, mine, column) * spread).astype(BF)
                made.append(grads[index] + dot(sim_grad, unit[index, at(column), :]))
            return tuple(made)

        def as_doc(row, grads):
            mask = docs[at(mine), :]
            made = []
            for index in range(3):
                spread = dot(mask, ratio_t[index, :, at(row)])
                sim_grad = (similar(index, mine, row) * spread).astype(BF)
                made.append(grads[index] + dot(sim_grad, unit[index, at(row), :]))
            return tuple(made)

        grads = (jnp.zeros((CB, 128), F32),) * 3
        grads = lax.fori_loop(doc0, jnp.where(mine < query_blocks, blocks, doc0), as_query, grads)
        grads = lax.fori_loop(0, jnp.where(mine >= doc0, query_blocks, 0), as_doc, grads)
        total = jnp.zeros((CB, 128), F32)
        for index, prefix in enumerate(widths):
            part = jnp.where(lane < prefix, emb_ref[at(mine), :].astype(F32), 0.0)
            scale = lax.rsqrt(jnp.sum(part * part, axis=1, keepdims=True) + eps_unit)
            full = part * scale
            back = scale * (grads[index] - full * jnp.sum(full * grads[index], axis=1, keepdims=True))
            total = total + jnp.where(lane < prefix, back, 0.0)
        grad_ref[pl.ds(own * CB, CB), :] = total.astype(BF)
    loss_ref[...] = jnp.broadcast_to(loss, loss_ref.shape)
    tgrad_ref[...] = jnp.broadcast_to(tgrad, tgrad_ref.shape)


def contrast(info, emb_all, seg_col, seg_row, counts, positive, temp_row, local):
    rows = emb_all.shape[0]
    return pl.pallas_call(
        contrast_kernel,
        in_specs=[pl.BlockSpec(memory_space=pltpu.SMEM)] + vmem_specs(6),
        out_specs=vmem_specs(3),
        out_shape=[
            jax.ShapeDtypeStruct((local, 128), BF),
            jax.ShapeDtypeStruct((8, 128), F32),
            jax.ShapeDtypeStruct((8, 128), F32),
        ],
        scratch_shapes=[
            pltpu.VMEM((3, rows, 128), BF),
            pltpu.VMEM((rows, 128), BF),
            pltpu.VMEM((128, rows), BF),
            pltpu.VMEM((rows, 128), F32),
            pltpu.VMEM((NQ, rows), F32),
            pltpu.VMEM((3, rows, 128), F32),
            pltpu.VMEM((3, 128, rows), BF),
            pltpu.VMEM((3, 128, 128), F32),
        ],
        compiler_params=pltpu.CompilerParams(vmem_limit_bytes=40 * 2**20),
        cost_estimate=pl.CostEstimate(flops=2**30, bytes_accessed=2**22, transcendentals=2**22),
    )(info, emb_all, seg_col, seg_row, counts, positive, temp_row)


CW = 512
HALF = CW // 2
SLOTS_S, SLOTS_R, SLOTS_T, SLOTS_K = 3, 4, 6, 14
SMALL_ROWS = 112
QKV_ROW = 48
LAGS = (4, 7, 2)
RING = 12


def neighbours():
    dp = lax.axis_index("dp")
    low = lax.rem(dp, 8)
    core = lax.rem(low, 2)
    x = lax.rem(low // 2, 2)
    y = low // 4
    return dp, low, core, x, y, dp + 1 - 2 * core, dp + 2 - 4 * x, dp + 4 - 8 * y


def entry_barrier(z, dp, plane, z_count):
    barrier = pltpu.get_barrier_semaphore()
    for other in plane:
        pl.semaphore_signal(barrier, inc=1, device_id={"dp": other, "tensor": z}, device_id_type=MESH)
    for step in range(1, z_count):
        peer = lax.rem(z + step, z_count)
        pl.semaphore_signal(barrier, inc=1, device_id={"dp": dp, "tensor": peer}, device_id_type=MESH)
    pl.semaphore_wait(barrier, len(plane) + z_count - 1)


def remote(src, dst, send_sem, recv_sem, dp, z):
    return pltpu.make_async_remote_copy(
        src_ref=src,
        dst_ref=dst,
        send_sem=send_sem,
        recv_sem=recv_sem,
        device_id={"dp": dp, "tensor": z},
        device_id_type=MESH,
    )


class Scatter:
    def __init__(self, goals, product, finish, refs):
        (self.sbuf, self.rbuf, self.ta, self.tb, self.xra, self.xrb, self.s2a, self.s2b, self.yra, self.yrb, self.keep,
         self.zs, self.zrl, self.zrr, self.s_sem, self.r_sem, self.t_sem, self.xr_sem, self.s2_sem, self.yr_sem,
         self.zs_sem, self.zr_sem, self.credit) = refs
        self.goals, self.product, self.finish = goals, product, finish
        self.count = len(goals)
        self.dp, low, self.core, self.x, self.y, self.to_core, self.to_x, self.to_y = neighbours()
        self.z = lax.axis_index("tensor")
        self.nz = 4
        self.steps = self.count + LAGS[1] + LAGS[2] * (self.nz - 1) + 1

    def barrier(self):
        entry_barrier(self.z, self.dp, (self.to_core, self.to_x, self.to_y), self.nz)

    def block(self, index):
        other, xj, yj = index // 4, index % 2, index % 4 // 2
        core, x, y = (bit + flip - 2 * bit * flip for bit, flip in ((self.core, other), (self.x, xj), (self.y, yj)))
        return pl.ds(pl.multiple_of((core + 2 * x + 4 * y) * 128, 128), 128)

    def core_move(self, i):
        s, r = i % SLOTS_S, i % SLOTS_R
        return remote(self.sbuf.at[s], self.rbuf.at[r], self.s_sem.at[s], self.r_sem.at[r], self.to_core, self.z)

    def ta_move(self, i):
        t, r = i % SLOTS_T, i % RING
        src = self.ta.at[t, pl.ds(2, 2)]
        return remote(src, self.xra.at[r], self.t_sem.at[t, 0], self.xr_sem.at[r, 0], self.to_x, self.z)

    def tb_move(self, i):
        t, r = i % SLOTS_T, i % RING
        src = self.tb.at[t, pl.ds(2, 2)]
        return remote(src, self.xrb.at[r], self.t_sem.at[t, 1], self.xr_sem.at[r, 1], self.to_y, self.z)

    def s2a_move(self, i):
        r = i % RING
        return remote(self.s2a.at[r], self.yra.at[r], self.s2_sem.at[r, 0], self.yr_sem.at[r, 0], self.to_y, self.z)

    def s2b_move(self, i):
        r = i % RING
        return remote(self.s2b.at[r], self.yrb.at[r], self.s2_sem.at[r, 1], self.yr_sem.at[r, 1], self.to_x, self.z)

    def right_move(self, i):
        return remote(self.zs.at[i], self.zrl.at[i], self.zs_sem.at[i], self.zr_sem.at[i, 0], self.dp, self.z + 1)

    def left_move(self, i):
        return remote(self.zs.at[i], self.zrr.at[i], self.zs_sem.at[i], self.zr_sem.at[i, 1], self.dp, self.z - 1)

    def stage_one(self, i):
        if i >= SLOTS_S:
            self.core_move(i - SLOTS_S).wait_send()

        self.sbuf[i % SLOTS_S] = self.product(i, 4).reshape(4, 128, CW).astype(BF)
        if i >= SLOTS_R:
            pl.semaphore_wait(self.credit, 1)
        self.core_move(i).start()

    def stage_two(self, i):
        self.core_move(i).wait_recv()
        slot = i % SLOTS_T
        if i >= SLOTS_T:
            self.ta_move(i - SLOTS_T).wait_send()
            self.tb_move(i - SLOTS_T).wait_send()

        total = self.product(i, 0).reshape(4, 128, CW) + self.rbuf[i % SLOTS_R].astype(F32)
        for j in range(4):
            self.ta[slot, j // 2 + 2 * (j % 2)] = total[j, :, :HALF].astype(BF)
            self.tb[slot, j] = total[j, :, HALF:].astype(BF)
        if i + SLOTS_R < self.count:
            where = {"dp": self.to_core, "tensor": self.z}
            pl.semaphore_signal(self.credit, inc=1, device_id=where, device_id_type=MESH)
        self.ta_move(i).start()
        self.tb_move(i).start()

    def stage_three(self, i):
        slot, k, r = i % SLOTS_T, i % SLOTS_K, i % RING
        if i >= RING:
            self.s2a_move(i - RING).wait_send()
            self.s2b_move(i - RING).wait_send()
        self.ta_move(i).wait_recv()
        self.s2a[r] = (self.ta[slot, 1].astype(F32) + self.xra[r, 1].astype(F32)).astype(BF)
        self.s2a_move(i).start()
        self.keep[k, :, :HALF] = self.ta[slot, 0].astype(F32) + self.xra[r, 0].astype(F32)
        self.tb_move(i).wait_recv()
        self.s2b[r] = (self.tb[slot, 1].astype(F32) + self.xrb[r, 1].astype(F32)).astype(BF)
        self.s2b_move(i).start()
        self.keep[k, :, HALF:] = self.tb[slot, 0].astype(F32) + self.xrb[r, 0].astype(F32)

    def pass_on(self, i, right):
        self.zs[i] = self.keep[i % SLOTS_K].astype(BF)
        (self.right_move(i) if right else self.left_move(i)).start()

    def stage_four(self, i):
        k = i % SLOTS_K
        self.s2a_move(i).wait_recv()
        self.keep[k, :, :HALF] += self.yra[i % RING].astype(F32)
        self.s2b_move(i).wait_recv()
        self.keep[k, :, HALF:] += self.yrb[i % RING].astype(F32)
        if self.goals[i] > 0:
            pl.when(self.z == 0)(lambda: self.pass_on(i, True))
        if self.goals[i] < self.nz - 1:
            pl.when(self.z == self.nz - 1)(lambda: self.pass_on(i, False))

    def stage_five(self, i, hop):
        k = i % SLOTS_K
        goal, last = self.goals[i], self.nz - 1
        if hop <= goal:

            @pl.when(self.z == hop)
            def _():
                self.right_move(i).wait_recv()
                self.keep[k] += self.zrl[i].astype(F32)
                if hop < goal:
                    self.pass_on(i, True)

        if hop <= last - goal:

            @pl.when(self.z == last - hop)
            def _():
                self.left_move(i).wait_recv()
                self.keep[k] += self.zrr[i].astype(F32)
                if last - hop > goal:
                    self.pass_on(i, False)

        if hop == last:
            pl.when(self.z == goal)(lambda: self.finish(i, self.keep.at[k]))

    def late_stages(self, step):
        lag_three, lag_four, spacing = LAGS
        if 0 <= step - lag_three < self.count:
            self.stage_three(step - lag_three)
        if 0 <= step - lag_four < self.count:
            self.stage_four(step - lag_four)
        for hop in range(1, self.nz):
            i = step - lag_four - spacing * hop
            if 0 <= i < self.count:
                self.stage_five(i, hop)

    def drain(self):
        for i in range(self.count):
            if i >= self.count - SLOTS_S:
                self.core_move(i).wait_send()
            if i >= self.count - SLOTS_T:
                self.ta_move(i).wait_send()
                self.tb_move(i).wait_send()
            if i >= self.count - RING:
                self.s2a_move(i).wait_send()
                self.s2b_move(i).wait_send()
            pl.when(self.z < self.goals[i])(lambda i=i: self.right_move(i).wait_send())
            pl.when(self.z > self.goals[i])(lambda i=i: self.left_move(i).wait_send())


def scatter_scratch(n):
    dma = pltpu.SemaphoreType.DMA
    slots_k = min(SLOTS_K, n)
    return [
        pltpu.VMEM((SLOTS_S, 4, 128, CW), BF),
        pltpu.VMEM((SLOTS_R, 4, 128, CW), BF),
        pltpu.VMEM((SLOTS_T, 4, 128, HALF), BF),
        pltpu.VMEM((SLOTS_T, 4, 128, HALF), BF),
        pltpu.VMEM((RING, 2, 128, HALF), BF),
        pltpu.VMEM((RING, 2, 128, HALF), BF),
        pltpu.VMEM((RING, 128, HALF), BF),
        pltpu.VMEM((RING, 128, HALF), BF),
        pltpu.VMEM((RING, 128, HALF), BF),
        pltpu.VMEM((RING, 128, HALF), BF),
        pltpu.VMEM((slots_k, 128, CW), F32),
        pltpu.VMEM((n, 128, CW), BF),
        pltpu.VMEM((n, 128, CW), BF),
        pltpu.VMEM((n, 128, CW), BF),
        dma((SLOTS_S,)),
        dma((SLOTS_R,)),
        dma((SLOTS_T, 2)),
        dma((RING, 2)),
        dma((RING, 2)),
        dma((RING, 2)),
        dma((n,)),
        dma((n, 2)),
        pltpu.SemaphoreType.REGULAR,
    ]


CHUNKS = (
    [("out", i) for i in range(4)] + [("qk", 0), ("vm", 0)] + [("out", i) for i in range(4, 8)] + [("qk", 1), ("vm", 1)]
    + [("in", i) for i in range(3)] + [("qk", 2), ("vm", 2)] + [("in", i) for i in range(3, 6)] + [("qk", 3), ("vm", 3)]
    + [("in", i) for i in range(6, 8)]
)
ATTEND_AT = {0: (0, 0), 3: (0, 1), 6: (1, 0), 9: (1, 1), 12: (2, 0), 14: (2, 1), 17: (3, 0), 19: (3, 1)}
TOKENS_AT = {
    4: ((0, 1),), 7: ((0, 0),), 8: ((0, 2),), 10: ((1, 1),), 12: ((1, 0),), 13: ((1, 2),), 15: ((2, 1),),
    17: ((2, 0),), 18: ((2, 2),), 20: ((3, 0), (3, 2)), 22: ((3, 1),),
}
HALO_AT = {21: 0, 23: 1, 25: 2, 27: 3}
HEADS_AT = {2: 1, 7: 2, 13: 3}
SMALL_AT = {20: 0, 22: 1, 24: 2, 26: 3, 30: 4}
INPUTS_AT = {0: 0, 4: 1, 5: 2, 12: 3}
WIDE = [i for i, (kind, part) in enumerate(CHUNKS) if kind in ("out", "in")]


def last_kernel(
    window, attn_grad, normed, ffn_grad, hidden, pre_grad, query, key, value, mixed, mixed_grad, qkv_all, resid_grad,
    lse_ref, segq_ref, segk_ref, cos_ref, sin_ref, small_ref,
    out_qkv, out_attn, out_in, out_out, head_sums, qkv_sums, in_sums, last_row, token_grad,
    xw, xa, xn, xf, gs, q_v, g_v, m_v, k_v, v_v, weight, dk_acc, dv_acc, dq_b, dk_b, dv_b, send_l, send_r, from_l, from_r,
    sums, sacc, srec, zsm, x_sem, g_sem, h_sem, w_sem, sm_sem, smz_sem, e_sem, *refs,
):
    local = attn_grad.shape[1]
    turned = ((ffn_grad, xf), (window, xw), (attn_grad, xa), (normed, xn))
    resid_load = pltpu.make_async_copy(resid_grad, token_grad, x_sem.at[4, 0])

    def x_loads(which):
        source, target = turned[which]
        return [
            pltpu.make_async_copy(source.at[plan.block(index), :], target.at[index], x_sem.at[which, index])
            for index in range(8)
        ]

    def g_load(order):
        kind, part = CHUNKS[WIDE[order]]
        source = hidden if kind == "out" else pre_grad
        return pltpu.make_async_copy(source.at[:, pl.ds(part * CW, CW)], gs.at[order % 3], g_sem.at[order % 3])

    def head_loads(shard):
        columns, slot = pl.ds(shard * 256, 256), shard % 2
        pairs = ((query, q_v), (mixed_grad, g_v), (mixed, m_v), (key, k_v), (value, v_v))
        return [
            pltpu.make_async_copy(source.at[:, columns], target.at[slot], h_sem.at[slot, index])
            for index, (source, target) in enumerate(pairs)
        ]

    def weight_load(shard):
        columns = pl.ds(shard * 256, 256)
        return pltpu.make_async_copy(qkv_all.at[:, :, columns], weight.at[shard % 2], w_sem.at[shard % 2])

    def product(i, start):
        kind, part = CHUNKS[i]
        four = slice(start, start + 4)
        if kind in ("out", "in"):
            left = (xf if kind == "out" else xn)[four].reshape(512, local)
            return dot(left, gs[WIDE.index(i) % 3])
        wide = xw[four].reshape(512, 3 * local)
        if kind == "qk":
            parts = dot(wide[:, local : 2 * local], dq_b[...]), dot(wide, dk_b[...])
        else:
            parts = dot(wide, dv_b[...]), dot(xa[four].reshape(512, local), m_v[part % 2])
        return jnp.concatenate(parts, axis=1)

    def finish(i, kept):
        kind, part = CHUNKS[i]
        if kind == "qk":
            out_qkv[:, 0:512] = kept[...]
        elif kind == "vm":
            out_qkv[:, 512:768] = kept[:, 0:256]
            out_attn[...] = kept[:, 256:512].T
        elif kind == "in":
            out_in[:, pl.ds((part % 2) * CW, CW)] = kept[...]
        else:
            out_out[pl.ds((part % 2) * CW, CW), :] = kept[...].T

    goals = [part if kind in ("qk", "vm") else part // 2 for kind, part in CHUNKS]
    plan = Scatter(goals, product, finish, refs)
    z, dp, nz = plan.z, plan.dp, plan.nz
    has_l, has_r = z > 0, z < nz - 1
    for copy in (
        *x_loads(0), g_load(0), *head_loads(0), g_load(1), *x_loads(1), g_load(2), *x_loads(2), *x_loads(3), resid_load
    ):
        copy.start()
    weight_load(0).start()
    plan.barrier()

    def to_left(piece):
        at = pl.ds(piece * 128, 128)
        return remote(send_l.at[at], from_r.at[at], e_sem.at[piece, 0], e_sem.at[piece, 1], dp, z - 1)

    def to_right(piece):
        at = pl.ds(piece * 128, 128)
        return remote(send_r.at[at], from_l.at[at], e_sem.at[piece, 2], e_sem.at[piece, 3], dp, z + 1)

    peers = (plan.to_core, plan.to_x, plan.to_y)

    def small_move(stage):
        return remote(sacc.at[stage], srec.at[stage], sm_sem.at[stage, 0], sm_sem.at[stage, 1], peers[stage], z)

    def small_z_move(step):
        sems = smz_sem.at[step - 1, 0], smz_sem.at[step - 1, 1]
        return remote(sacc.at[3], zsm.at[step - 1], *sems, dp, lax.rem(z + step, nz))

    def small_stage(stage):
        if stage == 0:
            sacc[0] = small_ref[...]
            sacc[0, QKV_ROW : QKV_ROW + 24, :] = sums[...]
        if 1 <= stage <= 3:
            small_move(stage - 1).wait_recv()
            sacc[stage] = sacc[stage - 1] + srec[stage - 1]
        if stage <= 2:
            small_move(stage).start()
        if stage == 3:
            for step in range(1, nz):
                small_z_move(step).start()
        if stage == 4:
            for step in range(1, nz):
                small_z_move(step).wait_recv()
            total = None
            for owner in range(nz):
                made = jnp.where(z == owner, sacc[3], 0.0)
                for step in range(1, nz):
                    made = jnp.where(lax.rem(z - step + nz, nz) == owner, zsm[step - 1], made)
                total = made if total is None else total + made
            zsm[0] = total
            head_sums[...] = total[:QKV_ROW]
            for kind in range(3):
                at = QKV_ROW + 8 * kind
                qkv_sums[2 * kind : 2 * kind + 2, :] = zsm[0, pl.ds(at + 2 * z, 2), :]
            in_sums[...] = zsm[0, pl.ds(pl.multiple_of(QKV_ROW + 24 + 8 * z, 8), 8), :]
            last_row[...] = total[QKV_ROW + 56 : QKV_ROW + 64]

    head_row = lax.broadcasted_iota(jnp.int32, (8, 128), 0)
    head_lane = lax.broadcasted_iota(jnp.int32, (8, 128), 1) // 64
    chosen = jnp.where(head_row == head_lane, 1.0, 0.0)
    groups = (0, 128)

    def attend_part(shard, block):
        slot = shard % 2
        if block == 0:
            for load in head_loads(shard):
                load.wait()
            dk_acc[...] = jnp.zeros_like(dk_acc)
            dv_acc[...] = jnp.zeros_like(dv_acc)
        rows = slice(block * BACK_ROWS, (block + 1) * BACK_ROWS)
        queries, grads, turned_q, turned_g, deltas, logs = [], [], [], [], [], []
        for group, at in enumerate(groups):
            lanes = slice(at, at + 128)
            scaled = q_v[slot, rows, lanes] * jnp.asarray(SCALE, BF)
            grad = g_v[slot, rows, lanes]
            queries.append(split_pair(scaled))
            grads.append(split_pair(grad))
            turned_q.append(split_pair(turn(scaled), 0))
            turned_g.append(split_pair(turn(grad), 0))
            delta = dot(chosen, m_v[slot, rows, lanes].astype(F32) * grad.astype(F32), 1, 1, lax.Precision.HIGHEST)
            deltas.append((delta[0:1], delta[1:2]))
            first_head = 4 * shard + 2 * group
            logs.append([lse_ref[first_head + head : first_head + head + 1, rows] for head in range(2)])
        seg_q = segq_ref[0:1, rows]

        def body(index, carry):
            keys_at = pl.ds(pl.multiple_of(index * BK, BK), BK)
            live = segk_ref[keys_at, 0:1] == seg_q
            made = []
            for group, at in enumerate(groups):
                lanes = slice(at, at + 128)
                keys = k_v[slot, keys_at, lanes]
                values = v_v[slot, keys_at, lanes]
                turned = turn(keys)
                dk, dv = 0.0, 0.0
                for head in range(2):
                    scores = jnp.where(live, dot(keys, turned_q[group][head]), -1e9)
                    probs = jnp.exp(scores - logs[group][head])
                    score_low = (probs * (dot(values, turned_g[group][head]) - deltas[group][head])).astype(BF)
                    made.append(carry[2 * group + head] + dot(turned, score_low))
                    dk = dk + dot(score_low, queries[group][head])
                    dv = dv + dot(probs.astype(BF), grads[group][head])
                dk_acc[keys_at, lanes] += dk
                dv_acc[keys_at, lanes] += dv
            return tuple(made)

        reach = local // BK * 2 + 1
        start = (jnp.zeros((128, BACK_ROWS), F32),) * 4
        done = lax.fori_loop(block, block + reach, body, start)
        at_window = slice(local + block * BACK_ROWS, local + (block + 1) * BACK_ROWS)
        for group, at in enumerate(groups):
            grad = jnp.concatenate([done[2 * group][0:64], done[2 * group + 1][64:128]], axis=0).T * SCALE
            back = rotate_lanes(grad, cos_ref[at_window, :], -sin_ref[at_window, :])
            dq_b[rows, at : at + 128] = back.astype(BF)
        if block == local // BACK_ROWS - 1:
            dk_b[...] = rotate_lanes(dk_acc[...], cos_ref[...], -sin_ref[...]).astype(BF)
            dv_b[...] = dv_acc[...].astype(BF)
            for kind, ref in enumerate((dq_b, dk_b, dv_b)):
                total = jnp.sum(ref[...].astype(F32), axis=0, keepdims=True)
                row = 8 * kind + 2 * shard
                sums[row : row + 1, :] = total[:, 0:128]
                sums[row + 1 : row + 2, :] = total[:, 128:256]

    def token_part(shard, part):
        slot = shard % 2
        if part == (0 if shard == 3 else 1):
            weight_load(shard).wait()
            if shard + 1 < 4:
                weight_load(shard + 1).start()
        if part == 1 and shard == 0:
            resid_load.wait()

        rows = slice(part * local, part * local + local)

        def body(index, unused):
            at = pl.ds(pl.multiple_of(index * 256, 256), 256)
            grad = dot(dk_b[rows, :], weight[slot, 1, at, :], 1, 1) + dot(dv_b[rows, :], weight[slot, 2, at, :], 1, 1)
            if part == 1:
                token_grad[:, at] += grad + dot(dq_b[...], weight[slot, 0, at, :], 1, 1)
            else:
                target = send_l if part == 0 else send_r
                target[:, at] = (grad if shard == 0 else grad + target[:, at].astype(F32)).astype(BF)
            return unused

        lax.fori_loop(0, weight.shape[2] // 256, body, 0)

    def add_halo(copy, there, source):
        @pl.when(there)
        def _():
            for piece in range(local // 128):
                copy(piece).wait_recv()
                rows = slice(piece * 128, piece * 128 + 128)
                token_grad[rows, :] += source[rows, :].astype(F32)

    for step in range(plan.steps):
        if step in INPUTS_AT:
            for load in x_loads(INPUTS_AT[step]):
                load.wait()
        if step < plan.count:
            if step in WIDE:
                g_load(WIDE.index(step)).wait()
            plan.stage_one(step)
        if 0 <= step - 1 < plan.count:
            plan.stage_two(step - 1)
            if step - 1 in WIDE and WIDE.index(step - 1) + 3 < len(WIDE):
                g_load(WIDE.index(step - 1) + 3).start()
        if step in HEADS_AT:
            for load in head_loads(HEADS_AT[step]):
                load.start()
        plan.late_stages(step)
        if step in ATTEND_AT:
            attend_part(*ATTEND_AT[step])
        for piece in TOKENS_AT.get(step, ()):
            token_part(*piece)
        if step in HALO_AT:
            pl.when(has_l)(lambda step=step: to_left(HALO_AT[step]).start())
            pl.when(has_r)(lambda step=step: to_right(HALO_AT[step]).start())
        if step in SMALL_AT:
            small_stage(SMALL_AT[step])
    add_halo(to_right, has_l, from_l)
    add_halo(to_left, has_r, from_r)
    plan.drain()
    for stage in range(3):
        small_move(stage).wait_send()
    for step in range(1, nz):
        small_z_move(step).wait_send()
    for piece in range(local // 128):
        pl.when(has_l)(lambda piece=piece: to_left(piece).wait_send())
        pl.when(has_r)(lambda piece=piece: to_right(piece).wait_send())


def last(
    window, attn_grad, normed, ffn_grad, hidden, pre_grad, query, key, value, mixed, mixed_grad, qkv_all, resid_grad,
    lse, seg_q, seg_k, cosine, sine, small,
):
    width, local = attn_grad.shape
    long = window.shape[1]
    shape = jax.ShapeDtypeStruct
    dma = pltpu.SemaphoreType.DMA
    return pl.pallas_call(
        last_kernel,
        in_specs=hbm_specs(13) + vmem_specs(6),
        out_specs=vmem_specs(9),
        out_shape=[
            shape((128, 768), F32),
            shape((256, 128), F32),
            shape((128, 1024), F32),
            shape((1024, 128), F32),
            shape((QKV_ROW, 128), F32),
            shape((6, 128), F32),
            shape((8, 128), F32),
            shape((8, 128), F32),
            shape((local, width), F32),
        ],
        scratch_shapes=[
            pltpu.VMEM((8, 128, long), BF),
            pltpu.VMEM((8, 128, local), BF),
            pltpu.VMEM((8, 128, local), BF),
            pltpu.VMEM((8, 128, local), BF),
            pltpu.VMEM((3, local, CW), BF),
            pltpu.VMEM((2, local, 256), BF),
            pltpu.VMEM((2, local, 256), BF),
            pltpu.VMEM((2, local, 256), BF),
            pltpu.VMEM((2, long, 256), BF),
            pltpu.VMEM((2, long, 256), BF),
            pltpu.VMEM((2, 3, width, 256), BF),
            pltpu.VMEM((long, 256), F32),
            pltpu.VMEM((long, 256), F32),
            pltpu.VMEM((local, 256), BF),
            pltpu.VMEM((long, 256), BF),
            pltpu.VMEM((long, 256), BF),
            pltpu.VMEM((local, width), BF),
            pltpu.VMEM((local, width), BF),
            pltpu.VMEM((local, width), BF),
            pltpu.VMEM((local, width), BF),
            pltpu.VMEM((24, 128), F32),
            pltpu.VMEM((4,) + small.shape, F32),
            pltpu.VMEM((3,) + small.shape, F32),
            pltpu.VMEM((3,) + small.shape, F32),
            dma((5, 8)),
            dma((3,)),
            dma((2, 5)),
            dma((2,)),
            dma((3, 2)),
            dma((3, 2)),
            dma((4, 4)),
        ]
        + scatter_scratch(len(CHUNKS)),
        compiler_params=pltpu.CompilerParams(
            collective_id=2, has_side_effects=True, vmem_limit_bytes=62 * 2**20
        ),
    )(
        window, attn_grad, normed, ffn_grad, hidden, pre_grad, query, key, value, mixed, mixed_grad, qkv_all, resid_grad,
        lse, seg_q, seg_k, cosine, sine, small,
    )


def shard_rows(kind, ref):
    return ref.shape[1] if kind == "qkv" else (512 if kind in ("out0", "out1") else ref.shape[0])


def source_rows(kind, ref, start, rows):
    if kind == "qkv":
        return ref.at[:, pl.ds(start, rows), :]
    if kind == "out1":
        start = pl.multiple_of(start + 512, 16)
    return ref.at[pl.ds(start, rows), :]


def gathered_rows(kind, ref, shard, start, rows):
    if kind == "qkv":
        return ref.at[:, pl.ds(start, rows), pl.ds(pl.multiple_of(shard * 256, 256), 256)]
    if kind == "in":
        return ref.at[pl.ds(start, rows), pl.ds(pl.multiple_of(shard * 1024, 1024), 1024)]
    per = ref.shape[0] // 4
    if kind == "out1":
        start = start + 512
    return ref.at[pl.ds(pl.multiple_of(shard * per + start, 16), rows), :]


class Gather:
    def __init__(self, kinds, srcs, outs, z_send, z_recv, p_send, p_recv, lag):
        self.kinds, self.srcs, self.outs = kinds, srcs, outs
        self.z_send, self.z_recv, self.p_send, self.p_recv = z_send, z_recv, p_send, p_recv
        self.dp, low, core, x, y, self.to_core, self.to_x, self.to_y = neighbours()
        self.z = lax.axis_index("tensor")
        self.nz = 4
        self.has_l, self.has_r = self.z > 0, self.z < self.nz - 1
        low_x, low_y = low + 2 - 4 * x, low + 4 - 8 * y
        low_xy = low_x + 4 - 8 * y
        self.low = low
        self.places = {
            0: (low, None), 1: (low, None), 4: (low, None), 2: (low_x, 0), 3: (low_y, 1),
            5: (low_x, None), 6: (low_y, None), 7: (low_xy, 0), 8: (low_xy, 1),
        }
        self.events = [(m, distance, side) for m in range(len(kinds)) for distance in (1, 2, 3) for side in (0, 1)]
        self.lag = lag
        self.steps = len(self.events) + 2 * lag

    def barrier(self):
        entry_barrier(self.z, self.dp, (self.to_core, self.to_x, self.to_y), self.nz)

    def piece(self, m, shard, index, half=None):
        rows = shard_rows(self.kinds[m], self.srcs[m]) // 8
        start = index * rows
        if half is not None:
            rows = rows // 2
            start = start + half * rows
        return gathered_rows(self.kinds[m], self.outs[m], shard, pl.multiple_of(start, 16), rows)

    def shard_of(self, side, distance):
        return self.z - distance if side == 0 else self.z + distance

    def onward(self, side):
        return self.z + 1 if side == 0 else self.z - 1

    def can_send(self, side):
        return self.has_r if side == 0 else self.has_l

    def arrives(self, side, distance):
        return self.z >= distance if side == 0 else self.z + distance < self.nz

    def own_move(self, m, side):
        rows = shard_rows(self.kinds[m], self.srcs[m]) // 8
        src = source_rows(self.kinds[m], self.srcs[m], pl.multiple_of(self.low * rows, 16), rows)
        sems = self.z_send.at[m, side, 0], self.z_recv.at[m, side, 0]
        return remote(src, self.piece(m, self.z, self.low), *sems, self.dp, self.onward(side))

    def relay_move(self, m, side, distance):
        at = self.piece(m, self.shard_of(side, distance), self.low)
        sems = self.z_send.at[m, side, distance], self.z_recv.at[m, side, distance]
        return remote(at, at, *sems, self.dp, self.onward(side))

    def plane_move(self, m, side, distance, kind):
        ref = self.piece(m, self.shard_of(side, distance), *self.places[kind])
        to = {0: self.to_x, 1: self.to_y, 2: self.to_y, 3: self.to_x}.get(kind, self.to_core)
        slot = side * 3 + distance - 1
        return remote(ref, ref, self.p_send.at[m, slot, kind], self.p_recv.at[m, slot, kind], to, self.z)

    def own_start(self, m):
        for side in (0, 1):
            pl.when(self.can_send(side))(lambda side=side: self.own_move(m, side).start())

    def stage_z(self, m, distance, side):
        if side == 0 and distance == 2 and m + 1 < len(self.kinds):
            self.own_start(m + 1)

        @pl.when(self.arrives(side, distance))
        def _():
            if distance == 1:
                self.own_move(m, side).wait_recv()
            else:
                self.relay_move(m, side, distance - 1).wait_recv()
            if distance < 3:
                pl.when(self.can_send(side))(lambda: self.relay_move(m, side, distance).start())
            for kind in (0, 1, 4):
                self.plane_move(m, side, distance, kind).start()

    def stage_plane(self, m, distance, side, waits, shift):
        @pl.when(self.arrives(side, distance))
        def _():
            for kind in waits:
                self.plane_move(m, side, distance, kind).wait_recv()
                for more in shift:
                    self.plane_move(m, side, distance, kind + more).start()

    def step(self, step):
        count = len(self.events)
        if step < count:
            self.stage_z(*self.events[step])
        if 0 <= step - self.lag < count:
            self.stage_plane(*self.events[step - self.lag], (0, 1), (2, 5))
        if 0 <= step - 2 * self.lag < count:
            self.stage_plane(*self.events[step - 2 * self.lag], (2, 3), (5,))

    def arrived(self, m, distance, side):
        self.stage_plane(m, distance, side, (4, 5, 6, 7, 8), ())

    def arrived_all(self, m):
        for distance in (1, 2, 3):
            for side in (0, 1):
                self.arrived(m, distance, side)

    def drain(self):
        for m, distance, side in self.events:

            @pl.when(self.arrives(side, distance))
            def _():
                for kind in range(9):
                    self.plane_move(m, side, distance, kind).wait_send()
                if distance < 3:
                    pl.when(self.can_send(side))(lambda: self.relay_move(m, side, distance).wait_send())

        for m in range(len(self.kinds)):
            for side in (0, 1):
                pl.when(self.can_send(side))(lambda side=side: self.own_move(m, side).wait_send())


def gather_sems(n):
    dma = pltpu.SemaphoreType.DMA
    return [dma((n, 2, 3)), dma((n, 2, 3)), dma((n, 6, 9)), dma((n, 6, 9))]


def first_kernel(
    qkv_src, attn_src, in_src, tokens, bias, cos_ref, sin_ref,
    qkv_out, attn_out, in_out, window_out, bias_all, query_out, key_out, value_out, value_t_out,
    weight, xw, turned, query, key, value, value_t, stage_a, stage_i,
    z_send, z_recv, p_send, p_recv, l_sem, h_sem, b_sem, o_sem,
):
    plan = Gather(
        ("qkv", "attn", "in"), (qkv_src, attn_src, in_src), (weight, attn_out, in_out), z_send, z_recv, p_send, p_recv, 4
    )
    z, dp, nz = plan.z, plan.dp, plan.nz
    local = tokens.shape[0]
    own_qkv = pltpu.make_async_copy(qkv_src, gathered_rows("qkv", weight, z, 0, qkv_src.shape[1]), l_sem.at[0])
    a_in = pltpu.make_async_copy(attn_src, stage_a, l_sem.at[1])
    i_in = pltpu.make_async_copy(in_src, stage_i, l_sem.at[2])
    a_out = pltpu.make_async_copy(stage_a, gathered_rows("attn", attn_out, z, 0, attn_src.shape[0]), l_sem.at[3])
    i_out = pltpu.make_async_copy(stage_i, gathered_rows("in", in_out, z, 0, in_src.shape[0]), l_sem.at[4])
    own_tokens = pltpu.make_async_copy(tokens, xw.at[pl.ds(local, local)], h_sem.at[4])
    fill_l = pltpu.make_async_copy(tokens, xw.at[pl.ds(0, local)], h_sem.at[5])
    fill_r = pltpu.make_async_copy(tokens, xw.at[pl.ds(2 * local, local)], h_sem.at[6])
    for copy in (own_qkv, a_in, i_in, own_tokens):
        copy.start()
    pl.when(jnp.logical_not(plan.has_l))(lambda: fill_l.start())
    pl.when(jnp.logical_not(plan.has_r))(lambda: fill_r.start())
    bias_all[pl.ds(z, 1)] = bias[...].reshape(1, *bias.shape)
    plan.barrier()
    to_left = remote(tokens, xw.at[pl.ds(2 * local, local)], h_sem.at[0], h_sem.at[1], dp, z - 1)
    to_right = remote(tokens, xw.at[pl.ds(0, local)], h_sem.at[2], h_sem.at[3], dp, z + 1)

    def bias_move(step):
        return remote(bias, bias_all.at[z], b_sem.at[0, step - 1], b_sem.at[1, step - 1], dp, lax.rem(z + step, nz))

    plan.own_start(0)
    for step in range(1, nz):
        bias_move(step).start()
    a_in.wait()
    a_out.start()
    i_in.wait()
    i_out.start()

    weight_out = pltpu.make_async_copy(weight, qkv_out, o_sem.at[0])

    def outputs(shard):
        columns = pl.ds(shard * 256, 256)
        return [
            pltpu.make_async_copy(turned.at[columns, :], window_out.at[columns, :], o_sem.at[1 + 5 * shard]),
            pltpu.make_async_copy(query.at[:, columns], query_out.at[:, columns], o_sem.at[2 + 5 * shard]),
            pltpu.make_async_copy(key.at[:, columns], key_out.at[:, columns], o_sem.at[3 + 5 * shard]),
            pltpu.make_async_copy(value.at[:, columns], value_out.at[:, columns], o_sem.at[4 + 5 * shard]),
            pltpu.make_async_copy(value_t.at[columns, :], value_t_out.at[columns, :], o_sem.at[5 + 5 * shard]),
        ]

    def ready():
        plan.arrived_all(0)
        own_qkv.wait()
        own_tokens.wait()
        weight_out.start()
        for step in range(1, nz):
            bias_move(step).wait_recv()

    def halo_ready():
        pl.when(plan.has_l)(lambda: to_right.wait_recv())
        pl.when(plan.has_r)(lambda: to_left.wait_recv())
        pl.when(jnp.logical_not(plan.has_l))(lambda: fill_l.wait())
        pl.when(jnp.logical_not(plan.has_r))(lambda: fill_r.wait())

    def compute(shard, part):
        columns = slice(shard * 256, shard * 256 + 256)
        rows = slice(part * local, part * local + local)
        window = xw[rows, :]
        cosine, sine = cos_ref[rows, :], sin_ref[rows, :]

        def made(kind):
            add = [bias_all[shard, 2 * kind + i : 2 * kind + i + 1, :].astype(F32) for i in range(2)]
            return dot(window, weight[kind, :, columns]) + jnp.concatenate(add, axis=1)

        turned[columns, rows] = turn(window[:, columns])
        if part == 1:
            query[:, columns] = rotate_lanes(made(0), cosine, sine).astype(BF)
        keys = rotate_lanes(made(1), cosine, sine)
        key[rows, columns] = keys.astype(BF)
        values = made(2)
        value[rows, columns] = values.astype(BF)
        value_t[columns, rows] = values.T.astype(BF)

    pieces = [ready]
    pieces += [partial(compute, shard, 1) for shard in range(4)]
    pieces += [halo_ready]
    for shard in range(4):
        pieces += [partial(compute, shard, 0), partial(compute, shard, 2)]
        pieces += [lambda shard=shard: [copy.start() for copy in outputs(shard)]]
    first_piece = 6 + 2 * plan.lag
    for step in range(max(plan.steps, first_piece + len(pieces))):
        if step < plan.steps:
            plan.step(step)
        if step == 5:
            pl.when(plan.has_l)(lambda: to_left.start())
            pl.when(plan.has_r)(lambda: to_right.start())
        if step >= first_piece and pieces:
            pieces.pop(0)()
    for m in (1, 2):
        plan.arrived_all(m)
    plan.drain()
    a_out.wait()
    i_out.wait()
    for step in range(1, nz):
        bias_move(step).wait_send()
    pl.when(plan.has_l)(lambda: to_left.wait_send())
    pl.when(plan.has_r)(lambda: to_right.wait_send())
    weight_out.wait()
    for shard in range(4):
        for copy in outputs(shard):
            copy.wait()


def first(qkv_weight, attn_weight, in_weight, tokens, bias, cosine, sine):
    local, width = tokens.shape
    long = 3 * local
    shape = jax.ShapeDtypeStruct
    dma = pltpu.SemaphoreType.DMA
    return pl.pallas_call(
        first_kernel,
        in_specs=hbm_specs(4) + vmem_specs(3),
        out_specs=hbm_specs(4) + vmem_specs(1) + hbm_specs(4),
        out_shape=[
            shape((3, width, width), BF),
            shape((width, width), BF),
            shape((width, 4 * width), BF),
            shape((width, long), BF),
            shape((4,) + bias.shape, BF),
            shape((local, width), BF),
            shape((long, width), BF),
            shape((long, width), BF),
            shape((width, long), BF),
        ],
        scratch_shapes=[
            pltpu.VMEM((3, width, width), BF),
            pltpu.VMEM((long, width), BF),
            pltpu.VMEM((width, long), BF),
            pltpu.VMEM((local, width), BF),
            pltpu.VMEM((long, width), BF),
            pltpu.VMEM((long, width), BF),
            pltpu.VMEM((width, long), BF),
            pltpu.VMEM(attn_weight.shape, BF),
            pltpu.VMEM(in_weight.shape, BF),
        ]
        + gather_sems(3)
        + [dma((5,)), dma((7,)), dma((2, 3)), dma((21,))],
        compiler_params=pltpu.CompilerParams(collective_id=0, has_side_effects=True, vmem_limit_bytes=VMEM_BIG),
    )(qkv_weight, attn_weight, in_weight, tokens, bias, cosine, sine)


def normalise(values):
    mean_value = jnp.mean(values, axis=1, keepdims=True)
    centered = values - mean_value
    variance = jnp.mean(centered * centered, axis=1, keepdims=True)
    scale = lax.rsqrt(variance + eps_norm)
    return centered * scale, scale


FF_STEP = 512
ROOT_HALF = math.sqrt(0.5)
ROOT_TURN = 1.0 / math.sqrt(2.0 * math.pi)


def second_kernel(
    out_src, mixed, tokens, attn_all, in_all, in_bias, vectors, proj_weight,
    out_all, hidden_out, slope_out, normed_out, unit_one_out, scale_one, output_out, unit_two_out, scale_two, emb_all,
    weight, mixed_v, tokens_v, attn_v, in_v, hidden, slope, normed, normed_low, normed_t, total, unit, output_low, unit_two, emb,
    z_send, z_recv, p_send, p_recv, l_sem, i_sem, o_sem, e_sem,
):
    plan = Gather(("out0", "out1"), (out_src, out_src), (weight, weight), z_send, z_recv, p_send, p_recv, 4)
    z, dp, nz = plan.z, plan.dp, plan.nz
    local = tokens.shape[0]
    per = out_src.shape[0]
    own = pltpu.make_async_copy(out_src, weight.at[pl.ds(pl.multiple_of(z * per, 16), per)], l_sem.at[0])
    loads = [
        pltpu.make_async_copy(src, dst, l_sem.at[1 + index])
        for index, (src, dst) in enumerate(((mixed, mixed_v), (attn_all, attn_v), (tokens, tokens_v)))
    ]
    ff = in_all.shape[1]
    ff_steps = ff // FF_STEP

    def in_load(index):
        return pltpu.make_async_copy(
            in_all.at[:, pl.ds(index * FF_STEP, FF_STEP)], in_v.at[index % 2], i_sem.at[index % 2]
        )

    for copy in (*loads, own, in_load(0), in_load(1)):
        copy.start()
    plan.barrier()
    plan.own_start(0)

    saves = [
        pltpu.make_async_copy(src, dst, o_sem.at[index])
        for index, (src, dst) in enumerate(
            ((hidden, hidden_out), (slope, slope_out), (normed_t, normed_out), (unit, unit_one_out),
             (output_low, output_out), (unit_two, unit_two_out), (weight, out_all))
        )
    ]

    def attn_half(half):
        if half == 0:
            for load in loads:
                load.wait()
        rows = slice(half * (local // 2), (half + 1) * (local // 2))
        attn_out = dot(mixed_v[rows, :], attn_v[...]) + vectors[0:1, :]
        made, scale = normalise(tokens_v[rows, :].astype(F32) + attn_out)
        unit[rows, :] = made
        scale_one[rows, :] = jnp.broadcast_to(scale, (local // 2, 128))
        full = made * vectors[2:3, :] + vectors[4:5, :]
        normed[rows, :] = full
        normed_low[rows, :] = full.astype(BF)
        normed_t[:, rows] = full.T.astype(BF)
        if half == 1:
            saves[2].start()
            saves[3].start()

    def ff_one(index):
        in_load(index).wait()
        columns = slice(index * FF_STEP, (index + 1) * FF_STEP)

        def body(part, unused):
            rows = pl.ds(pl.multiple_of(part * 128, 128), 128)
            pre = dot(normed_low[rows, :], in_v[index % 2]) + in_bias[0:1, columns]
            spread = 0.5 + 0.5 * lax.erf(pre * ROOT_HALF)
            hidden[rows, columns] = (pre * spread).astype(BF)
            slope[rows, columns] = (spread + pre * (ROOT_TURN * jnp.exp(-0.5 * pre * pre))).astype(BF)
            return unused

        lax.fori_loop(0, local // 128, body, 0)
        if index + 2 < ff_steps:
            in_load(index + 2).start()
        if index == ff_steps - 1:
            saves[0].start()
            saves[1].start()

    def out_own():
        own.wait()
        at = pl.ds(pl.multiple_of(z * per, 128), per)
        total[...] = dot(hidden[:, at], weight[at, :]) + normed[...] + vectors[1:2, :]

    def out_shard(half, distance, side):
        plan.arrived(half, distance, side)

        @pl.when(plan.arrives(side, distance))
        def _():
            at = pl.ds(pl.multiple_of(plan.shard_of(side, distance) * per + half * 512, 128), 512)
            total[...] += dot(hidden[:, at], weight[at, :])

    pieces = [partial(attn_half, 0), partial(attn_half, 1)]
    pieces += [partial(ff_one, index) for index in range(ff_steps)]
    pieces += [out_own]
    pieces += [partial(out_shard, *event) for event in plan.events]
    for step in range(max(plan.steps, len(pieces))):
        if step < plan.steps:
            plan.step(step)
        if step < len(pieces):
            pieces[step]()
    saves[6].start()

    made, scale = normalise(total[...])
    unit_two[...] = made
    saves[5].start()
    scale_two[...] = jnp.broadcast_to(scale, (local, 128))
    output_low[...] = (made * vectors[3:4, :] + vectors[5:6, :]).astype(BF)
    saves[4].start()
    emb[...] = dot(output_low[...], proj_weight[...]).astype(BF)
    emb_all[pl.ds(z, 1)] = emb[...].reshape(1, local, 128)

    def emb_move(step):
        return remote(emb, emb_all.at[z], e_sem.at[0, step - 1], e_sem.at[1, step - 1], dp, lax.rem(z + step, nz))

    for step in range(1, nz):
        emb_move(step).start()
    plan.drain()
    for save in saves:
        save.wait()
    for step in range(1, nz):
        emb_move(step).wait()


def second(out_weight, mixed, tokens, attn_all, in_all, in_bias, vectors, proj_weight):
    local, width = tokens.shape
    ff = in_all.shape[1]
    shape = jax.ShapeDtypeStruct
    dma = pltpu.SemaphoreType.DMA
    return pl.pallas_call(
        second_kernel,
        in_specs=hbm_specs(5) + vmem_specs(3),
        out_specs=hbm_specs(5) + vmem_specs(1) + hbm_specs(2) + vmem_specs(2),
        out_shape=[
            shape((ff, width), BF),
            shape((local, ff), BF),
            shape((local, ff), BF),
            shape((width, local), BF),
            shape((local, width), F32),
            shape((local, 128), F32),
            shape((local, width), BF),
            shape((local, width), F32),
            shape((local, 128), F32),
            shape((4, local, 128), BF),
        ],
        scratch_shapes=[
            pltpu.VMEM((ff, width), BF),
            pltpu.VMEM((local, width), BF),
            pltpu.VMEM((local, width), BF),
            pltpu.VMEM((width, width), BF),
            pltpu.VMEM((2, width, FF_STEP), BF),
            pltpu.VMEM((local, ff), BF),
            pltpu.VMEM((local, ff), BF),
            pltpu.VMEM((local, width), F32),
            pltpu.VMEM((local, width), BF),
            pltpu.VMEM((width, local), BF),
            pltpu.VMEM((local, width), F32),
            pltpu.VMEM((local, width), F32),
            pltpu.VMEM((local, width), BF),
            pltpu.VMEM((local, width), F32),
            pltpu.VMEM((local, 128), BF),
        ]
        + gather_sems(2)
        + [dma((4,)), dma((2,)), dma((7,)), dma((2, 3))],
        compiler_params=pltpu.CompilerParams(collective_id=1, has_side_effects=True, vmem_limit_bytes=VMEM_BIG),
    )(out_weight, mixed, tokens, attn_all, in_all, in_bias, vectors, proj_weight)


def norm_back(unit, scale, gain, grad):
    dn = grad * gain
    back = scale * (
        dn - jnp.mean(dn, axis=-1, keepdims=True) - unit * jnp.mean(dn * unit, axis=-1, keepdims=True)
    )
    return back, jnp.sum(grad * unit, axis=0), jnp.sum(grad, axis=0)


def segment_facts(lengths, doc_pairs, log_temp, local, z, dp_count):
    base = z * local
    row_lengths = lengths[0]
    seg_range = jnp.arange(SEGS, dtype=jnp.int32)
    seg_ends = jnp.sum(jnp.where(seg_range[:, None] >= seg_range[None, :], row_lengths[None, :], 0), axis=1)
    seg_starts = seg_ends - row_lengths
    positions = jnp.arange(SEQ, dtype=jnp.int32)
    seg_ids = jnp.sum((positions[:, None] >= seg_ends[None, :]).astype(jnp.int32), axis=1)
    near = jnp.arange(3 * local, dtype=jnp.int32) + base - local
    near_ids = jnp.sum((near[:, None] >= seg_ends[None, :]).astype(jnp.int32), axis=1)
    near_ids = jnp.where((near >= 0) & (near < SEQ), near_ids, -1)
    near_member = near_ids[:, None] == jnp.arange(SEGS, dtype=jnp.int32)[None, :]
    near_starts = jnp.sum(jnp.where(near_member, seg_starts[None, :], 0), axis=1)
    offsets = jnp.where(near_ids >= 0, near - near_starts, 0)
    half_dim = HDIM // 2
    inv_freq = jnp.exp(jnp.arange(half_dim, dtype=F32) * (-2.0 * math.log(10000.0) / HDIM))
    angles = offsets.astype(F32)[:, None] * jnp.tile(inv_freq, 4)[None, :]
    side = jnp.where(jnp.arange(128) % HDIM < half_dim, -1.0, 1.0).astype(F32)
    cosine, sine = jnp.cos(angles), jnp.sin(angles) * side[None, :]
    seg_q = jnp.broadcast_to(lax.slice_in_dim(near_ids, local, 2 * local)[None, :], (8, local))
    seg_k = jnp.broadcast_to(near_ids[:, None], (3 * local, 128))
    key_starts = jnp.where(near_ids >= 0, near_starts - base + local, 0)
    near_ends = jnp.sum(jnp.where(near_member, seg_ends[None, :], 0), axis=1)
    key_ends = jnp.where(near_ids >= 0, near_ends - base + local, 0)

    def live_blocks(rows):
        first_key = key_starts[local : 2 * local : rows]
        last_key = key_ends[local + rows - 1 : 2 * local : rows]
        return jnp.stack([first_key // BK, (last_key + BK - 1) // BK], axis=1)

    bounds = live_blocks(FWD_ROWS)
    query_end = seg_ends[NQ - 1]
    info = jnp.stack([base // CB, (query_end + CB - 1) // CB, query_end // CB])
    seg_col = jnp.broadcast_to(seg_ids[:, None], (SEQ, 128))
    seg_row = jnp.broadcast_to(seg_ids[None, :], (8, SEQ))
    counts = jnp.broadcast_to(row_lengths.astype(F32)[:, None], (SEGS, 128))
    positive = (doc_pairs[0][:, None] == jnp.arange(128, dtype=jnp.int32)[None, :]).astype(F32)
    loss_scale = 1.0 / (NQ * dp_count)
    temp_row = jnp.concatenate([log_temp, jnp.full((127,), loss_scale, F32)]).reshape(1, 128)

    return bounds, seg_q, seg_k, cosine, sine, info, seg_col, seg_row, counts, positive, temp_row


def per_device(
    tokens, lengths, doc_pairs, qkv_weight, qkv_bias, attn_weight, attn_bias, ffn_in_weight, ffn_in_bias,
    ffn_out_weight, ffn_out_bias, norm_gains, norm_shifts, proj_weight, log_temp,
):
    local, width = tokens.shape
    dp_count = lax.axis_size("dp")
    tensor_count = lax.axis_size("tensor")
    groups = dp_count // 8
    z = lax.axis_index("tensor")
    bounds, seg_q, seg_k, cosine, sine, info, seg_col, seg_row, counts, positive, temp_row = segment_facts(
        lengths, doc_pairs, log_temp, local, z, dp_count
    )
    gains = norm_gains.astype(F32)
    shifts = norm_shifts.astype(F32)
    bias = jnp.concatenate([qkv_bias.reshape(6, 128), ffn_in_bias.reshape(8, 128), jnp.zeros((2, 128), BF)])
    qkv_all, attn_all, in_all, window_t, bias_all, queries, keys, values, values_t = first(
        jnp.transpose(qkv_weight, (1, 0, 2)), attn_weight, ffn_in_weight, tokens, bias, cosine, sine
    )
    in_bias_all = bias_all[:, 6:14].reshape(1, 4 * width).astype(F32)
    vectors = jnp.concatenate(
        [attn_bias.astype(F32)[None], ffn_out_bias.astype(F32)[None], gains, shifts, jnp.zeros((2, width), F32)]
    )
    mixed, lse = attend(bounds, queries, keys, values_t, seg_q, seg_k)
    out_all, hidden, slope, normed_t, unit_one, scale_one, output_low, unit_two, scale_two, embedded_all = second(
        ffn_out_weight, mixed, tokens, attn_all, in_all, in_bias_all, vectors, proj_weight
    )
    embedded_all = embedded_all.reshape(-1, EMB)
    scale_one, scale_two = scale_one[:, :1], scale_two[:, :1]
    emb_grad, row_loss, row_temp = contrast(info, embedded_all, seg_col, seg_row, counts, positive, temp_row, local)

    proj_grad = dot(output_low, emb_grad, 0, 0)
    output_grad = dot(emb_grad, proj_weight, 1, 1)
    resid_two_grad, gain_two_grad, shift_two_grad = norm_back(unit_two, scale_two, gains[1], output_grad)
    ffn_grad = resid_two_grad.astype(BF)
    out_bias_grad = jnp.sum(ffn_grad.astype(F32), axis=0)
    hidden_grad = dot(ffn_grad, out_all, 1, 1)
    pre_grad = (hidden_grad * slope.astype(F32)).astype(BF)
    in_bias_grad = jnp.sum(pre_grad.astype(F32), axis=0)
    normed_grad = dot(pre_grad, in_all, 1, 1) + resid_two_grad
    resid_one_grad, gain_one_grad, shift_one_grad = norm_back(unit_one, scale_one, gains[0], normed_grad)
    attn_grad = resid_one_grad.astype(BF)
    attn_bias_grad = jnp.sum(attn_grad.astype(F32), axis=0)
    mixed_grad = dot(attn_grad, attn_all, 1, 1).astype(BF)
    share = 1.0 / tensor_count
    proj_red = lax.psum(proj_grad, ("dp", "tensor"))
    small = jnp.concatenate(
        [
            attn_bias_grad, out_bias_grad, gain_one_grad, gain_two_grad, shift_one_grad, shift_two_grad,
            jnp.zeros((3 * width,), F32), in_bias_grad, row_loss[0, :1] * share, row_temp[0, :1] * share,
            jnp.zeros((SMALL_ROWS * 128 - 13 * width - 2,), F32),
        ]
    ).reshape(SMALL_ROWS, 128)

    def arrange(array):
        if groups == 1:
            return array
        columns = array.shape[1]
        return array.reshape(groups, 8, -1, columns).transpose(1, 0, 2, 3).reshape(width, columns)

    qkv_red, attn_red, in_red, out_red, *sums, tokens_grad = last(
        arrange(window_t), arrange(attn_grad.T), arrange(normed_t), arrange(ffn_grad.T), hidden, pre_grad,
        queries, keys, values, mixed, mixed_grad, qkv_all, resid_one_grad, lse, seg_q, seg_k, cosine, sine, small,
    )
    if groups > 1:
        ranks = [[high * 8 + low for high in range(groups)] for low in range(8)]
        qkv_red, attn_red, in_red, out_red = (
            lax.psum_scatter(part, "dp", scatter_dimension=dim, axis_index_groups=ranks, tiled=True)
            for part, dim in ((qkv_red, 0), (attn_red, 1), (in_red, 0), (out_red, 1))
        )
        sums = lax.psum(sums, "dp", axis_index_groups=ranks)
    head_sums, qkv_bias_red, in_bias_red, last_row = sums
    return (
        last_row[0, :1],
        output_low,
        tokens_grad,
        qkv_red.reshape(-1, 3, 256),
        qkv_bias_red.reshape(3, -1),
        attn_red,
        head_sums[0:8].reshape(-1),
        in_red,
        in_bias_red.reshape(-1),
        out_red,
        head_sums[8:16].reshape(-1),
        head_sums[16:32].reshape(2, width),
        head_sums[32:48].reshape(2, width),
        proj_red,
        last_row[0, 1:2],
    )


def solution(mesh):
    in_specs = (
        P(("dp", "tensor"), None),
        P("dp", None),
        P("dp", None),
        P(None, None, "tensor"),
        P(None, "tensor"),
        P("tensor", None),
        P(),
        P(None, "tensor"),
        P("tensor"),
        P("tensor", None),
        P(),
        P(),
        P(),
        P(),
        P(),
    )
    out_specs = (
        P(),
        P(("dp", "tensor"), None),
        P(("dp", "tensor"), None),
        P("dp", None, "tensor"),
        P(None, "tensor"),
        P("tensor", "dp"),
        P(),
        P("dp", "tensor"),
        P("tensor"),
        P("tensor", "dp"),
        P(),
        P(),
        P(),
        P(),
        P(),
    )
    return jax.shard_map(
        per_device, mesh=mesh, in_specs=in_specs, out_specs=out_specs, check_vma=False
    )
```
